32 devices in a mesh: seq: 4 (over y, x), fsdp: 8 (over z, core).
Axes of the slice: x: 2, y: 2, z: 4, core: 2. Of those that a mesh axis runs over, the one named last changes fastest.
Arguments:
- hidden_in: bfloat16 [16, 1024, 1024], P('fsdp', 'seq'), may hold values from -6 to 6
- segments: int32 [16, 1024], P('fsdp'), may hold values from 0 to 17, as said below
- q_weight: bfloat16 [1024, 1024], P('fsdp'), may hold values from -0.1875 to 0.1875
- k_weight: bfloat16 [1024, 1024], P('fsdp'), may hold values from -0.1875 to 0.1875
- v_weight: bfloat16 [1024, 1024], P('fsdp'), may hold values from -0.1875 to 0.1875
- out_weight: bfloat16 [1024, 1024], P('fsdp'), may hold values from -0.75 to 0.75
- q_bias: bfloat16 [1024], P('fsdp'), may hold values from -3 to 3
- v_bias: bfloat16 [1024], P('fsdp'), may hold values from -3 to 3
- out_bias: bfloat16 [1024], P('fsdp'), may hold values from -3 to 3
- up_weight: bfloat16 [1024, 4096], P('fsdp'), may hold values from -0.1875 to 0.1875
- up_bias: bfloat16 [4096], P('fsdp'), may hold values from -3 to 3
- down_weight: bfloat16 [4096, 1024], P('fsdp'), may hold values from -0.09375 to 0.09375
- down_bias: bfloat16 [1024], P('fsdp'), may hold values from -3 to 3
- norm1_gain: bfloat16 [1024], P('fsdp'), may hold values from 0.5 to 1.5
- norm1_bias: bfloat16 [1024], P('fsdp'), may hold values from -3 to 3
- norm2_gain: bfloat16 [1024], P('fsdp'), may hold values from 0.5 to 1.5
- norm2_bias: bfloat16 [1024], P('fsdp'), may hold values from -3 to 3
- out_grad: bfloat16 [16, 1024, 1024], P('fsdp', 'seq'), may hold values from -6 to 6
Outputs:
- layer_out: bfloat16 [16, 1024, 1024], P('fsdp', 'seq')
- input_grad: float32 [16, 1024, 1024], P('fsdp', 'seq')
- q_weight_grad: float32 [1024, 1024], P('fsdp')
- k_weight_grad: float32 [1024, 1024], P('fsdp')
- v_weight_grad: float32 [1024, 1024], P('fsdp')
- out_weight_grad: float32 [1024, 1024], P('fsdp')
- q_bias_grad: float32 [1024], P('fsdp')
- v_bias_grad: float32 [1024], P('fsdp')
- out_bias_grad: float32 [1024], P('fsdp')
- up_weight_grad: float32 [1024, 4096], P('fsdp')
- up_bias_grad: float32 [4096], P('fsdp')
- down_weight_grad: float32 [4096, 1024], P('fsdp')
- down_bias_grad: float32 [1024], P('fsdp')
- norm1_gain_grad: float32 [1024], P('fsdp')
- norm1_bias_grad: float32 [1024], P('fsdp')
- norm2_gain_grad: float32 [1024], P('fsdp')
- norm2_bias_grad: float32 [1024], P('fsdp')
The draws below stay inside these ranges and needn't reach their ends.
Inputs may be any that keep to these rules, and one draw needn't show every extreme that they name: `segments`: along a sequence the numbers start at 1 and rise by one at each new document, then end in a tail of 0. Documents are at least max(60, 2) tokens long. In every aligned group of 2 sequences one sequence is a single document of all 1024 tokens and another holds the most documents; every sequence but the single document ends in 1 to 128 pad tokens.
All inputs are finite; a program needn't handle non-finite values.
Results may differ from the reference program's by a relative error of at most 0.02.
Values may be sent and summed in bfloat16 or wider, within the bound.
No kernel may reach another device: no remote copies, remote signals or barrier semaphores. Data moves between devices by JAX's collectives and lax.ppermute only.
A program may use at most 192 MiB of HBM per device.

```python
import math
import jax
import jax.numpy as jnp
from jax import lax

D = 1024
FF = 4096
HEADS = 16
HEAD_DIM = 64
LEN = 1024
SEQ_DEV = 2
SEQS = 16


def draw_segments(key, part):
    key = jax.random.fold_in(key, 11)
    least_doc = max(LEN * 60 // 1024, 2)
    most_doc = max(LEN * 800 // 1024, least_doc + 1)
    doc_count = LEN // least_doc + 1
    packed_docs = (LEN - 1) // least_doc
    key_len, key_pad, key_whole, key_packed = jax.random.split(key, 4)
    lengths = jax.random.randint(key_len, (SEQS, doc_count), least_doc, most_doc + 1)
    doc_ends = jnp.cumsum(lengths, axis=1)
    positions = jnp.arange(LEN)
    numbers = 1 + jnp.sum((doc_ends[:, None, :] <= positions[None, :, None]).astype(jnp.int32), axis=2)
    pad_count = jax.random.randint(key_pad, (SEQS, 1), 1, LEN // 8 + 1)
    numbers = jnp.where(positions[None, :] >= LEN - pad_count, 0, numbers)
    packed_row = jnp.where(positions < packed_docs * least_doc, positions // least_doc + 1, 0)
    whole_pick = jax.random.randint(key_whole, (SEQS // SEQ_DEV,), 0, SEQ_DEV)
    packed_step = jax.random.randint(key_packed, (SEQS // SEQ_DEV,), 1, SEQ_DEV)
    packed_pick = (whole_pick + packed_step) % SEQ_DEV
    local_rows = jnp.arange(SEQS) % SEQ_DEV
    whole_rows = local_rows == jnp.repeat(whole_pick, SEQ_DEV)
    packed_rows = local_rows == jnp.repeat(packed_pick, SEQ_DEV)
    numbers = jnp.where(packed_rows[:, None], packed_row[None, :], numbers)
    numbers = jnp.where(whole_rows[:, None], 1, numbers)
    return numbers.astype(jnp.int32)


def levels(key, dims, pieces, least, high):
    level, own = 1.0, jax.random.fold_in(key, 6)
    for dim, shards_of in pieces:
        heights = jnp.exp(jax.random.uniform(jax.random.fold_in(own, dim), (shards_of,), jnp.float32, least / len(pieces), high / len(pieces)))
        level = level * jnp.repeat(heights, dims[dim] // shards_of).reshape([-1 if axis == dim else 1 for axis in range(len(dims))])
    return level


def noise(rng, shape, scale, reach, shards=(), held_as=jnp.bfloat16):
    values = jax.random.normal(rng, shape, jnp.float32) * scale
    if len(shards) > 0:
        values = levels(rng, shape, shards, -0.22, 0.18) * values
    return jnp.clip(values, min=-reach, max=reach).astype(held_as)


def setup_inputs(seed: int = 0) -> dict:
    key_list = jax.random.split(jax.random.key(seed), 19)
    return {
        "hidden_in": noise(key_list[0], (SEQS, LEN, D), 1.0, 6.0, ((0, 8), (1, 4))),
        "segments": draw_segments(jax.random.fold_in(key_list[18], 71), 0),
        "q_weight": noise(key_list[2], (D, D), D ** -0.5, 0.1875, ((0, 8),)),
        "k_weight": noise(key_list[3], (D, D), D ** -0.5, 0.1875, ((0, 8),)),
        "v_weight": noise(key_list[4], (D, D), D ** -0.5, 0.1875, ((0, 8),)),
        "out_weight": noise(key_list[5], (D, D), (D // 16) ** -0.5, 0.75, ((0, 8),)),
        "q_bias": noise(key_list[6], (D,), 0.3, 3.0, ((0, 8),)),
        "v_bias": noise(key_list[7], (D,), 0.3, 3.0, ((0, 8),)),
        "out_bias": noise(key_list[8], (D,), 0.3, 3.0, ((0, 8),)),
        "up_weight": noise(key_list[9], (D, FF), D ** -0.5, 0.1875, ((0, 8),)),
        "up_bias": noise(key_list[10], (FF,), 0.5, 3.0, ((0, 8),)),
        "down_weight": noise(key_list[11], (FF, D), FF ** -0.5, 0.09375, ((0, 8),)),
        "down_bias": noise(key_list[12], (D,), 0.3, 3.0, ((0, 8),)),
        "norm1_gain": jnp.clip(1.0 + 0.1 * jax.random.normal(key_list[13], (D,), jnp.float32), 0.5, 1.5).astype(jnp.bfloat16),
        "norm1_bias": noise(key_list[14], (D,), 0.3, 3.0, ((0, 8),)),
        "norm2_gain": jnp.clip(1.0 + 0.1 * jax.random.normal(key_list[15], (D,), jnp.float32), 0.5, 1.5).astype(jnp.bfloat16),
        "norm2_bias": noise(key_list[16], (D,), 0.3, 3.0, ((0, 8),)),
        "out_grad": noise(key_list[17], (SEQS, LEN, D), 1.0, 6.0, ((0, 8), (1, 4))),
    }


@jax.custom_vjp
def low(v):
    return lax.optimization_barrier(v.astype(jnp.bfloat16)).astype(jnp.float32)

@jax.custom_vjp
def low_back(v):
    return v

def low_keep(v):
    return (low(v), None)

def low_pass(kept, grad):
    return (grad,)

def back_keep(v):
    return (v, None)

def back_low(kept, grad):
    return (low(grad),)
low.defvjp(low_keep, low_pass)
low_back.defvjp(back_keep, back_low)
HIGHEST = lax.Precision.HIGHEST

def matmul(left_side, right_side):
    return jnp.dot(left_side, right_side, precision=HIGHEST)

def layer_norm(values, gain_vec, shift_vec):
    center = lax.optimization_barrier(jnp.mean(values, axis=-1, keepdims=True))
    offset = values - center
    spread = lax.optimization_barrier(jnp.mean(offset * offset, axis=-1, keepdims=True))
    return offset * lax.rsqrt(spread + 1e-05) * gain_vec + shift_vec

def gelu_exact(values):
    return 0.5 * values * (1.0 + lax.erf(values * 0.7071067811865476))

def attend(queries, key_rows, value_rows, doc_ids):
    product = low_back(jnp.einsum('qhd,khd->hqk', queries, key_rows, precision=HIGHEST))
    scores = product * HEAD_DIM ** (-0.5)
    same_doc = doc_ids[:, None] == doc_ids[None, :]
    scores = jnp.where(same_doc[None], scores, -1e+30)
    row_peak = lax.optimization_barrier(jnp.max(scores, axis=-1, keepdims=True))
    exponent = jnp.exp(scores - row_peak)
    weights = exponent / lax.optimization_barrier(jnp.sum(exponent, axis=-1, keepdims=True))
    return jnp.einsum('hqk,khd->qhd', low(weights), value_rows, precision=HIGHEST)

def per_seq(items):
    return attend(items[0], items[1], items[2], items[3])

def forward(doc_ids, hidden, q_weight, k_weight, v_weight, out_weight, q_bias, v_bias, out_bias, up_weight, up_bias, down_weight, down_bias, norm1_gain, norm1_bias, norm2_gain, norm2_bias):
    seq_count = hidden.shape[0]
    tok_rows = hidden.reshape(-1, D)
    queries = low(low_back(matmul(tok_rows, q_weight) + q_bias))
    key_rows = low(low_back(matmul(tok_rows, k_weight)))
    value_rows = low(low_back(matmul(tok_rows, v_weight) + v_bias))
    shaped = (seq_count, LEN, HEADS, HEAD_DIM)
    context = lax.map(jax.checkpoint(per_seq), (queries.reshape(shaped), key_rows.reshape(shaped), value_rows.reshape(shaped), doc_ids))
    context = low(low_back(context.reshape(-1, D)))
    branch = low_back(matmul(context, out_weight) + out_bias)
    normed_first = layer_norm(tok_rows + branch, norm1_gain, norm1_bias)
    upper_pre = low_back(matmul(low(normed_first), up_weight) + up_bias)
    mlp_out = low_back(matmul(low(gelu_exact(upper_pre)), down_weight) + down_bias)
    return layer_norm(normed_first + mlp_out, norm2_gain, norm2_bias).reshape(hidden.shape)

def reference(hidden_in, segments, q_weight, k_weight, v_weight, out_weight, q_bias, v_bias, out_bias, up_weight, up_bias, down_weight, down_bias, norm1_gain, norm1_bias, norm2_gain, norm2_bias, out_grad):
    params = tuple((tensor.astype(jnp.float32) for tensor in (q_weight, k_weight, v_weight, out_weight, q_bias, v_bias, out_bias, up_weight, up_bias, down_weight, down_bias, norm1_gain, norm1_bias, norm2_gain, norm2_bias)))
    group_size = math.gcd(SEQS, 4)
    blocks = SEQS // group_size
    inputs = hidden_in.astype(jnp.float32).reshape(blocks, group_size, LEN, D)
    keep_mask = (segments != 0).astype(jnp.float32)
    cotangent = (out_grad.astype(jnp.float32) * keep_mask[:, :, None]).reshape(blocks, group_size, LEN, D)
    doc_groups = segments.reshape(blocks, group_size, LEN)

    def accumulate(totals, items):
        hidden, doc_ids, tangent = items
        result, pullback = jax.vjp(lambda hidden_part, *weights: forward(doc_ids, hidden_part, *weights), hidden, *params)
        gradients = pullback(tangent)
        totals = jax.tree.map(jnp.add, totals, tuple(gradients[1:]))
        return (totals, (result, gradients[0]))
    zero_sums = tuple((jnp.zeros_like(tensor) for tensor in params))
    totals, outputs = lax.scan(accumulate, zero_sums, (inputs, doc_groups, cotangent))
    layer_out = outputs[0].reshape(SEQS, LEN, D).astype(jnp.bfloat16)
    input_grad = outputs[1].reshape(SEQS, LEN, D)
    return (layer_out, input_grad, totals[0], totals[1], totals[2], totals[3], totals[4], totals[5], totals[6], totals[7], totals[8], totals[9], totals[10], totals[11], totals[12], totals[13], totals[14])
```

```python
import functools

import jax
import jax.numpy as jnp
from jax import lax
from jax.experimental import pallas as pl
from jax.experimental.pallas import tpu as pltpu
from jax.sharding import Mesh
from jax.sharding import PartitionSpec as P

HEAD_DIM=64
SPAN=128
MASKED=-1e30

def dot(a,b,ca,cb):
    return lax.dot_general(a,b,(((ca,),(cb,)),((),())),preferred_element_type=jnp.float32)

def plan_rows(segments):
    b, t = segments.shape
    n = t // SPAN
    win = min(3 * SPAN, t)
    spans = segments.reshape(b, n, SPAN)
    place = jnp.arange(t, dtype=jnp.int32)
    low = jnp.min(jnp.where(segments[:, None, :] == spans[:, :, :1], place, t), axis=2)
    high = jnp.max(jnp.where(segments[:, None, :] == spans[:, :, -1:], place, -1), axis=2)
    start = jnp.minimum(low // SPAN * SPAN, t - win)
    fits = jnp.all(high < start + win, axis=1)
    single = jnp.all(segments == segments[:, :1], axis=1)
    kind = jnp.where(single, 0, jnp.where(fits, 1, 2))
    return kind.astype(jnp.int32), start.astype(jnp.int32)

def fwd_kernel(heads, kind_ref, start_ref, qkv_ref, row_ref, col_ref, ctx_ref, lse_ref):
    b = pl.program_id(0)
    t = qkv_ref.shape[1]
    hw = heads * HEAD_DIM
    win = min(3 * SPAN, t)
    kind = kind_ref[b]

    def piece(h, which, rows):
        lo = which * hw + h * HEAD_DIM
        return qkv_ref[0, rows, lo:lo + HEAD_DIM]

    def attend(h, rows, count, keys, masked):
        q = piece(h, 0, rows)
        s = dot(q, piece(h, 1, keys), 1, 1)
        if masked:
            s = jnp.where(col_ref[0, rows, :] == row_ref[0, :, keys], s, MASKED)
        m = jnp.max(s, axis=1, keepdims=True)
        e = jnp.exp(s - m)
        total = jnp.sum(e, axis=1, keepdims=True)
        c = dot(e.astype(jnp.bfloat16), piece(h, 2, keys), 1, 0) / total
        ctx_ref[0, rows, h * HEAD_DIM:(h + 1) * HEAD_DIM] = c.astype(jnp.bfloat16)
        lse = jnp.broadcast_to(m + jnp.log(total), (count, 128))
        lse_ref[0, h:h + 1, rows] = jnp.transpose(lse)[0:1, :]

    def dense(masked):
        tile = min(256, t)
        def body(i, _):
            rows = pl.ds(pl.multiple_of(i * tile, tile), tile)
            for h in range(heads):
                attend(h, rows, tile, pl.ds(0, t), masked)
            return 0
        lax.fori_loop(0, t // tile, body, 0)

    @pl.when(kind == 0)
    def _():
        dense(False)

    @pl.when(kind == 2)
    def _():
        dense(True)

    @pl.when(kind == 1)
    def _():
        def body(i, _):
            rows = pl.ds(pl.multiple_of(i * SPAN, SPAN), SPAN)
            keys = pl.ds(pl.multiple_of(start_ref[b, i], SPAN), win)
            for h in range(heads):
                attend(h, rows, SPAN, keys, True)
            return 0
        lax.fori_loop(0, t // SPAN, body, 0)

def attention(qkv, segments, kind, start):
    b, t, w = qkv.shape
    hw = w // 3
    heads = hw // HEAD_DIM
    return pl.pallas_call(
        functools.partial(fwd_kernel, heads),
        grid_spec=pltpu.PrefetchScalarGridSpec(
            num_scalar_prefetch=2,
            grid=(b,),
            in_specs=[
                pl.BlockSpec((1, t, w), lambda i, *_: (i, 0, 0)),
                pl.BlockSpec((1, 1, t), lambda i, *_: (i, 0, 0)),
                pl.BlockSpec((1, t, 1), lambda i, *_: (i, 0, 0)),
            ],
            out_specs=[
                pl.BlockSpec((1, t, hw), lambda i, *_: (i, 0, 0)),
                pl.BlockSpec((1, heads, t), lambda i, *_: (i, 0, 0)),
            ],
        ),
        out_shape=[
            jax.ShapeDtypeStruct((b, t, hw), jnp.bfloat16),
            jax.ShapeDtypeStruct((b, heads, t), jnp.float32),
        ],
        compiler_params=pltpu.CompilerParams(vmem_limit_bytes=40 << 20),
        cost_estimate=pl.CostEstimate(flops=b*heads*t*t*HEAD_DIM*16, bytes_accessed=8*b*t*hw, transcendentals=b*heads*t*t),
        name="attention_forward",
    )(kind, start, qkv, segments[:, None, :], segments[:, :, None])

def bwd_kernel(heads, kind_ref, start_ref, qkv_ref, do_ref, ctx_ref, lse_ref, row_ref, col_ref, out_ref, dq_acc, delta_ref):
    b = pl.program_id(0)
    t = qkv_ref.shape[1]
    hw = heads * HEAD_DIM
    win = min(3 * SPAN, t)
    kind = kind_ref[b]

    def lanes(h, which=0):
        lo = which * hw + h * HEAD_DIM
        return slice(lo, lo + HEAD_DIM)

    for h in range(heads):
        prod = do_ref[0, :, lanes(h)].astype(jnp.float32) * ctx_ref[0, :, lanes(h)].astype(jnp.float32)
        d = jnp.sum(prod, axis=1, keepdims=True)
        delta_ref[h:h + 1, :] = jnp.transpose(jnp.broadcast_to(d, (t, 128)))[0:1, :]

    def back(h, keys, queries, masked):
        k = qkv_ref[0, keys, lanes(h, 1)]
        v = qkv_ref[0, keys, lanes(h, 2)]
        q = qkv_ref[0, queries, lanes(h, 0)]
        do = do_ref[0, queries, lanes(h)]
        s = dot(k, q, 1, 1)
        if masked:
            s = jnp.where(col_ref[0, keys, :] == row_ref[0, :, queries], s, MASKED)
        p = jnp.exp(s - lse_ref[0, h:h + 1, queries])
        dp = dot(v, do, 1, 1)
        ds = (p * (dp - delta_ref[h:h + 1, queries])).astype(jnp.bfloat16)
        dv = dot(p.astype(jnp.bfloat16), do, 1, 0)
        dk = dot(ds, q, 1, 0)
        out_ref[0, keys, lanes(h, 1)] = dk.astype(jnp.bfloat16)
        out_ref[0, keys, lanes(h, 2)] = dv.astype(jnp.bfloat16)
        return dot(k, ds, 0, 0)

    dq_acc[...] = jnp.zeros_like(dq_acc)

    def dense(masked):
        tile = min(256, t)
        def body(j, _):
            keys = pl.ds(pl.multiple_of(j * tile, tile), tile)
            for h in range(heads):
                dq_acc[h] += back(h, keys, pl.ds(0, t), masked)
            return 0
        lax.fori_loop(0, t // tile, body, 0)

    @pl.when(kind == 0)
    def _():
        dense(False)

    @pl.when(kind == 2)
    def _():
        dense(True)

    @pl.when(kind == 1)
    def _():
        def body(j, _):
            keys = pl.ds(pl.multiple_of(j * SPAN, SPAN), SPAN)
            queries = pl.ds(pl.multiple_of(start_ref[b, j], SPAN), win)
            for h in range(heads):
                dq_acc[h, :, queries] += back(h, keys, queries, True)
            return 0
        lax.fori_loop(0, t // SPAN, body, 0)

    for h in range(heads):
        dq = jnp.transpose(dq_acc[h]) * (HEAD_DIM ** -0.5)
        out_ref[0, :, lanes(h, 0)] = dq.astype(jnp.bfloat16)

def attention_back(qkv, dctx, ctx, lse, segments, kind, start):
    b, t, w = qkv.shape
    hw = w // 3
    heads = hw // HEAD_DIM
    return pl.pallas_call(
        functools.partial(bwd_kernel, heads),
        grid_spec=pltpu.PrefetchScalarGridSpec(
            num_scalar_prefetch=2,
            grid=(b,),
            in_specs=[
                pl.BlockSpec((1, t, w), lambda i, *_: (i, 0, 0)),
                pl.BlockSpec((1, t, hw), lambda i, *_: (i, 0, 0)),
                pl.BlockSpec((1, t, hw), lambda i, *_: (i, 0, 0)),
                pl.BlockSpec((1, heads, t), lambda i, *_: (i, 0, 0)),
                pl.BlockSpec((1, 1, t), lambda i, *_: (i, 0, 0)),
                pl.BlockSpec((1, t, 1), lambda i, *_: (i, 0, 0)),
            ],
            out_specs=pl.BlockSpec((1, t, w), lambda i, *_: (i, 0, 0)),
            scratch_shapes=[
                pltpu.VMEM((heads, HEAD_DIM, t), jnp.float32),
                pltpu.VMEM((heads, t), jnp.float32),
            ],
        ),
        out_shape=jax.ShapeDtypeStruct((b, t, w), jnp.bfloat16),
        compiler_params=pltpu.CompilerParams(vmem_limit_bytes=40 << 20),
        cost_estimate=pl.CostEstimate(flops=b*heads*t*t*HEAD_DIM*40, bytes_accessed=16*b*t*hw, transcendentals=b*heads*t*t),
        name="attention_backward",
    )(kind, start, qkv, dctx, ctx, lse, segments[:, None, :], segments[:, :, None])


AXES = ("seq", "z", "core")
ROWS = ("z", "core")
EXTRA = 16


def to_float(tensor):
    return tensor.astype(jnp.float32)


def low(tensor):
    return tensor.astype(jnp.bfloat16)


def product(left_side, right_side):
    return jnp.dot(left_side, right_side, preferred_element_type=jnp.float32)


def column_product(left_side, right_side):
    return dot(left_side, right_side, 0, 0)


def row_product(left_side, right_side):
    return dot(left_side, right_side, 1, 1)


def norm_forward(values, gain_vec, shift_vec):
    center = jnp.mean(values, axis=-1, keepdims=True)
    offset = values - center
    inverse = lax.rsqrt(jnp.mean(offset * offset, axis=-1, keepdims=True) + 1e-05)
    normed = offset * inverse
    return (normed * to_float(gain_vec) + to_float(shift_vec), normed, inverse)


def norm_backward(upstream, normed, inverse, gain_vec):
    scaled = upstream * to_float(gain_vec)
    centered = (
        scaled
        - jnp.mean(scaled, axis=-1, keepdims=True)
        - normed * jnp.mean(scaled * normed, axis=-1, keepdims=True)
    )
    return (inverse * centered, jnp.sum(upstream * normed, axis=0), jnp.sum(upstream, axis=0))


class Ring:
    def __init__(self):
        self.ranks = lax.axis_size("seq")
        self.chips = lax.axis_size("z")
        self.index = lax.axis_index("seq")
        self.core = lax.axis_index("core")
        self.count = self.ranks.bit_length() - 1

    def bit(self, k, core):
        if self.count == 2 and core == 1:
            k = 1 - k
        return 1 << k

    def offset(self, q, core):
        return sum(self.bit(k, core) for k in range(self.count) if q >> k & 1)

    def place(self, q):
        return jnp.bitwise_xor(self.index, jnp.where(self.core == 0, self.offset(q, 0), self.offset(q, 1)))

    def hop(self, block, k):
        pairs = []
        for s in range(self.ranks):
            for z in range(self.chips):
                for c in range(2):
                    to = s ^ self.bit(k, c)
                    pairs.append(((s * self.chips + z) * 2 + c, (to * self.chips + z) * 2 + c))
        return lax.ppermute(block, AXES, pairs)

    def gather(self, block):
        blocks = [block]
        for k in range(self.count):
            blocks = blocks + [self.hop(b, k) for b in blocks]
        return blocks

    def reduce(self, blocks):
        for k in range(self.count):
            kept = {}
            step = 1 << k
            for q in range(0, self.ranks, 2 * step):
                kept[q] = to_float(blocks[q]) + to_float(self.hop(low(blocks[q + step]), k))
            blocks = kept
        return blocks[0]

    def total(self, block):
        for k in range(self.count):
            block = to_float(block) + to_float(self.hop(low(block), k))
        return block


def swap(block):
    return lax.ppermute(block, "core", [(0, 1), (1, 0)])


def put(blocks, ring, axis):
    shape = list(blocks[0].shape)
    size = shape[axis]
    shape[axis] = size * len(blocks)
    whole = jnp.zeros(shape, blocks[0].dtype)
    for q, block in enumerate(blocks):
        whole = lax.dynamic_update_slice_in_dim(whole, block, ring.place(q) * size, axis)
    return whole


def local(
    hidden_in,
    segments,
    q_weight,
    k_weight,
    v_weight,
    out_weight,
    q_bias,
    v_bias,
    out_bias,
    up_weight,
    up_bias,
    down_weight,
    down_bias,
    norm1_gain,
    norm1_bias,
    norm2_gain,
    norm2_bias,
    out_grad,
):
    ring = Ring()
    here, core = ring.index, ring.core
    ranks, chips = ring.ranks, ring.chips
    owners = chips * 2
    owner = lax.axis_index("z") * 2 + core
    seqs, length, width = hidden_in.shape
    full = length * ranks
    head_width = width // ranks
    wide = 3 * head_width
    rows = width // owners
    units = down_weight.shape[0]
    part = units // ranks
    score_scale = HEAD_DIM ** (-0.5)
    kind, start = plan_rows(segments)

    heads_at = here * head_width
    mine = jnp.concatenate(
        [lax.dynamic_slice_in_dim(w, heads_at, head_width, 1) for w in (q_weight, k_weight, v_weight)], axis=1
    )
    vectors = (q_bias, v_bias, out_bias, down_bias, norm1_gain, norm1_bias, norm2_gain, norm2_bias, up_bias)
    packed = jnp.concatenate(vectors)
    packed = jnp.pad(packed, (0, EXTRA * wide - packed.shape[0])).reshape(EXTRA, wide)
    gathered = lax.all_gather(jnp.concatenate([mine, packed], axis=0), ROWS, axis=0)
    qkv_weight = gathered[:, :rows].reshape(width, wide)
    vectors = gathered[:, rows:].reshape(owners, EXTRA * wide)
    query_bias, value_bias, output_bias, lower_bias, gain_first, shift_first, gain_second, shift_second = (
        vectors[:, i * rows : (i + 1) * rows].reshape(width) for i in range(8)
    )
    upper_bias = vectors[:, 8 * rows : 8 * rows + units].reshape(chips, 2, ranks, part)
    upper_bias = lax.dynamic_index_in_dim(upper_bias, core, 1, False)

    def up_columns(of_core):
        return jnp.concatenate(
            [
                lax.dynamic_slice_in_dim(up_weight, ((z * 2 + of_core) * ranks + here) * part, part, 1)
                for z in range(chips)
            ],
            axis=1,
        )

    own_up, other_up = up_columns(core), swap(up_columns(1 - core))
    first_core = core == 0
    up_rows = jnp.concatenate(
        [jnp.where(first_core, own_up, other_up), jnp.where(first_core, other_up, own_up)], axis=0
    )
    up_block = lax.all_gather(up_rows, "z", axis=0, tiled=True)
    down_block = lax.all_gather(
        lax.dynamic_slice_in_dim(down_weight, here * part, part, 0), "z", axis=0, tiled=True
    )
    output_weight = lax.all_gather(out_weight, ROWS, axis=0, tiled=True)
    up_blocks = ring.gather(up_block)
    down_blocks = ring.gather(down_block)

    tokens = put(ring.gather(hidden_in), ring, 1).reshape(-1, width)
    bias_at = (lax.dynamic_slice_in_dim(query_bias, heads_at, head_width), lax.dynamic_slice_in_dim(value_bias, heads_at, head_width))
    qkv_bias = to_float(jnp.concatenate([bias_at[0], jnp.zeros_like(bias_at[0]), bias_at[1]]))
    column = jnp.arange(wide)
    qkv = low(product(tokens, qkv_weight) + qkv_bias)
    qkv = qkv * low(jnp.where(column < head_width, score_scale, 1.0))
    qkv = qkv.reshape(seqs, full, wide)
    contexts, log_totals = attention(qkv, segments, kind, start)
    context_rows = lax.all_to_all(contexts, "seq", split_axis=1, concat_axis=2, tiled=True).reshape(-1, width)

    own_rows = hidden_in.reshape(-1, width)
    branch = product(context_rows, output_weight) + to_float(output_bias)
    first, normed_one, inverse_one = norm_forward(to_float(own_rows) + branch, gain_first, shift_first)

    own_count = own_rows.shape[0]
    first_low = low(first)
    pair_low = jnp.concatenate([first_low, swap(first_low)], axis=0)
    actives, slopes = [], []
    mixed = 0.0
    for q in range(ranks):
        bias = lax.dynamic_index_in_dim(upper_bias, ring.place(q), 1, False).reshape(-1)
        upper = product(pair_low, up_blocks[q]) + to_float(bias)
        tail = 0.5 * (1.0 + lax.erf(upper * 0.7071067811865476))
        actives.append(low(upper * tail))
        slopes.append(low(tail + upper * jnp.exp(-0.5 * upper * upper) * 0.3989422804014327))
        mixed = mixed + product(actives[q], down_blocks[q])
    mixed = mixed[:own_count] + to_float(swap(low(mixed[own_count:]))) + to_float(lower_bias)
    result, normed_two, inverse_two = norm_forward(first + mixed, gain_second, shift_second)
    layer_out = low(result).reshape(hidden_in.shape)

    local_docs = lax.dynamic_slice_in_dim(segments, here * length, length, 1)
    cotangent = to_float(out_grad).reshape(-1, width) * to_float(local_docs.reshape(-1, 1) != 0)
    dsum_two, gain_two_grad, shift_two_grad = norm_backward(cotangent, normed_two, inverse_two, gain_second)
    dmixed = low(dsum_two)
    lower_bias_grad = jnp.sum(to_float(dmixed), axis=0)
    pair_dmixed = jnp.concatenate([dmixed, swap(dmixed)], axis=0)
    down_grads, up_grads, up_bias_grads = [], [], []
    dfirst = 0.0
    for q in range(ranks):
        down_grads.append(low(column_product(actives[q], pair_dmixed)))
        dupper = low(row_product(pair_dmixed, down_blocks[q]) * to_float(slopes[q]))
        up_grads.append(low(column_product(pair_low, dupper)))
        up_bias_grads.append(jnp.sum(to_float(dupper), axis=0).reshape(chips, 1, part))
        dfirst = dfirst + row_product(dupper, up_blocks[q])
    dfirst = dsum_two + dfirst[:own_count] + to_float(swap(low(dfirst[own_count:])))
    dsum_one, gain_one_grad, shift_one_grad = norm_backward(dfirst, normed_one, inverse_one, gain_first)
    dbranch = low(dsum_one)
    output_bias_grad = jnp.sum(to_float(dbranch), axis=0)
    dcontext = low(row_product(dbranch, output_weight)).reshape(seqs, length, width)
    dcontexts = lax.all_to_all(dcontext, "seq", split_axis=2, concat_axis=1, tiled=True)
    dqkv = attention_back(qkv, dcontexts, contexts, log_totals, segments, kind, start)

    down_shard = lax.psum_scatter(low(ring.reduce(down_grads)), "z", scatter_dimension=0, tiled=True)
    down_weight_grad = put(ring.gather(down_shard), ring, 0)
    up_shard = lax.psum_scatter(low(ring.reduce(up_grads)), "z", scatter_dimension=0, tiled=True)
    keep_part = lax.dynamic_slice_in_dim(up_shard, core * rows, rows, 0)
    take_part = swap(lax.dynamic_slice_in_dim(up_shard, (1 - core) * rows, rows, 0))
    up_pair = jnp.stack([jnp.where(first_core, keep_part, take_part), jnp.where(first_core, take_part, keep_part)])
    up_all = put([b[None] for b in ring.gather(up_pair)], ring, 0)
    up_weight_grad = (
        up_all.reshape(ranks, 2, rows, chips, part).transpose(2, 3, 1, 0, 4).reshape(rows, owners * units)
    )

    output_weight_grad = low(column_product(context_rows, dbranch)).reshape(owners, rows, width)
    up_bias_sum = put(up_bias_grads, ring, 1)
    up_bias_sum = jnp.where(jnp.arange(2)[None, :, None, None] == core, up_bias_sum[:, None], 0.0)
    small = jnp.concatenate(
        [
            v.reshape(owners, -1)
            for v in (output_bias_grad, lower_bias_grad, gain_one_grad, shift_one_grad, gain_two_grad, shift_two_grad, up_bias_sum)
        ],
        axis=1,
    )
    small = low(jnp.pad(small, ((0, 0), (0, EXTRA * width - small.shape[1])))).reshape(owners, EXTRA, width)
    out_pack = jnp.concatenate([output_weight_grad, small], axis=1).reshape(-1, width)
    out_pack = ring.total(lax.psum_scatter(out_pack, ROWS, scatter_dimension=0, tiled=True))
    small = out_pack[rows:].reshape(-1)

    dqkv_rows = dqkv.reshape(-1, wide)
    qkv_grad = low(column_product(tokens, dqkv_rows)).reshape(owners, rows, wide)
    qkv_bias_grad = jnp.sum(to_float(dqkv_rows), axis=0)
    qkv_bias_rows = jnp.broadcast_to(
        jnp.pad(low(qkv_bias_grad)[None], ((0, EXTRA - 1), (0, 0)))[None], (owners, EXTRA, wide)
    )
    qkv_pack = jnp.concatenate([qkv_grad, qkv_bias_rows], axis=1).reshape(-1, wide)
    qkv_pack = lax.psum_scatter(qkv_pack, ROWS, scatter_dimension=0, tiled=True)
    qkv_all = put([b[None] for b in ring.gather(qkv_pack)], ring, 0)
    qkv_all = qkv_all.reshape(ranks, rows + EXTRA, 3, head_width).transpose(2, 1, 0, 3).reshape(3, rows + EXTRA, width)
    qkv_all = to_float(qkv_all)
    bias_all = lax.dynamic_slice_in_dim(qkv_all[:, rows], owner * rows, rows, 1)

    dinput = row_product(dqkv_rows, qkv_weight).reshape(seqs, full, width)
    dinput = [
        lax.dynamic_slice_in_dim(dinput, ring.place(q) * length, length, 1) for q in range(ranks)
    ]
    input_grad = dsum_one.reshape(hidden_in.shape) + ring.reduce(dinput)

    def piece(i):
        return small[i * rows : (i + 1) * rows]

    return (
        layer_out,
        input_grad,
        qkv_all[0, :rows],
        qkv_all[1, :rows],
        qkv_all[2, :rows],
        out_pack[:rows],
        bias_all[0],
        bias_all[2],
        piece(0),
        to_float(up_weight_grad),
        small[6 * rows : 6 * rows + units],
        to_float(down_weight_grad),
        piece(1),
        piece(2),
        piece(3),
        piece(4),
        piece(5),
    )


def solution(mesh):
    ranks, owners = mesh.shape["seq"], mesh.shape["fsdp"]
    grid = Mesh(mesh.devices.reshape(ranks, owners // 2, 2), AXES)
    tokens, matrix, vector = P(ROWS, "seq", None), P(ROWS, None), P(ROWS)
    return jax.shard_map(
        local,
        mesh=grid,
        in_specs=(
            tokens,
            matrix,
            matrix,
            matrix,
            matrix,
            matrix,
            vector,
            vector,
            vector,
            matrix,
            vector,
            matrix,
            vector,
            vector,
            vector,
            vector,
            vector,
            tokens,
        ),
        out_specs=(
            tokens,
            tokens,
            matrix,
            matrix,
            matrix,
            matrix,
            vector,
            vector,
            vector,
            matrix,
            vector,
            matrix,
            vector,
            vector,
            vector,
            vector,
            vector,
        ),
        check_vma=False,
    )
```

```python
import functools

import jax
import jax.numpy as jnp
from jax import lax
from jax.experimental import pallas as pl
from jax.experimental.pallas import tpu as pltpu
from jax.sharding import Mesh
from jax.sharding import PartitionSpec as P

HEAD_DIM = 64
SPAN = 128
MASKED = -1e30


def dot(a,b,ca,cb):
    return lax.dot_general(a,b,(((ca,),(cb,)),((),())),preferred_element_type=jnp.float32)


TILE = 256


def run(kernel, name, grid, ins, outs, shapes, operands, prefetch=(), scratch=(), alias=None, waits=(), cost=10):
    known = len(prefetch) + len(ins)

    def waiting(*refs):
        kernel(*refs[:known], *refs[known + len(waits) :])

    ins = list(ins) + [pl.BlockSpec(memory_space=pl.ANY)] * len(waits)
    operands = list(operands) + list(waits)
    return pl.pallas_call(
        waiting,
        grid_spec=pltpu.PrefetchScalarGridSpec(
            num_scalar_prefetch=len(prefetch), grid=grid, in_specs=ins, out_specs=outs, scratch_shapes=scratch
        ),
        out_shape=shapes,
        input_output_aliases=alias or {},
        compiler_params=pltpu.CompilerParams(vmem_limit_bytes=28 << 20),
        cost_estimate=pl.CostEstimate(flops=cost * 1000000000, bytes_accessed=1000, transcendentals=0),
        name=name,
    )(*prefetch, *operands)


def fixed(array):
    rank = array.ndim
    return pl.BlockSpec(array.shape, lambda *_: (0,) * rank, pipeline_mode=pl.Buffered(buffer_count=1))


class View:
    def __init__(self, array, i=None):
        self.array, self.i = array, i
        self.shape = array.shape if i is None else array.shape[1:]

    def spec(self, block, place):
        i = self.i
        if i is None:
            return pl.BlockSpec(block, place)
        return pl.BlockSpec((None,) + tuple(block), lambda *a: (i,) + tuple(place(*a)))

    def whole(self):
        rank, i = len(self.shape), self.i
        once = pl.Buffered(buffer_count=1)
        if i is None:
            return pl.BlockSpec(self.shape, lambda *_: (0,) * rank, pipeline_mode=once)
        return pl.BlockSpec((None,) + tuple(self.shape), lambda *_: (i,) + (0,) * rank, pipeline_mode=once)

    def value(self):
        return self.array if self.i is None else self.array[self.i]


def arrays(views):
    return [v.array for v in views]


def kind_of(shape, dtype=jnp.bfloat16):
    return jax.ShapeDtypeStruct(tuple(shape), dtype)


def wide(tensor):
    return tensor.astype(jnp.float32)


def standardize(values):
    center = jnp.mean(values, axis=1, keepdims=True)
    offset = values - center
    inverse = lax.rsqrt(jnp.mean(offset * offset, axis=1, keepdims=True) + 1e-05)
    return offset * inverse, inverse


def standardize_back(upstream, normed, inverse, gain):
    scaled = upstream * gain
    return inverse * (
        scaled
        - jnp.mean(scaled, axis=1, keepdims=True)
        - normed * jnp.mean(scaled * normed, axis=1, keepdims=True)
    )


def column_sum(values):
    return jnp.sum(values, axis=0, keepdims=True)


OUT_BIAS, DOWN_BIAS, GAIN_ONE, SHIFT_ONE, GAIN_TWO, SHIFT_TWO = 2, 3, 4, 5, 6, 7


def project(places, blocks, weight, bias, scale):
    seqs, length, width = blocks[0].shape
    ranks = len(blocks)
    out_width = weight.shape[1]

    def kernel(place_ref, weight_ref, bias_ref, scale_ref, *refs):
        for q in range(ranks):

            @pl.when(pl.program_id(0) // seqs == q)
            def _(q=q):
                product = dot(refs[q][0], weight_ref[...], 1, 0) + bias_ref[...]
                refs[ranks][0] = (product * scale_ref[...]).astype(jnp.bfloat16)

    def source(q):
        return lambda i, p: (jnp.clip(i - q * seqs, 0, seqs - 1), 0, 0)

    return run(
        kernel,
        "project",
        (ranks * seqs,),
        [fixed(weight), fixed(bias), fixed(scale)]
        + [blocks[q].spec((1, length, width), source(q)) for q in range(ranks)],
        pl.BlockSpec((1, length, out_width), lambda i, p: (i % seqs, p[i // seqs], 0)),
        kind_of((seqs, length * ranks, out_width)),
        [weight, bias, scale, *arrays(blocks)],
        prefetch=(places,),
    )


def out_norm(places, contexts, weight, hidden, vectors, waits=()):
    seqs, length, width = hidden.shape
    ranks = len(contexts)
    part = contexts[0].shape[2]

    def kernel(place_ref, *refs):
        weight_ref, hidden_ref, vector_ref, sum_ref, first_ref = refs[ranks:]
        total = wide(hidden_ref[0]) + vector_ref[OUT_BIAS : OUT_BIAS + 1, :]
        for q in range(ranks):
            rows = pl.ds(pl.multiple_of(place_ref[q] * part, part), part)
            total = total + dot(refs[q][0], weight_ref[rows, :], 1, 0)
        sum_ref[0] = total
        normed, _ = standardize(total)
        first = normed * vector_ref[GAIN_ONE : GAIN_ONE + 1, :] + vector_ref[SHIFT_ONE : SHIFT_ONE + 1, :]
        first_ref[0] = first.astype(jnp.bfloat16)

    tokens = pl.BlockSpec((1, length, width), lambda b, p: (b, 0, 0))
    return run(
        kernel,
        "out_norm",
        (seqs,),
        [pl.BlockSpec((1, length, part), lambda b, p: (b, 0, 0))] * ranks + [fixed(weight), tokens, fixed(vectors)],
        [tokens, tokens],
        [kind_of(hidden.shape, jnp.float32), kind_of(hidden.shape)],
        [*contexts, weight, hidden, vectors],
        prefetch=(places,),
        waits=waits,
    )


def up_forward(own, other, weights, biases, waits=()):
    count, width = own.shape
    units = weights[0].shape[1]
    blocks = len(weights)
    tile = min(TILE, count)
    half = count // tile

    def kernel(own_ref, other_ref, *refs):
        def body(tokens):
            for q in range(blocks):
                upper = dot(tokens, refs[q][...], 1, 0) + refs[blocks + q][...]
                tail = 0.5 * (1.0 + lax.erf(upper * 0.7071067811865476))
                refs[2 * blocks + q][...] = (upper * tail).astype(jnp.bfloat16)
                bell = jnp.exp(-0.5 * upper * upper) * 0.3989422804014327
                refs[3 * blocks + q][...] = (tail + upper * bell).astype(jnp.bfloat16)

        @pl.when(pl.program_id(0) < half)
        def _():
            body(own_ref[...])

        @pl.when(pl.program_id(0) >= half)
        def _():
            body(other_ref[...])

    outs = run(
        kernel,
        "up_forward",
        (2 * half,),
        [
            pl.BlockSpec((tile, width), lambda i: (jnp.minimum(i, half - 1), 0)),
            pl.BlockSpec((tile, width), lambda i: (jnp.maximum(i - half, 0), 0)),
        ]
        + [w.whole() for w in weights]
        + [fixed(b) for b in biases],
        [pl.BlockSpec((tile, units), lambda i: (i, 0))] * (2 * blocks),
        [kind_of((2 * count, units))] * (2 * blocks),
        [own, other, *arrays(weights), *biases],
        waits=waits,
    )
    return list(outs[:blocks]), list(outs[blocks:])


def down_forward(actives, weights, first, count, dtype, waits=()):
    blocks = len(actives)
    units, width = weights[0].shape
    tile = min(TILE, count)

    def kernel(*refs):
        total = dot(refs[0][...], refs[blocks][...], 1, 0)
        for q in range(1, blocks):
            total = total + dot(refs[q][...], refs[blocks + q][...], 1, 0)
        refs[-1][...] = total.astype(dtype)

    return run(
        kernel,
        "down_forward",
        (count // tile,),
        [pl.BlockSpec((tile, units), lambda i: (i + first // tile, 0))] * blocks + [w.whole() for w in weights],
        pl.BlockSpec((tile, width), lambda i: (i, 0)),
        kind_of((count, width), dtype),
        [*actives, *arrays(weights)],
        waits=waits,
    )


def norm_two(mixed, mixed_other, sums_one, vectors, out_grad, keep):
    seqs, length, width = sums_one.shape

    def kernel(mixed_ref, other_ref, sum_ref, vector_ref, grad_ref, keep_ref, out_ref, dsum_ref, dmixed_ref, total_ref):
        @pl.when(pl.program_id(0) == 0)
        def _():
            total_ref[...] = jnp.zeros_like(total_ref)

        def vector(i):
            return vector_ref[i : i + 1, :]

        normed, _ = standardize(sum_ref[0])
        first = normed * vector(GAIN_ONE) + vector(SHIFT_ONE)
        mixed = mixed_ref[0] + wide(other_ref[0]) + vector(DOWN_BIAS)
        normed, inverse = standardize(first + mixed)
        out_ref[0] = (normed * vector(GAIN_TWO) + vector(SHIFT_TWO)).astype(jnp.bfloat16)
        cot = wide(grad_ref[0]) * keep_ref[0]
        dsum = standardize_back(cot, normed, inverse, vector(GAIN_TWO))
        dsum_ref[0] = dsum
        dmixed = dsum.astype(jnp.bfloat16)
        dmixed_ref[0] = dmixed
        total_ref[0:1, :] += column_sum(wide(dmixed))
        total_ref[1:2, :] += column_sum(cot * normed)
        total_ref[2:3, :] += column_sum(cot)

    tokens = pl.BlockSpec((1, length, width), lambda b: (b, 0, 0))
    shape = sums_one.shape
    return run(
        kernel,
        "norm_two",
        (seqs,),
        [tokens, tokens, tokens, fixed(vectors), tokens, pl.BlockSpec((1, length, 1), lambda b: (b, 0, 0))],
        [tokens, tokens, tokens, pl.BlockSpec((8, width), lambda b: (0, 0))],
        [kind_of(shape), kind_of(shape, jnp.float32), kind_of(shape), kind_of((8, width), jnp.float32)],
        [mixed.reshape(shape), mixed_other.reshape(shape), sums_one, vectors, out_grad, keep],
    )


def ffn_back(own, other, slopes, downs, ups, waits=()):
    blocks = len(slopes)
    count, width = own.shape
    units = slopes[0].shape[1]
    tile = min(TILE, count)
    half = count // tile

    def kernel(own_ref, other_ref, *refs):
        slope_refs, down_refs, up_refs = refs[:blocks], refs[blocks : 2 * blocks], refs[2 * blocks : 3 * blocks]
        upper_refs, total_ref, here_ref, there_ref = refs[3 * blocks : 4 * blocks], refs[-3], refs[-2], refs[-1]
        step = pl.program_id(0)

        @pl.when(step == 0)
        def _():
            total_ref[...] = jnp.zeros_like(total_ref)

        def body(grad):
            total = 0.0
            for q in range(blocks):
                upper = (dot(grad, down_refs[q][...], 1, 1) * wide(slope_refs[q][...])).astype(jnp.bfloat16)
                upper_refs[q][...] = upper
                total_ref[q : q + 1, :] += column_sum(wide(upper))
                total = total + dot(upper, up_refs[q][...], 1, 1)
            return total

        @pl.when(step < half)
        def _():
            there_ref[...] = body(other_ref[...]).astype(jnp.bfloat16)

        @pl.when(step >= half)
        def _():
            here_ref[...] = body(own_ref[...])

    def early(i):
        return (jnp.minimum(i, half - 1), 0)

    def late(i):
        return (jnp.maximum(i - half, 0), 0)

    def both(i):
        return ((i + half) % (2 * half), 0)

    outs = run(
        kernel,
        "feed_forward_back",
        (2 * half,),
        [pl.BlockSpec((tile, width), late), pl.BlockSpec((tile, width), early)]
        + [pl.BlockSpec((tile, units), both)] * blocks
        + [w.whole() for w in (*downs, *ups)],
        [pl.BlockSpec((tile, units), both)] * blocks
        + [
            pl.BlockSpec((max(8, blocks), units), lambda i: (0, 0)),
            pl.BlockSpec((tile, width), late),
            pl.BlockSpec((tile, width), early),
        ],
        [kind_of((2 * count, units))] * blocks
        + [
            kind_of((max(8, blocks), units), jnp.float32),
            kind_of((count, width), jnp.float32),
            kind_of((count, width)),
        ],
        [own, other, *slopes, *arrays(downs), *arrays(ups)],
        waits=waits,
    )
    return list(outs[:blocks]), outs[blocks], outs[blocks + 1], outs[blocks + 2]


def down_grad(actives, own, other, addends, waits=()):
    count, width = own.shape
    units = actives[0].shape[1]
    tile = min(TILE, units)
    blocks = len(actives)
    spread = [(q, a) for q in range(blocks) for a in addends[q]]

    def kernel(own_ref, other_ref, *refs):
        for q in range(blocks):
            total = dot(refs[q][:count, :], own_ref[...], 0, 0) + dot(refs[q][count:, :], other_ref[...], 0, 0)
            for j, (of, _) in enumerate(spread):
                if of == q:
                    total = total + wide(refs[blocks + j][...])
            refs[-1][q] = total.astype(jnp.bfloat16)

    return run(
        kernel,
        "down_grad",
        (units // tile,),
        [fixed(own), fixed(other)]
        + [pl.BlockSpec((2 * count, tile), lambda i: (0, i))] * blocks
        + [a.spec((tile, width), lambda i: (i, 0)) for _, a in spread],
        pl.BlockSpec((blocks, tile, width), lambda i: (0, i, 0)),
        kind_of((blocks, units, width)),
        [own, other, *actives, *(a.array for _, a in spread)],
        waits=waits,
    )


def up_grad(uppers, own, other, addends, waits=()):
    count, width = own.shape
    units = uppers[0].shape[1]
    tile = min(TILE, width)
    blocks = len(uppers)
    spread = [(q, a) for q in range(blocks) for a in addends[q]]

    def kernel(own_ref, other_ref, *refs):
        for q in range(blocks):
            total = dot(own_ref[...], refs[q][:count, :], 0, 0) + dot(other_ref[...], refs[q][count:, :], 0, 0)
            for j, (of, _) in enumerate(spread):
                if of == q:
                    total = total + wide(refs[blocks + j][...])
            refs[-1][q] = total.astype(jnp.bfloat16)

    columns = pl.BlockSpec((count, tile), lambda i: (0, i))
    return run(
        kernel,
        "up_grad",
        (width // tile,),
        [columns, columns]
        + [fixed(u) for u in uppers]
        + [a.spec((tile, units), lambda i: (i, 0)) for _, a in spread],
        pl.BlockSpec((blocks, tile, units), lambda i: (0, i, 0)),
        kind_of((blocks, width, units)),
        [own, other, *uppers, *(a.array for _, a in spread)],
        waits=waits,
    )


def norm_one_back(places, dfirst, dfirst_other, dsum_two, sums_one, vectors, weight, part, waits=()):
    seqs, length, width = sums_one.shape
    ranks = width // part

    def kernel(place_ref, own_ref, other_ref, dsum_ref, sum_ref, vector_ref, weight_ref, *outs):
        @pl.when(pl.program_id(0) == 0)
        def _():
            outs[-1][...] = jnp.zeros_like(outs[-1])

        upstream = dsum_ref[0] + own_ref[0] + wide(other_ref[0])
        normed, inverse = standardize(sum_ref[0])
        dsum = standardize_back(upstream, normed, inverse, vector_ref[GAIN_ONE : GAIN_ONE + 1, :])
        outs[0][0] = dsum
        dbranch = dsum.astype(jnp.bfloat16)
        outs[1][0] = dbranch
        for q in range(ranks):
            rows = pl.ds(pl.multiple_of(place_ref[q] * part, part), part)
            outs[2 + q][0] = dot(dbranch, weight_ref[rows, :], 1, 1).astype(jnp.bfloat16)
        outs[-1][0:1, :] += column_sum(wide(dbranch))
        outs[-1][1:2, :] += column_sum(upstream * normed)
        outs[-1][2:3, :] += column_sum(upstream)

    tokens = pl.BlockSpec((1, length, width), lambda b, p: (b, 0, 0))
    shape = sums_one.shape
    outs = run(
        kernel,
        "norm_one_back",
        (seqs,),
        [tokens, tokens, tokens, tokens, fixed(vectors), fixed(weight)],
        [tokens, tokens]
        + [pl.BlockSpec((1, length, part), lambda b, p: (b, 0, 0))] * ranks
        + [pl.BlockSpec((8, width), lambda b, p: (0, 0))],
        [kind_of(shape, jnp.float32), kind_of(shape)]
        + [kind_of((seqs, length, part))] * ranks
        + [kind_of((8, width), jnp.float32)],
        [dfirst.reshape(shape), dfirst_other.reshape(shape), dsum_two, sums_one, vectors, weight],
        prefetch=(places,),
        waits=waits,
    )
    return outs[0], outs[1], list(outs[2 : 2 + ranks]), outs[-1]


def out_grad_pack(places, contexts, dbranch, small, owners, waits=()):
    seqs, length, width = dbranch.shape
    ranks = len(contexts)
    part = contexts[0].shape[2]
    rows = width // owners
    extra = small.shape[0]
    each = part // rows

    def kernel(place_ref, *refs):
        dbranch_ref, small_ref, out_ref = refs[ranks:]
        grad = dbranch_ref[...].reshape(seqs * length, width)
        for q in range(ranks):
            product = dot(refs[q][...].reshape(seqs * length, part), grad, 0, 0).astype(jnp.bfloat16)
            for e in range(each):
                out_ref[place_ref[q] * each + e, :rows, :] = product[e * rows : (e + 1) * rows, :]
        for f in range(owners):
            out_ref[f, rows:, :] = jnp.zeros((extra, width), jnp.bfloat16)
            out_ref[f, rows:, :rows] = small_ref[:, f * rows : (f + 1) * rows]

    shape = (owners, rows + extra, width)
    return run(
        kernel,
        "out_grad_pack",
        (1,),
        [fixed(c) for c in contexts] + [fixed(dbranch), fixed(small)],
        pl.BlockSpec(shape, lambda i, p: (0, 0, 0)),
        kind_of(shape),
        [*contexts, dbranch, small],
        prefetch=(places,),
        waits=waits,
    )


def hidden_grad(places, dqkv, weight, length, picks, addends, dtype, waits=()):
    seqs, _, out_width = dqkv.shape
    width = weight.shape[0]
    blocks = len(picks)
    spread = [(k, a) for k in range(blocks) for a in addends[k]]

    def kernel(place_ref, weight_ref, *refs):
        for k in range(blocks):
            total = dot(refs[k][0], weight_ref[...], 1, 1)
            for j, (of, _) in enumerate(spread):
                if of == k:
                    total = total + wide(refs[blocks + j][0])
            refs[-1][k, 0] = total.astype(dtype)

    return run(
        kernel,
        "hidden_grad",
        (seqs,),
        [fixed(weight)]
        + [pl.BlockSpec((1, length, out_width), lambda b, p, q=q: (b, p[q], 0)) for q in picks]
        + [a.spec((1, length, width), lambda b, p: (b, 0, 0)) for _, a in spread],
        pl.BlockSpec((blocks, 1, length, width), lambda b, p: (0, b, 0, 0)),
        kind_of((blocks, seqs, length, width), dtype),
        [weight] + [dqkv] * blocks + [a.array for _, a in spread],
        prefetch=(places,),
        waits=waits,
        cost=10,
    )


def project_grad_pack(places, blocks, dqkv, owners, extra, waits=()):
    seqs, length, width = blocks[0].shape
    ranks = len(blocks)
    out_width = dqkv.shape[2]
    rows = width // owners
    group = max(1, TILE // rows)

    def kernel(place_ref, *refs):
        dqkv_ref, out_ref, total_ref = refs[ranks:]

        @pl.when(pl.program_id(0) == 0)
        def _():
            total_ref[...] = jnp.zeros_like(total_ref)
            total_ref[0:1, :] = column_sum(wide(dqkv_ref[...].reshape(-1, out_width)))

        total = 0.0
        for q in range(ranks):
            at = pl.ds(pl.multiple_of(place_ref[q] * length, length), length)
            for b in range(seqs):
                total = total + dot(refs[q][b], dqkv_ref[b, at, :], 0, 0)
        total = total.astype(jnp.bfloat16)
        sums = total_ref[...].astype(jnp.bfloat16)
        for e in range(group):
            out_ref[e, :rows, :] = total[e * rows : (e + 1) * rows, :]
            out_ref[e, rows:, :] = sums

    return run(
        kernel,
        "project_grad_pack",
        (owners // group,),
        [x.spec((seqs, length, group * rows), lambda i, p: (0, 0, i)) for x in blocks] + [fixed(dqkv)],
        pl.BlockSpec((group, rows + extra, out_width), lambda i, p: (i, 0, 0)),
        kind_of((owners, rows + extra, out_width)),
        [*arrays(blocks), dqkv],
        prefetch=(places,),
        scratch=(pltpu.VMEM((extra, out_width), jnp.float32),),
        waits=waits,
        cost=10,
    )


def lay_columns(places, blocks, rows):
    total, out_width = blocks[0].shape
    part = out_width // 3
    ranks = len(blocks)
    width = part * ranks

    def kernel(place_ref, *refs):
        for q in range(ranks):
            at = pl.ds(pl.multiple_of(place_ref[q] * part, part), part)
            for k in range(3):
                block = wide(refs[q][:, k * part : (k + 1) * part])
                refs[ranks + k][:, at] = block[:rows, :]
                refs[ranks + 3 + k][:, at] = block[rows : rows + 8, :]

    shape, below = (rows, width), (8, width)
    return run(
        kernel,
        "lay_columns",
        (1,),
        [b.whole() for b in blocks],
        [pl.BlockSpec(shape, lambda i, p: (0, 0))] * 3 + [pl.BlockSpec(below, lambda i, p: (0, 0))] * 3,
        [kind_of(shape, jnp.float32)] * 3 + [kind_of(below, jnp.float32)] * 3,
        arrays(blocks),
        prefetch=(places,),
        cost=10,
    )


def lay_up(places, blocks, chips, part):
    _, rows, _ = blocks[0].shape
    ranks = len(blocks)
    shape = (rows, 2 * chips * ranks * part)

    def kernel(place_ref, *refs):
        for q in range(ranks):
            for c in range(2):
                for z in range(chips):
                    at = pl.multiple_of(((z * 2 + c) * ranks + place_ref[q]) * part, part)
                    refs[ranks][:, pl.ds(at, part)] = wide(refs[q][c, :, z * part : (z + 1) * part])

    return run(
        kernel,
        "lay_up",
        (1,),
        [b.whole() for b in blocks],
        pl.BlockSpec(shape, lambda i, p: (0, 0)),
        kind_of(shape, jnp.float32),
        arrays(blocks),
        prefetch=(places,),
        cost=10,
    )


def lay_rows(places, blocks, waits=()):
    part, width = blocks[0].shape
    ranks = len(blocks)
    shape = (part * ranks, width)

    def kernel(place_ref, *refs):
        for q in range(ranks):
            refs[ranks][pl.ds(pl.multiple_of(place_ref[q] * part, part), part), :] = wide(refs[q][...])

    return run(
        kernel,
        "lay_rows",
        (1,),
        [b.whole() for b in blocks],
        pl.BlockSpec(shape, lambda i, p: (0, 0)),
        kind_of(shape, jnp.float32),
        arrays(blocks),
        prefetch=(places,),
        waits=waits,
        cost=10,
    )


def lay_chips(at, blocks, waits):
    rows, width = blocks[0].shape
    chips = len(blocks)

    def kernel(at_ref, *refs):
        for d in range(chips):
            refs[chips][at_ref[d]] = refs[d][...]

    shape = (chips, rows, width)
    return run(
        kernel,
        "lay_chips",
        (1,),
        [fixed(b) for b in blocks],
        pl.BlockSpec(shape, lambda i, p: (0, 0, 0)),
        kind_of(shape),
        blocks,
        prefetch=(at,),
        cost=100,
        waits=waits,
    )


def hold(array, waits):
    def kernel(from_ref, to_ref):
        to_ref[...] = from_ref[...]

    rank = array.ndim
    return run(
        kernel,
        "hold",
        (1,),
        [fixed(array)],
        pl.BlockSpec(array.shape, lambda i: (0,) * rank),
        kind_of(array.shape, array.dtype),
        [array],
        waits=waits,
    )


def split(at, own, size, waits=()):
    _, width = own.shape
    chips = at.shape[0]

    def kernel(at_ref, own_ref, *outs):
        for d in range(chips):
            outs[d][...] = own_ref[pl.ds(pl.multiple_of(at_ref[d] * size, size), size), :]

    return run(
        kernel,
        "split",
        (1,),
        [fixed(own)],
        [pl.BlockSpec((size, width), lambda i, p: (0, 0))] * chips,
        [kind_of((size, width))] * chips,
        [own],
        prefetch=(at,),
        waits=waits,
    )


def tick(*waits, cost=10):
    def kernel(out_ref):
        out_ref[...] = jnp.zeros_like(out_ref)

    return run(
        kernel, "tick", (1,), [], pl.BlockSpec((8, 128), lambda i: (0, 0)), kind_of((8, 128), jnp.float32), [], waits=waits, cost=cost
    )


def total_rows(pieces, waits=()):
    def kernel(*refs):
        total = wide(refs[0][...])
        for ref in refs[1:-1]:
            total = total + wide(ref[...])
        refs[-1][...] = total.astype(jnp.bfloat16)

    shape = pieces[0].shape
    return run(
        kernel,
        "total_rows",
        (1,),
        [fixed(p) for p in pieces],
        pl.BlockSpec(shape, lambda i: (0, 0)),
        kind_of(shape),
        pieces,
        waits=waits,
    )


def total_halves(core, pieces, waits=()):
    rows, width = pieces[0].shape
    half = rows // 2

    def kernel(core_ref, *refs):
        for out_ref, of in ((refs[-2], core_ref[0]), (refs[-1], 1 - core_ref[0])):
            at = pl.ds(pl.multiple_of(of * half, half), half)
            total = wide(refs[0][at, :])
            for ref in refs[1:-2]:
                total = total + wide(ref[at, :])
            out_ref[...] = total.astype(jnp.bfloat16)

    return run(
        kernel,
        "total_halves",
        (1,),
        [fixed(p) for p in pieces],
        [pl.BlockSpec((half, width), lambda i, p: (0, 0))] * 2,
        [kind_of((half, width))] * 2,
        pieces,
        prefetch=(core,),
        waits=waits,
    )


def pair(core, own, other, waits=()):
    rows, width = own.shape

    def kernel(core_ref, own_ref, other_ref, out_ref):
        out_ref[core_ref[0]] = own_ref[...]
        out_ref[1 - core_ref[0]] = other_ref[...]

    shape = (2, rows, width)
    return run(
        kernel,
        "pair",
        (1,),
        [fixed(own), fixed(other)],
        pl.BlockSpec(shape, lambda i, p: (0, 0, 0)),
        kind_of(shape),
        [own, other],
        prefetch=(core,),
        waits=waits,
    )


def plan_rows(segments):
    b, t = segments.shape
    n = t // SPAN
    win = min(3 * SPAN, t)
    spans = segments.reshape(b, n, SPAN)
    place = jnp.arange(t, dtype=jnp.int32)
    low = jnp.min(jnp.where(segments[:, None, :] == spans[:, :, :1], place, t), axis=2)
    high = jnp.max(jnp.where(segments[:, None, :] == spans[:, :, -1:], place, -1), axis=2)
    start = jnp.minimum(low // SPAN * SPAN, t - win)
    fits = jnp.all(high < start + win, axis=1)
    single = jnp.all(segments == segments[:, :1], axis=1)
    kind = jnp.where(single, 0, jnp.where(fits, 1, 2))
    return kind.astype(jnp.int32), start.astype(jnp.int32)

def fwd_kernel(heads, kind_ref, start_ref, place_ref, qkv_ref, row_ref, col_ref, ctx_ref, lse_ref, *part_refs):
    b = pl.program_id(0)
    t = qkv_ref.shape[1]
    hw = heads * HEAD_DIM
    win = min(3 * SPAN, t)
    kind = kind_ref[b]

    def piece(h, which, rows):
        lo = which * hw + h * HEAD_DIM
        return qkv_ref[0, rows, lo:lo + HEAD_DIM]

    def attend(h, rows, count, keys, masked):
        q = piece(h, 0, rows)
        s = dot(q, piece(h, 1, keys), 1, 1)
        if masked:
            s = jnp.where(col_ref[0, rows, :] == row_ref[0, :, keys], s, MASKED)
        m = jnp.max(s, axis=1, keepdims=True)
        e = jnp.exp(s - m)
        total = jnp.sum(e, axis=1, keepdims=True)
        c = dot(e.astype(jnp.bfloat16), piece(h, 2, keys), 1, 0) / total
        ctx_ref[0, rows, h * HEAD_DIM:(h + 1) * HEAD_DIM] = c.astype(jnp.bfloat16)
        lse = jnp.broadcast_to(m + jnp.log(total), (count, 128))
        lse_ref[0, h:h + 1, rows] = jnp.transpose(lse)[0:1, :]

    def dense(masked):
        tile = min(256, t)
        def body(i, _):
            rows = pl.ds(pl.multiple_of(i * tile, tile), tile)
            for h in range(heads):
                attend(h, rows, tile, pl.ds(0, t), masked)
            return 0
        lax.fori_loop(0, t // tile, body, 0)

    @pl.when(kind == 0)
    def _():
        dense(False)

    @pl.when(kind == 2)
    def _():
        dense(True)

    @pl.when(kind == 1)
    def _():
        def body(i, _):
            rows = pl.ds(pl.multiple_of(i * SPAN, SPAN), SPAN)
            keys = pl.ds(pl.multiple_of(start_ref[b, i], SPAN), win)
            for h in range(heads):
                attend(h, rows, SPAN, keys, True)
            return 0
        lax.fori_loop(0, t // SPAN, body, 0)

    length = part_refs[0].shape[1]
    for q, part_ref in enumerate(part_refs):
        part_ref[0] = ctx_ref[0, pl.ds(pl.multiple_of(place_ref[q] * length, length), length), :]


def attention(qkv, segments, kind, start, places, waits):
    ranks = places.shape[0]
    b, t, w = qkv.shape
    hw = w // 3
    heads = hw // HEAD_DIM

    def at(i, *_):
        return (i, 0, 0)

    return run(
        functools.partial(fwd_kernel, heads),
        "attention_forward",
        (b,),
        [pl.BlockSpec((1, t, w), at), pl.BlockSpec((1, 1, t), at), pl.BlockSpec((1, t, 1), at)],
        [pl.BlockSpec((1, t, hw), at), pl.BlockSpec((1, heads, t), at)]
        + [pl.BlockSpec((1, t // ranks, hw), at)] * ranks,
        [kind_of((b, t, hw)), kind_of((b, heads, t), jnp.float32)] + [kind_of((b, t // ranks, hw))] * ranks,
        [qkv, segments[:, None, :], segments[:, :, None]],
        prefetch=(kind, start, places),
        waits=waits,
        cost=100,
    )

def bwd_kernel(heads, b, kind_ref, start_ref, qkv_ref, do_ref, ctx_ref, lse_ref, row_ref, col_ref, out_ref, dq_acc, delta_ref):
    t = qkv_ref.shape[1]
    hw = heads * HEAD_DIM
    win = min(3 * SPAN, t)
    kind = kind_ref[b]

    def lanes(h, which=0):
        lo = which * hw + h * HEAD_DIM
        return slice(lo, lo + HEAD_DIM)

    for h in range(heads):
        prod = do_ref[0, :, lanes(h)].astype(jnp.float32) * ctx_ref[0, :, lanes(h)].astype(jnp.float32)
        d = jnp.sum(prod, axis=1, keepdims=True)
        delta_ref[h:h + 1, :] = jnp.transpose(jnp.broadcast_to(d, (t, 128)))[0:1, :]

    def back(h, keys, queries, masked):
        k = qkv_ref[0, keys, lanes(h, 1)]
        v = qkv_ref[0, keys, lanes(h, 2)]
        q = qkv_ref[0, queries, lanes(h, 0)]
        do = do_ref[0, queries, lanes(h)]
        s = dot(k, q, 1, 1)
        if masked:
            s = jnp.where(col_ref[0, keys, :] == row_ref[0, :, queries], s, MASKED)
        p = jnp.exp(s - lse_ref[0, h:h + 1, queries])
        dp = dot(v, do, 1, 1)
        ds = (p * (dp - delta_ref[h:h + 1, queries])).astype(jnp.bfloat16)
        dv = dot(p.astype(jnp.bfloat16), do, 1, 0)
        dk = dot(ds, q, 1, 0)
        out_ref[0, keys, lanes(h, 1)] = dk.astype(jnp.bfloat16)
        out_ref[0, keys, lanes(h, 2)] = dv.astype(jnp.bfloat16)
        return dot(k, ds, 0, 0)

    dq_acc[...] = jnp.zeros_like(dq_acc)

    def dense(masked):
        tile = min(256, t)
        def body(j, _):
            keys = pl.ds(pl.multiple_of(j * tile, tile), tile)
            for h in range(heads):
                dq_acc[h] += back(h, keys, pl.ds(0, t), masked)
            return 0
        lax.fori_loop(0, t // tile, body, 0)

    @pl.when(kind == 0)
    def _():
        dense(False)

    @pl.when(kind == 2)
    def _():
        dense(True)

    @pl.when(kind == 1)
    def _():
        def body(j, _):
            keys = pl.ds(pl.multiple_of(j * SPAN, SPAN), SPAN)
            queries = pl.ds(pl.multiple_of(start_ref[b, j], SPAN), win)
            for h in range(heads):
                dq_acc[h, :, queries] += back(h, keys, queries, True)
            return 0
        lax.fori_loop(0, t // SPAN, body, 0)

    for h in range(heads):
        dq = jnp.transpose(dq_acc[h]) * (HEAD_DIM ** -0.5)
        out_ref[0, :, lanes(h, 0)] = dq.astype(jnp.bfloat16)

def attention_back(qkv, dparts, ctx, lse, segments, kind, start, places, which, buffer, waits):
    b, t, w = qkv.shape
    hw = w // 3
    heads = hw // HEAD_DIM
    ranks = len(dparts)
    length = t // ranks

    def kernel(kind_ref, start_ref, place_ref, qkv_ref, *refs):
        grad_ref = refs[-1]
        for q in range(ranks):
            grad_ref[0, pl.ds(pl.multiple_of(place_ref[q] * length, length), length), :] = refs[q][0]
        bwd_kernel(heads, which, kind_ref, start_ref, qkv_ref, grad_ref, *refs[ranks : ranks + 4], *refs[-4:-1])

    def at(i, *_):
        return (which, 0, 0)

    ins = [pl.BlockSpec((1, t, w), at)] + [pl.BlockSpec((1, length, hw), at)] * ranks
    ins += [
        pl.BlockSpec((1, t, hw), at),
        pl.BlockSpec((1, heads, t), at),
        pl.BlockSpec((1, 1, t), at),
        pl.BlockSpec((1, t, 1), at),
    ]
    operands = [qkv, *dparts, ctx, lse, segments[:, None, :], segments[:, :, None]]
    alias = None
    if buffer is not None:
        ins.append(pl.BlockSpec(memory_space=pl.ANY))
        operands.append(buffer)
        alias = {3 + len(ins) - 1: 0}
    return run(
        kernel,
        "attention_backward",
        (1,),
        ins,
        pl.BlockSpec((1, t, w), at),
        kind_of((b, t, w)),
        operands,
        prefetch=(kind, start, places),
        scratch=(
            pltpu.VMEM((heads, HEAD_DIM, t), jnp.float32),
            pltpu.VMEM((heads, t), jnp.float32),
            pltpu.VMEM((1, t, hw), jnp.bfloat16),
        ),
        alias=alias,
        waits=waits,
    )


AXES = ("seq", "z", "core")
ROWS = ("z", "core")
EXTRA = 16


def low(tensor):
    return tensor.astype(jnp.bfloat16)


class Ring:
    def __init__(self):
        self.ranks = lax.axis_size("seq")
        self.chips = lax.axis_size("z")
        self.index = lax.axis_index("seq")
        self.core = lax.axis_index("core")
        self.count = self.ranks.bit_length() - 1

    def bit(self, k, core):
        if self.count == 2 and core == 1:
            k = 1 - k
        return 1 << k

    def offset(self, q, core):
        return sum(self.bit(k, core) for k in range(self.count) if q >> k & 1)

    def place(self, q):
        return jnp.bitwise_xor(self.index, jnp.where(self.core == 0, self.offset(q, 0), self.offset(q, 1)))

    def hop(self, block, k):
        pairs = []
        for s in range(self.ranks):
            for z in range(self.chips):
                for c in range(2):
                    to = s ^ self.bit(k, c)
                    pairs.append(((s * self.chips + z) * 2 + c, (to * self.chips + z) * 2 + c))
        return lax.ppermute(block, AXES, pairs)

    def gather(self, block):
        blocks = [block]
        for k in range(self.count):
            blocks = blocks + [self.hop(b, k) for b in blocks]
        return [View(b) for b in blocks]

    def total(self, block):
        for k in range(self.count):
            block = wide(block) + wide(self.hop(low(block), k))
        return block


    def exchange(self, blocks):
        out = [blocks[0]]
        for q in range(1, self.ranks):
            pairs = []
            for s in range(self.ranks):
                for z in range(self.chips):
                    for c in range(2):
                        to = s ^ self.offset(q, c)
                        pairs.append(((s * self.chips + z) * 2 + c, (to * self.chips + z) * 2 + c))
            out.append(lax.ppermute(blocks[q], AXES, pairs))
        return out

    def shift(self, block, d):
        return lax.ppermute(block, "z", [(z, (z + d) % self.chips) for z in range(self.chips)])


def swap(block):
    return lax.ppermute(block, "core", [(0, 1), (1, 0)])


def put(blocks, ring, axis):
    shape = list(blocks[0].shape)
    size = shape[axis]
    shape[axis] = size * len(blocks)
    whole = jnp.zeros(shape, blocks[0].dtype)
    for q, block in enumerate(blocks):
        whole = lax.dynamic_update_slice_in_dim(whole, block, ring.place(q) * size, axis)
    return whole


def local(
    hidden_in,
    segments,
    q_weight,
    k_weight,
    v_weight,
    out_weight,
    q_bias,
    v_bias,
    out_bias,
    up_weight,
    up_bias,
    down_weight,
    down_bias,
    norm1_gain,
    norm1_bias,
    norm2_gain,
    norm2_bias,
    out_grad,
):
    ring = Ring()
    here, core = ring.index, ring.core
    ranks, chips = ring.ranks, ring.chips
    owners = chips * 2
    z_index = lax.axis_index("z")
    owner = z_index * 2 + core
    seqs, length, width = hidden_in.shape
    full = length * ranks
    head_width = width // ranks
    out_width = 3 * head_width
    rows = width // owners
    units = down_weight.shape[0]
    part = units // ranks
    count = seqs * length
    score_scale = HEAD_DIM ** (-0.5)
    first_core = core == 0
    core_index = core.astype(jnp.int32).reshape(1)
    places = jnp.stack([ring.place(q) for q in range(ranks)]).astype(jnp.int32)
    blocks = range(ranks)

    heads_at = here * head_width
    mine = jnp.concatenate(
        [lax.dynamic_slice_in_dim(w, heads_at, head_width, 1) for w in (q_weight, k_weight, v_weight)], axis=1
    )
    vectors = (q_bias, v_bias, out_bias, down_bias, norm1_gain, norm1_bias, norm2_gain, norm2_bias)
    known = len(vectors)
    packed = jnp.pad(
        up_bias.reshape(-1, rows), ((known, EXTRA - known - units // rows), (0, out_width - rows))
    )
    for i, vector in enumerate(vectors):
        packed = packed + jnp.pad(vector[None], ((i, EXTRA - 1 - i), (0, out_width - rows)))
    mine = jnp.concatenate([mine, packed], axis=0)
    gathered = lax.all_gather(mine, ROWS, axis=0)

    def up_columns(of_core):
        return jnp.concatenate(
            [
                lax.dynamic_slice_in_dim(up_weight, ((z * 2 + of_core) * ranks + here) * part, part, 1)
                for z in range(chips)
            ],
            axis=1,
        )

    own_up, other_up = up_columns(core), swap(up_columns(1 - core))
    up_rows = jnp.concatenate(
        [jnp.where(first_core, own_up, other_up), jnp.where(first_core, other_up, own_up)], axis=0
    )
    hidden = ring.gather(hidden_in)
    shifts = jnp.stack([(z_index - d) % chips for d in range(chips)]).astype(jnp.int32)
    up_block = lay_chips(shifts, [up_rows] + [ring.shift(up_rows, d) for d in range(1, chips)], ())
    up_block = hold(up_block.reshape(width, chips * part), (hidden[-1].array,))
    down_rows = hold(lax.dynamic_slice_in_dim(down_weight, here * part, part, 0), (gathered,))
    down_block = lax.all_gather(down_rows, "z", axis=0, tiled=True)
    output_weight = lax.all_gather(hold(out_weight, (down_rows,)), ROWS, axis=0, tiled=True)
    up_weights = ring.gather(up_block)
    kind, start = plan_rows(segments)
    keep = wide(lax.dynamic_slice_in_dim(segments, here * length, length, 1) != 0)[:, :, None]

    qkv_weight = gathered[:, :rows].reshape(width, out_width)
    gathered = wide(gathered[:, rows:, :rows])
    vectors = gathered.transpose(1, 0, 2).reshape(EXTRA, width)
    biases = lax.dynamic_slice_in_dim(vectors, heads_at, head_width, 1)
    qkv_bias = jnp.concatenate([biases[0], jnp.zeros_like(biases[0]), biases[1]])[None]
    scales = jnp.where(jnp.arange(out_width) < head_width, score_scale, 1.0)[None]
    qkv = project(places, hidden, qkv_weight, qkv_bias, scales)
    contexts, log_totals, *context_parts = attention(
        qkv, segments, kind, start, places, (*arrays(up_weights[1:3]), down_block)
    )
    context_parts = ring.exchange(context_parts)
    down_weights = ring.gather(down_block)
    sums_one, first_low = out_norm(
        places,
        context_parts,
        output_weight,
        hidden_in,
        vectors,
        arrays(down_weights[1:2]),
    )

    first_low = first_low.reshape(count, width)
    first_other = swap(first_low)
    upper_bias = gathered[:, known : known + units // rows].reshape(chips, 2, ranks, part)
    upper_bias = lax.dynamic_index_in_dim(upper_bias, core, 1, False)
    upper_bias = [
        lax.dynamic_index_in_dim(upper_bias, ring.place(q), 1, False).reshape(1, -1) for q in blocks
    ]
    actives, slopes = up_forward(first_low, first_other, up_weights, upper_bias)
    mixed_other = down_forward(actives, down_weights, count, count, jnp.bfloat16)
    mixed = down_forward(actives, down_weights, 0, count, jnp.float32, (mixed_other,))
    layer_out, dsum_two, dmixed, totals_two = norm_two(mixed, swap(mixed_other), sums_one, vectors, out_grad, keep)

    dmixed = dmixed.reshape(count, width)
    dmixed_other = swap(dmixed)
    none = [()] * ranks
    odd, even = [q for q in blocks if q % 2], [q for q in blocks if q % 2 == 0]
    down_sent = down_grad([actives[q] for q in odd], dmixed, dmixed_other, none)
    duppers, up_sums, dfirst, dfirst_other = ffn_back(
        dmixed, dmixed_other, slopes, down_weights, up_weights, (tick(down_sent),)
    )
    dfirst_other = swap(dfirst_other)
    dsum_one, dbranch, dcontexts, totals_one = norm_one_back(
        places, dfirst, dfirst_other, dsum_two, sums_one, vectors, output_weight, head_width, (tick(duppers[0], cost=10),)
    )
    dcontexts = ring.exchange(dcontexts)

    def spread(made, sent):
        came = {q: [] for q in blocks}
        for k in range(ring.count):
            step = 1 << k
            got = ring.hop(sent, k)
            for i, q in enumerate(range(0, ranks, 2 * step)):
                came[q].append(View(got, i))
            if k + 1 < ring.count:
                turn = [q + 2 * step for q in range(0, ranks, 4 * step)]
                sent = made(turn, [came[q] for q in turn])
        return came[0], sent

    def down_made(turn, addends):
        return down_grad([actives[q] for q in turn], dmixed, dmixed_other, addends, (tick(dbranch),))

    down_came, down_hop = spread(down_made, down_sent)
    up_sent = up_grad([duppers[q] for q in odd], first_low, first_other, none, (down_hop,))

    extra = -(-(6 + ranks) // EXTRA) * EXTRA
    up_totals = put([up_sums[q : q + 1] for q in blocks], ring, 0).reshape(ranks, chips, 1, part)
    up_totals = jnp.where(jnp.arange(2)[None, None, :, None] == core, up_totals, 0.0)
    up_totals = jnp.pad(up_totals, ((0, 0), (0, 0), (0, 0), (0, rows - part))).reshape(ranks, width)
    small = jnp.concatenate(
        [totals_two[:3], totals_one[:3], up_totals, jnp.zeros((extra - 6 - ranks, width), jnp.float32)], axis=0
    )
    out_pack = out_grad_pack(places, context_parts, dbranch, low(small), owners, (up_sent,))
    out_shard = lax.psum_scatter(out_pack.reshape(-1, width), ROWS, scatter_dimension=0, tiled=True)

    common = (qkv, dcontexts, contexts, log_totals, segments, kind, start, places)
    dqkv = attention_back(*common, 0, None, (out_pack,))

    def up_made(turn, addends):
        return up_grad([duppers[q] for q in turn], first_low, first_other, addends, (dqkv,))

    up_came, up_hop = spread(up_made, up_sent)
    down_own = down_grad([actives[0]], dmixed, dmixed_other, [down_came], (up_hop,))[0]
    ahead = jnp.stack([(z_index + d) % chips for d in range(chips)]).astype(jnp.int32)
    down_pieces = split(ahead, down_own, part)
    for which in range(1, seqs):
        dqkv = attention_back(*common, which, dqkv, (down_pieces[0], up_hop))

    def shifted(pieces):
        return [pieces[0]] + [ring.shift(pieces[d], d) for d in range(1, chips)]

    down_shard = total_rows(shifted(down_pieces), (dqkv, out_shard))
    down_parts = ring.gather(down_shard)

    def hidden_made(turn, addends, waits=()):
        return hidden_grad(places, dqkv, qkv_weight, length, turn, addends, jnp.bfloat16, waits or (qkv_pack,))

    up_own = up_grad([duppers[0]], first_low, first_other, [up_came], (dqkv,))[0]
    up_pieces = split(ahead, up_own, 2 * rows)
    hidden_sent = hidden_made(odd, none, (up_pieces[0], down_shard))
    qkv_pack = project_grad_pack(places, hidden, dqkv, owners, EXTRA, (hidden_sent, *arrays(down_parts)))
    qkv_shard = lax.psum_scatter(qkv_pack.reshape(-1, out_width), ROWS, scatter_dimension=0, tiled=True)

    hidden_came, hidden_hop = spread(hidden_made, hidden_sent)
    keep_part, take_part = total_halves(core_index, shifted(up_pieces), (qkv_pack,))
    down_weight_grad = lay_rows(places, down_parts, (keep_part,))
    up_pair = pair(core_index, keep_part, swap(take_part), (down_weight_grad,))
    input_grad = hidden_grad(
        places, dqkv, qkv_weight, length, [0], [[View(dsum_one)] + hidden_came], jnp.float32
    )[0]

    up_parts = ring.gather(up_pair)
    qkv_parts = ring.gather(qkv_shard)
    out_pack = ring.total(out_shard)
    if part % 128 == 0:
        up_weight_grad = lay_up(places, up_parts, chips, part)
    else:
        up_weight_grad = wide(put([b.value()[None] for b in up_parts], ring, 0))
        up_weight_grad = (
            up_weight_grad.reshape(ranks, 2, rows, chips, part).transpose(2, 3, 1, 0, 4).reshape(rows, owners * units)
        )
    if head_width % 128 == 0:
        *qkv_grads, q_sums, _, v_sums = lay_columns(places, qkv_parts, rows)
    else:
        laid = wide(put([b.value()[None] for b in qkv_parts], ring, 0))
        laid = laid.reshape(ranks, rows + EXTRA, 3, head_width).transpose(2, 1, 0, 3).reshape(3, -1, width)
        qkv_grads, q_sums, v_sums = [g[:rows] for g in laid], laid[0, rows:], laid[2, rows:]

    def mine_of(sums):
        return lax.dynamic_slice_in_dim(sums[0], owner * rows, rows, 0)

    small = out_pack[rows:, :rows]
    up_bias_grad = small[6 : 6 + ranks, :part].reshape(-1)
    return (
        layer_out,
        input_grad,
        *qkv_grads,
        out_pack[:rows],
        mine_of(q_sums),
        mine_of(v_sums),
        small[3],
        up_weight_grad,
        up_bias_grad,
        down_weight_grad,
        small[0],
        small[4],
        small[5],
        small[1],
        small[2],
    )


def solution(mesh):
    ranks, owners = mesh.shape["seq"], mesh.shape["fsdp"]
    grid = Mesh(mesh.devices.reshape(ranks, owners // 2, 2), AXES)
    tokens, matrix, vector = P(ROWS, "seq", None), P(ROWS, None), P(ROWS)
    return jax.shard_map(
        local,
        mesh=grid,
        in_specs=(
            tokens,
            matrix,
            matrix,
            matrix,
            matrix,
            matrix,
            vector,
            vector,
            vector,
            matrix,
            vector,
            matrix,
            vector,
            vector,
            vector,
            vector,
            vector,
            tokens,
        ),
        out_specs=(
            tokens,
            tokens,
            matrix,
            matrix,
            matrix,
            matrix,
            vector,
            vector,
            vector,
            matrix,
            vector,
            matrix,
            vector,
            vector,
            vector,
            vector,
            vector,
        ),
        check_vma=False,
    )
```

```python
import functools

import jax
import jax.numpy as jnp
from jax import lax
from jax.experimental import pallas as pl
from jax.experimental.pallas import tpu as pltpu
from jax.sharding import Mesh
from jax.sharding import PartitionSpec as P

HEAD_DIM = 64
SPAN = 256
ALIGN = 128
WINDOW = 512
FORWARD_SPAN = 1024
BACKWARD_SPAN = 512
UNROLL = True
MASKED = -1e30


def dot(a,b,ca,cb):
    return lax.dot_general(a,b,(((ca,),(cb,)),((),())),preferred_element_type=jnp.float32)


TILE = 256


def run(kernel, name, grid, ins, outs, shapes, operands, prefetch=(), scratch=(), alias=None, waits=(), cost=10):
    known = len(prefetch) + len(ins)

    def waiting(*refs):
        kernel(*refs[:known], *refs[known + len(waits) :])

    ins = list(ins) + [pl.BlockSpec(memory_space=pl.ANY)] * len(waits)
    operands = list(operands) + list(waits)
    return pl.pallas_call(
        waiting,
        grid_spec=pltpu.PrefetchScalarGridSpec(
            num_scalar_prefetch=len(prefetch), grid=grid, in_specs=ins, out_specs=outs, scratch_shapes=scratch
        ),
        out_shape=shapes,
        input_output_aliases=alias or {},
        compiler_params=pltpu.CompilerParams(vmem_limit_bytes=50 << 20),
        cost_estimate=pl.CostEstimate(flops=cost * 3000000000, bytes_accessed=1000, transcendentals=0),
        name=name,
    )(*prefetch, *operands)


def fixed(array):
    rank = array.ndim
    return pl.BlockSpec(array.shape, lambda *_: (0,) * rank, pipeline_mode=pl.Buffered(buffer_count=1))


class View:
    def __init__(self, array, i=None):
        self.array, self.i = array, i
        self.shape = array.shape if i is None else array.shape[1:]

    def spec(self, block, place):
        i = self.i
        if i is None:
            return pl.BlockSpec(block, place)
        return pl.BlockSpec((None,) + tuple(block), lambda *a: (i,) + tuple(place(*a)))

    def whole(self):
        rank, i = len(self.shape), self.i
        once = pl.Buffered(buffer_count=1)
        if i is None:
            return pl.BlockSpec(self.shape, lambda *_: (0,) * rank, pipeline_mode=once)
        return pl.BlockSpec((None,) + tuple(self.shape), lambda *_: (i,) + (0,) * rank, pipeline_mode=once)

    def value(self):
        return self.array if self.i is None else self.array[self.i]


def arrays(views):
    return [v.array for v in views]


def kind_of(shape, dtype=jnp.bfloat16):
    return jax.ShapeDtypeStruct(tuple(shape), dtype)


def wide(tensor):
    return tensor.astype(jnp.float32)


def standardize(values):
    center = jnp.mean(values, axis=1, keepdims=True)
    offset = values - center
    inverse = lax.rsqrt(jnp.mean(offset * offset, axis=1, keepdims=True) + 1e-05)
    return offset * inverse, inverse


def standardize_back(upstream, normed, inverse, gain):
    scaled = upstream * gain
    return inverse * (
        scaled
        - jnp.mean(scaled, axis=1, keepdims=True)
        - normed * jnp.mean(scaled * normed, axis=1, keepdims=True)
    )


def column_sum(values):
    return jnp.sum(values, axis=0, keepdims=True)


OUT_BIAS, DOWN_BIAS, GAIN_ONE, SHIFT_ONE, GAIN_TWO, SHIFT_TWO = 2, 3, 4, 5, 6, 7


def project(places, blocks, weight, bias, scale):
    seqs, length, width = blocks[0].shape
    ranks = len(blocks)
    out_width = weight.shape[1]

    def kernel(place_ref, weight_ref, bias_ref, scale_ref, *refs):
        for q in range(ranks):

            @pl.when(pl.program_id(0) // seqs == q)
            def _(q=q):
                product = dot(refs[q][0], weight_ref[...], 1, 0) + bias_ref[...]
                refs[ranks][0] = (product * scale_ref[...]).astype(jnp.bfloat16)

    def source(q):
        return lambda i, p: (jnp.clip(i - q * seqs, 0, seqs - 1), 0, 0)

    return run(
        kernel,
        "project",
        (ranks * seqs,),
        [fixed(weight), fixed(bias), fixed(scale)]
        + [blocks[q].spec((1, length, width), source(q)) for q in range(ranks)],
        pl.BlockSpec((1, length, out_width), lambda i, p: (i % seqs, p[i // seqs], 0)),
        kind_of((seqs, length * ranks, out_width)),
        [weight, bias, scale, *arrays(blocks)],
        prefetch=(places,),
    )


def out_norm(places, contexts, weight, hidden, vectors, waits=()):
    seqs, length, width = hidden.shape
    ranks = len(contexts)
    part = contexts[0].shape[2]

    def kernel(place_ref, *refs):
        weight_ref, hidden_ref, vector_ref, sum_ref, first_ref = refs[ranks:]
        total = wide(hidden_ref[0]) + vector_ref[OUT_BIAS : OUT_BIAS + 1, :]
        for q in range(ranks):
            rows = pl.ds(pl.multiple_of(place_ref[q] * part, part), part)
            total = total + dot(refs[q][0], weight_ref[rows, :], 1, 0)
        sum_ref[0] = total
        normed, _ = standardize(total)
        first = normed * vector_ref[GAIN_ONE : GAIN_ONE + 1, :] + vector_ref[SHIFT_ONE : SHIFT_ONE + 1, :]
        first_ref[0] = first.astype(jnp.bfloat16)

    tokens = pl.BlockSpec((1, length, width), lambda b, p: (b, 0, 0))
    return run(
        kernel,
        "out_norm",
        (seqs,),
        [pl.BlockSpec((1, length, part), lambda b, p: (b, 0, 0))] * ranks + [fixed(weight), tokens, fixed(vectors)],
        [tokens, tokens],
        [kind_of(hidden.shape, jnp.float32), kind_of(hidden.shape)],
        [*contexts, weight, hidden, vectors],
        prefetch=(places,),
        waits=waits,
    )


def up_forward(own, other, weights, biases, waits=()):
    count, width = own.shape
    units = weights[0].shape[1]
    blocks = len(weights)
    tile = min(TILE, count)
    half = count // tile

    def kernel(own_ref, other_ref, *refs):
        def body(tokens):
            for q in range(blocks):
                upper = dot(tokens, refs[q][...], 1, 0) + refs[blocks + q][...]
                tail = 0.5 * (1.0 + lax.erf(upper * 0.7071067811865476))
                refs[2 * blocks + q][...] = (upper * tail).astype(jnp.bfloat16)
                bell = jnp.exp(-0.5 * upper * upper) * 0.3989422804014327
                refs[3 * blocks + q][...] = (tail + upper * bell).astype(jnp.bfloat16)

        @pl.when(pl.program_id(0) < half)
        def _():
            body(own_ref[...])

        @pl.when(pl.program_id(0) >= half)
        def _():
            body(other_ref[...])

    outs = run(
        kernel,
        "up_forward",
        (2 * half,),
        [
            pl.BlockSpec((tile, width), lambda i: (jnp.minimum(i, half - 1), 0)),
            pl.BlockSpec((tile, width), lambda i: (jnp.maximum(i - half, 0), 0)),
        ]
        + [w.whole() for w in weights]
        + [fixed(b) for b in biases],
        [pl.BlockSpec((tile, units), lambda i: (i, 0))] * (2 * blocks),
        [kind_of((2 * count, units))] * (2 * blocks),
        [own, other, *arrays(weights), *biases],
        waits=waits,
    )
    return list(outs[:blocks]), list(outs[blocks:])


def down_forward(actives, weights, first, count, dtype, waits=()):
    blocks = len(actives)
    units, width = weights[0].shape
    tile = min(TILE, count)

    def kernel(*refs):
        total = dot(refs[0][...], refs[blocks][...], 1, 0)
        for q in range(1, blocks):
            total = total + dot(refs[q][...], refs[blocks + q][...], 1, 0)
        refs[-1][...] = total.astype(dtype)

    return run(
        kernel,
        "down_forward",
        (count // tile,),
        [pl.BlockSpec((tile, units), lambda i: (i + first // tile, 0))] * blocks + [w.whole() for w in weights],
        pl.BlockSpec((tile, width), lambda i: (i, 0)),
        kind_of((count, width), dtype),
        [*actives, *arrays(weights)],
        waits=waits,
    )


def norm_two(mixed, mixed_other, sums_one, vectors, out_grad, keep):
    seqs, length, width = sums_one.shape

    def kernel(mixed_ref, other_ref, sum_ref, vector_ref, grad_ref, keep_ref, out_ref, dsum_ref, dmixed_ref, total_ref):
        @pl.when(pl.program_id(0) == 0)
        def _():
            total_ref[...] = jnp.zeros_like(total_ref)

        def vector(i):
            return vector_ref[i : i + 1, :]

        normed, _ = standardize(sum_ref[0])
        first = normed * vector(GAIN_ONE) + vector(SHIFT_ONE)
        mixed = mixed_ref[0] + wide(other_ref[0]) + vector(DOWN_BIAS)
        normed, inverse = standardize(first + mixed)
        out_ref[0] = (normed * vector(GAIN_TWO) + vector(SHIFT_TWO)).astype(jnp.bfloat16)
        cot = wide(grad_ref[0]) * keep_ref[0]
        dsum = standardize_back(cot, normed, inverse, vector(GAIN_TWO))
        dsum_ref[0] = dsum
        dmixed = dsum.astype(jnp.bfloat16)
        dmixed_ref[0] = dmixed
        total_ref[0:1, :] += column_sum(wide(dmixed))
        total_ref[1:2, :] += column_sum(cot * normed)
        total_ref[2:3, :] += column_sum(cot)

    tokens = pl.BlockSpec((1, length, width), lambda b: (b, 0, 0))
    shape = sums_one.shape
    return run(
        kernel,
        "norm_two",
        (seqs,),
        [tokens, tokens, tokens, fixed(vectors), tokens, pl.BlockSpec((1, length, 1), lambda b: (b, 0, 0))],
        [tokens, tokens, tokens, pl.BlockSpec((8, width), lambda b: (0, 0))],
        [kind_of(shape), kind_of(shape, jnp.float32), kind_of(shape), kind_of((8, width), jnp.float32)],
        [mixed.reshape(shape), mixed_other.reshape(shape), sums_one, vectors, out_grad, keep],
    )


def ffn_back(own, other, slopes, downs, ups, waits=()):
    blocks = len(slopes)
    count, width = own.shape
    units = slopes[0].shape[1]
    tile = min(TILE, count)
    half = count // tile

    def kernel(own_ref, other_ref, *refs):
        slope_refs, down_refs, up_refs = refs[:blocks], refs[blocks : 2 * blocks], refs[2 * blocks : 3 * blocks]
        upper_refs, total_ref, here_ref, there_ref = refs[3 * blocks : 4 * blocks], refs[-3], refs[-2], refs[-1]
        step = pl.program_id(0)

        @pl.when(step == 0)
        def _():
            total_ref[...] = jnp.zeros_like(total_ref)

        def body(grad):
            total = 0.0
            for q in range(blocks):
                upper = (dot(grad, down_refs[q][...], 1, 1) * wide(slope_refs[q][...])).astype(jnp.bfloat16)
                upper_refs[q][...] = upper
                total_ref[q : q + 1, :] += column_sum(wide(upper))
                total = total + dot(upper, up_refs[q][...], 1, 1)
            return total

        @pl.when(step < half)
        def _():
            there_ref[...] = body(other_ref[...]).astype(jnp.bfloat16)

        @pl.when(step >= half)
        def _():
            here_ref[...] = body(own_ref[...])

    def early(i):
        return (jnp.minimum(i, half - 1), 0)

    def late(i):
        return (jnp.maximum(i - half, 0), 0)

    def both(i):
        return ((i + half) % (2 * half), 0)

    outs = run(
        kernel,
        "feed_forward_back",
        (2 * half,),
        [pl.BlockSpec((tile, width), late), pl.BlockSpec((tile, width), early)]
        + [pl.BlockSpec((tile, units), both)] * blocks
        + [w.whole() for w in (*downs, *ups)],
        [pl.BlockSpec((tile, units), both)] * blocks
        + [
            pl.BlockSpec((max(8, blocks), units), lambda i: (0, 0)),
            pl.BlockSpec((tile, width), late),
            pl.BlockSpec((tile, width), early),
        ],
        [kind_of((2 * count, units))] * blocks
        + [
            kind_of((max(8, blocks), units), jnp.float32),
            kind_of((count, width), jnp.float32),
            kind_of((count, width)),
        ],
        [own, other, *slopes, *arrays(downs), *arrays(ups)],
        waits=waits,
    )
    return list(outs[:blocks]), outs[blocks], outs[blocks + 1], outs[blocks + 2]


def down_grad(actives, own, other, addends, waits=()):
    count, width = own.shape
    units = actives[0].shape[1]
    tile = min(TILE, units)
    blocks = len(actives)
    spread = [(q, a) for q in range(blocks) for a in addends[q]]

    def kernel(own_ref, other_ref, *refs):
        for q in range(blocks):
            total = dot(refs[q][:count, :], own_ref[...], 0, 0) + dot(refs[q][count:, :], other_ref[...], 0, 0)
            for j, (of, _) in enumerate(spread):
                if of == q:
                    total = total + wide(refs[blocks + j][...])
            refs[-1][q] = total.astype(jnp.bfloat16)

    return run(
        kernel,
        "down_grad",
        (units // tile,),
        [fixed(own), fixed(other)]
        + [pl.BlockSpec((2 * count, tile), lambda i: (0, i))] * blocks
        + [a.spec((tile, width), lambda i: (i, 0)) for _, a in spread],
        pl.BlockSpec((blocks, tile, width), lambda i: (0, i, 0)),
        kind_of((blocks, units, width)),
        [own, other, *actives, *(a.array for _, a in spread)],
        waits=waits,
    )


def up_grad(uppers, own, other, addends, waits=()):
    count, width = own.shape
    units = uppers[0].shape[1]
    tile = min(TILE, width)
    blocks = len(uppers)
    spread = [(q, a) for q in range(blocks) for a in addends[q]]

    def kernel(own_ref, other_ref, *refs):
        for q in range(blocks):
            total = dot(own_ref[...], refs[q][:count, :], 0, 0) + dot(other_ref[...], refs[q][count:, :], 0, 0)
            for j, (of, _) in enumerate(spread):
                if of == q:
                    total = total + wide(refs[blocks + j][...])
            refs[-1][q] = total.astype(jnp.bfloat16)

    columns = pl.BlockSpec((count, tile), lambda i: (0, i))
    return run(
        kernel,
        "up_grad",
        (width // tile,),
        [columns, columns]
        + [fixed(u) for u in uppers]
        + [a.spec((tile, units), lambda i: (i, 0)) for _, a in spread],
        pl.BlockSpec((blocks, tile, units), lambda i: (0, i, 0)),
        kind_of((blocks, width, units)),
        [own, other, *uppers, *(a.array for _, a in spread)],
        waits=waits,
    )


def norm_one_back(places, dfirst, dfirst_other, dsum_two, sums_one, vectors, weight, part, waits=()):
    seqs, length, width = sums_one.shape
    ranks = width // part

    def kernel(place_ref, own_ref, other_ref, dsum_ref, sum_ref, vector_ref, weight_ref, *outs):
        @pl.when(pl.program_id(0) == 0)
        def _():
            outs[-1][...] = jnp.zeros_like(outs[-1])

        upstream = dsum_ref[0] + own_ref[0] + wide(other_ref[0])
        normed, inverse = standardize(sum_ref[0])
        dsum = standardize_back(upstream, normed, inverse, vector_ref[GAIN_ONE : GAIN_ONE + 1, :])
        outs[0][0] = dsum
        dbranch = dsum.astype(jnp.bfloat16)
        outs[1][0] = dbranch
        for q in range(ranks):
            rows = pl.ds(pl.multiple_of(place_ref[q] * part, part), part)
            outs[2 + q][0] = dot(dbranch, weight_ref[rows, :], 1, 1).astype(jnp.bfloat16)
        outs[-1][0:1, :] += column_sum(wide(dbranch))
        outs[-1][1:2, :] += column_sum(upstream * normed)
        outs[-1][2:3, :] += column_sum(upstream)

    tokens = pl.BlockSpec((1, length, width), lambda b, p: (b, 0, 0))
    shape = sums_one.shape
    outs = run(
        kernel,
        "norm_one_back",
        (seqs,),
        [tokens, tokens, tokens, tokens, fixed(vectors), fixed(weight)],
        [tokens, tokens]
        + [pl.BlockSpec((1, length, part), lambda b, p: (b, 0, 0))] * ranks
        + [pl.BlockSpec((8, width), lambda b, p: (0, 0))],
        [kind_of(shape, jnp.float32), kind_of(shape)]
        + [kind_of((seqs, length, part))] * ranks
        + [kind_of((8, width), jnp.float32)],
        [dfirst.reshape(shape), dfirst_other.reshape(shape), dsum_two, sums_one, vectors, weight],
        prefetch=(places,),
        waits=waits,
    )
    return outs[0], outs[1], list(outs[2 : 2 + ranks]), outs[-1]


def out_grad_pack(places, contexts, dbranch, small, owners, waits=()):
    seqs, length, width = dbranch.shape
    ranks = len(contexts)
    part = contexts[0].shape[2]
    rows = width // owners
    extra = small.shape[0]
    each = part // rows

    def kernel(place_ref, *refs):
        dbranch_ref, small_ref, out_ref = refs[ranks:]
        grad = dbranch_ref[...].reshape(seqs * length, width)
        for q in range(ranks):
            product = dot(refs[q][...].reshape(seqs * length, part), grad, 0, 0).astype(jnp.bfloat16)
            for e in range(each):
                out_ref[place_ref[q] * each + e, :rows, :] = product[e * rows : (e + 1) * rows, :]
        for f in range(owners):
            out_ref[f, rows:, :] = jnp.zeros((extra, width), jnp.bfloat16)
            out_ref[f, rows:, :rows] = small_ref[:, f * rows : (f + 1) * rows]

    shape = (owners, rows + extra, width)
    return run(
        kernel,
        "out_grad_pack",
        (1,),
        [fixed(c) for c in contexts] + [fixed(dbranch), fixed(small)],
        pl.BlockSpec(shape, lambda i, p: (0, 0, 0)),
        kind_of(shape),
        [*contexts, dbranch, small],
        prefetch=(places,),
        waits=waits,
    )


def hidden_grad(places, dqkv, weight, length, picks, addends, dtype, waits=()):
    seqs, _, out_width = dqkv.shape
    width = weight.shape[0]
    blocks = len(picks)
    spread = [(k, a) for k in range(blocks) for a in addends[k]]

    def kernel(place_ref, weight_ref, *refs):
        for k in range(blocks):
            total = dot(refs[k][0], weight_ref[...], 1, 1)
            for j, (of, _) in enumerate(spread):
                if of == k:
                    total = total + wide(refs[blocks + j][0])
            refs[-1][k, 0] = total.astype(dtype)

    return run(
        kernel,
        "hidden_grad",
        (seqs,),
        [fixed(weight)]
        + [pl.BlockSpec((1, length, out_width), lambda b, p, q=q: (b, p[q], 0)) for q in picks]
        + [a.spec((1, length, width), lambda b, p: (b, 0, 0)) for _, a in spread],
        pl.BlockSpec((blocks, 1, length, width), lambda b, p: (0, b, 0, 0)),
        kind_of((blocks, seqs, length, width), dtype),
        [weight] + [dqkv] * blocks + [a.array for _, a in spread],
        prefetch=(places,),
        waits=waits,
        cost=10,
    )


def project_grad_pack(places, blocks, dqkv, owners, extra, waits=()):
    seqs, length, width = blocks[0].shape
    ranks = len(blocks)
    out_width = dqkv.shape[2]
    rows = width // owners
    group = max(1, TILE // rows)

    def kernel(place_ref, *refs):
        dqkv_ref, out_ref, total_ref = refs[ranks:]

        @pl.when(pl.program_id(0) == 0)
        def _():
            total_ref[...] = jnp.zeros_like(total_ref)
            total_ref[0:1, :] = column_sum(wide(dqkv_ref[...].reshape(-1, out_width)))

        total = 0.0
        for q in range(ranks):
            at = pl.ds(pl.multiple_of(place_ref[q] * length, length), length)
            for b in range(seqs):
                total = total + dot(refs[q][b], dqkv_ref[b, at, :], 0, 0)
        total = total.astype(jnp.bfloat16)
        sums = total_ref[...].astype(jnp.bfloat16)
        for e in range(group):
            out_ref[e, :rows, :] = total[e * rows : (e + 1) * rows, :]
            out_ref[e, rows:, :] = sums

    return run(
        kernel,
        "project_grad_pack",
        (owners // group,),
        [x.spec((seqs, length, group * rows), lambda i, p: (0, 0, i)) for x in blocks] + [fixed(dqkv)],
        pl.BlockSpec((group, rows + extra, out_width), lambda i, p: (i, 0, 0)),
        kind_of((owners, rows + extra, out_width)),
        [*arrays(blocks), dqkv],
        prefetch=(places,),
        scratch=(pltpu.VMEM((extra, out_width), jnp.float32),),
        waits=waits,
        cost=10,
    )


def lay_columns(places, blocks, rows):
    total, out_width = blocks[0].shape
    part = out_width // 3
    ranks = len(blocks)
    width = part * ranks

    def kernel(place_ref, *refs):
        for q in range(ranks):
            at = pl.ds(pl.multiple_of(place_ref[q] * part, part), part)
            for k in range(3):
                block = wide(refs[q][:, k * part : (k + 1) * part])
                refs[ranks + k][:, at] = block[:rows, :]
                refs[ranks + 3 + k][:, at] = block[rows : rows + 8, :]

    shape, below = (rows, width), (8, width)
    return run(
        kernel,
        "lay_columns",
        (1,),
        [b.whole() for b in blocks],
        [pl.BlockSpec(shape, lambda i, p: (0, 0))] * 3 + [pl.BlockSpec(below, lambda i, p: (0, 0))] * 3,
        [kind_of(shape, jnp.float32)] * 3 + [kind_of(below, jnp.float32)] * 3,
        arrays(blocks),
        prefetch=(places,),
        cost=10,
    )


def lay_up(places, blocks, chips, part, waits=()):
    _, rows, _ = blocks[0].shape
    ranks = len(blocks)
    shape = (rows, 2 * chips * ranks * part)

    def kernel(place_ref, *refs):
        for q in range(ranks):
            for c in range(2):
                for z in range(chips):
                    at = pl.multiple_of(((z * 2 + c) * ranks + place_ref[q]) * part, part)
                    refs[ranks][:, pl.ds(at, part)] = wide(refs[q][c, :, z * part : (z + 1) * part])

    return run(
        kernel,
        "lay_up",
        (1,),
        [b.whole() for b in blocks],
        pl.BlockSpec(shape, lambda i, p: (0, 0)),
        kind_of(shape, jnp.float32),
        arrays(blocks),
        prefetch=(places,),
        waits=waits,
        cost=10,
    )


def lay_rows(places, blocks, waits=()):
    part, width = blocks[0].shape
    ranks = len(blocks)
    shape = (part * ranks, width)

    def kernel(place_ref, *refs):
        for q in range(ranks):
            refs[ranks][pl.ds(pl.multiple_of(place_ref[q] * part, part), part), :] = wide(refs[q][...])

    return run(
        kernel,
        "lay_rows",
        (1,),
        [b.whole() for b in blocks],
        pl.BlockSpec(shape, lambda i, p: (0, 0)),
        kind_of(shape, jnp.float32),
        arrays(blocks),
        prefetch=(places,),
        waits=waits,
        cost=10,
    )


def lay_chips(at, blocks, waits):
    rows, width = blocks[0].shape
    chips = len(blocks)

    def kernel(at_ref, *refs):
        for d in range(chips):
            refs[chips][at_ref[d]] = refs[d][...]

    shape = (chips, rows, width)
    return run(
        kernel,
        "lay_chips",
        (1,),
        [fixed(b) for b in blocks],
        pl.BlockSpec(shape, lambda i, p: (0, 0, 0)),
        kind_of(shape),
        blocks,
        prefetch=(at,),
        cost=100,
        waits=waits,
    )


def hold(array, waits):
    def kernel(from_ref, to_ref):
        to_ref[...] = from_ref[...]

    rank = array.ndim
    return run(
        kernel,
        "hold",
        (1,),
        [fixed(array)],
        pl.BlockSpec(array.shape, lambda i: (0,) * rank),
        kind_of(array.shape, array.dtype),
        [array],
        waits=waits,
    )


def split(at, own, size, waits=()):
    _, width = own.shape
    chips = at.shape[0]

    def kernel(at_ref, own_ref, *outs):
        for d in range(chips):
            outs[d][...] = own_ref[pl.ds(pl.multiple_of(at_ref[d] * size, size), size), :]

    return run(
        kernel,
        "split",
        (1,),
        [fixed(own)],
        [pl.BlockSpec((size, width), lambda i, p: (0, 0))] * chips,
        [kind_of((size, width))] * chips,
        [own],
        prefetch=(at,),
        cost=100,
        waits=waits,
    )


def tick(*waits, cost=10):
    def kernel(out_ref):
        out_ref[...] = jnp.zeros_like(out_ref)

    return run(
        kernel, "tick", (1,), [], pl.BlockSpec((8, 128), lambda i: (0, 0)), kind_of((8, 128), jnp.float32), [], waits=waits, cost=cost
    )


def total_rows(pieces, waits=()):
    def kernel(*refs):
        total = wide(refs[0][...])
        for ref in refs[1:-1]:
            total = total + wide(ref[...])
        refs[-1][...] = total.astype(jnp.bfloat16)

    shape = pieces[0].shape
    return run(
        kernel,
        "total_rows",
        (1,),
        [fixed(p) for p in pieces],
        pl.BlockSpec(shape, lambda i: (0, 0)),
        kind_of(shape),
        pieces,
        waits=waits,
    )


def total_halves(core, pieces, waits=()):
    rows, width = pieces[0].shape
    half = rows // 2

    def kernel(core_ref, *refs):
        for out_ref, of in ((refs[-2], core_ref[0]), (refs[-1], 1 - core_ref[0])):
            at = pl.ds(pl.multiple_of(of * half, half), half)
            total = wide(refs[0][at, :])
            for ref in refs[1:-2]:
                total = total + wide(ref[at, :])
            out_ref[...] = total.astype(jnp.bfloat16)

    return run(
        kernel,
        "total_halves",
        (1,),
        [fixed(p) for p in pieces],
        [pl.BlockSpec((half, width), lambda i, p: (0, 0))] * 2,
        [kind_of((half, width))] * 2,
        pieces,
        prefetch=(core,),
        waits=waits,
    )


def pair(core, own, other, waits=()):
    rows, width = own.shape

    def kernel(core_ref, own_ref, other_ref, out_ref):
        out_ref[core_ref[0]] = own_ref[...]
        out_ref[1 - core_ref[0]] = other_ref[...]

    shape = (2, rows, width)
    return run(
        kernel,
        "pair",
        (1,),
        [fixed(own), fixed(other)],
        pl.BlockSpec(shape, lambda i, p: (0, 0, 0)),
        kind_of(shape),
        [own, other],
        prefetch=(core,),
        waits=waits,
    )


def plan_rows(segments):
    b, t = segments.shape
    span, win = min(SPAN, t), min(WINDOW, t)
    spans = segments.reshape(b, t // span, span)
    place = jnp.arange(t, dtype=jnp.int32)
    low = jnp.min(jnp.where(segments[:, None, :] == spans[:, :, :1], place, t), axis=2)
    high = jnp.max(jnp.where(segments[:, None, :] == spans[:, :, -1:], place, -1), axis=2)
    start = jnp.minimum(low // ALIGN * ALIGN, t - win)
    fits = jnp.all(high < start + win, axis=1)
    single = jnp.all(segments == segments[:, :1], axis=1)
    kind = jnp.where(single, 0, jnp.where(fits, 1, 2))
    return kind.astype(jnp.int32), start.astype(jnp.int32)

def aligned(start, size):
    return start if isinstance(start, int) else pl.multiple_of(start, size)


def bias_of(col_ref, keys, row_ref, queries):
    return jnp.where(col_ref[0, keys, :] == row_ref[0, :, queries], 0.0, MASKED)


def over(count, body):
    if count == 1:
        body(0)
    else:
        lax.fori_loop(0, count, lambda g, c: (body(g), c)[1], 0, unroll=UNROLL)


def fwd_kernel(heads, kind_ref, start_ref, place_ref, qkv_ref, row_ref, col_ref, ctx_ref, lse_ref, *part_refs):
    b = pl.program_id(0)
    t = qkv_ref.shape[1]
    hw = heads * HEAD_DIM
    span, win = min(SPAN, t), min(WINDOW, t)
    kind = kind_ref[b]

    group = min(2, heads)
    lanes = group * HEAD_DIM

    def attend(g, rows, keys, bias):
        def piece(which):
            return pl.ds(aligned(which * hw + g * lanes, lanes), lanes)

        query, key, value = (qkv_ref[0, r, piece(w)] for w, r in enumerate((rows, keys, keys)))
        parts = []
        for e in range(group):
            at = slice(e * HEAD_DIM, (e + 1) * HEAD_DIM)
            s = dot(key[:, at], query[:, at], 1, 1)
            if bias is not None:
                s = s + bias
            m = jnp.max(s, axis=0, keepdims=True)
            p = jnp.exp(s - m)
            total = jnp.sum(p, axis=0, keepdims=True)
            parts.append(dot(value[:, at], p.astype(jnp.bfloat16), 0, 0) / total)
            lse_ref[0, pl.ds(g * group + e, 1), rows] = m + jnp.log(total)
        ctx_ref[0, rows, piece(0)] = jnp.transpose(jnp.concatenate(parts, axis=0)).astype(jnp.bfloat16)

    def each(size, masked, keys_of):
        size = min(size, t)

        def body(i, _):
            rows = pl.ds(pl.multiple_of(i * size, size), size)
            bias = bias_of(col_ref, keys_of(i), row_ref, rows) if masked else None
            over(heads // group, lambda g: attend(g, rows, keys_of(i), bias))
            return 0

        lax.fori_loop(0, t // size, body, 0)

    @pl.when(kind == 0)
    def _():
        each(FORWARD_SPAN, False, lambda i: pl.ds(0, t))

    @pl.when(kind == 2)
    def _():
        each(span, True, lambda i: pl.ds(0, t))

    @pl.when(kind == 1)
    def _():
        each(span, True, lambda i: pl.ds(pl.multiple_of(start_ref[b, i], ALIGN), win))

    length = part_refs[0].shape[1]
    for q, part_ref in enumerate(part_refs):
        part_ref[0] = ctx_ref[0, pl.ds(pl.multiple_of(place_ref[q] * length, length), length), :]


def attention(qkv, segments, kind, start, places, waits):
    ranks = places.shape[0]
    b, t, w = qkv.shape
    hw = w // 3
    heads = hw // HEAD_DIM

    def at(i, *_):
        return (i, 0, 0)

    return run(
        functools.partial(fwd_kernel, heads),
        "attention_forward",
        (b,),
        [pl.BlockSpec((1, t, w), at), pl.BlockSpec((1, 1, t), at), pl.BlockSpec((1, t, 1), at)],
        [pl.BlockSpec((1, t, hw), at), pl.BlockSpec((1, heads, t), at)]
        + [pl.BlockSpec((1, t // ranks, hw), at)] * ranks,
        [kind_of((b, t, hw)), kind_of((b, heads, t), jnp.float32)] + [kind_of((b, t // ranks, hw))] * ranks,
        [qkv, segments[:, None, :], segments[:, :, None]],
        prefetch=(kind, start, places),
        waits=waits,
        cost=100,
    )

def bwd_kernel(heads, b, kind_ref, start_ref, qkv_ref, do_ref, ctx_ref, lse_ref, row_ref, col_ref, out_ref, dq_acc, delta_ref):
    t = qkv_ref.shape[1]
    hw = heads * HEAD_DIM
    span, win = min(SPAN, t), min(WINDOW, t)
    kind = kind_ref[b]

    def lanes(h, which=0):
        lo = which * hw + h * HEAD_DIM
        return slice(lo, lo + HEAD_DIM)

    prod = do_ref[0].astype(jnp.float32) * ctx_ref[0].astype(jnp.float32)
    high = prod.astype(jnp.bfloat16)
    rest = (prod - high.astype(jnp.float32)).astype(jnp.bfloat16)
    head = lax.broadcasted_iota(jnp.int32, (delta_ref.shape[0], hw), 0)
    of = lax.broadcasted_iota(jnp.int32, (delta_ref.shape[0], hw), 1) // HEAD_DIM
    ones = (head == of).astype(jnp.bfloat16)
    delta_ref[...] = dot(ones, high, 1, 1) + dot(ones, rest, 1, 1)

    group = min(2, heads)
    lanes = group * HEAD_DIM

    def back(g, keys, queries, bias):
        def piece(which):
            return pl.ds(aligned(which * hw + g * lanes, lanes), lanes)

        query, key, value = (qkv_ref[0, r, piece(w)] for w, r in enumerate((queries, keys, keys)))
        grad = do_ref[0, queries, piece(0)]
        key_grads, value_grads = [], []
        for e in range(group):
            at = slice(e * HEAD_DIM, (e + 1) * HEAD_DIM)
            row = pl.ds(g * group + e, 1)
            s = dot(key[:, at], query[:, at], 1, 1)
            if bias is not None:
                s = s + bias
            p = jnp.exp(s - lse_ref[0, row, queries])
            dp = dot(value[:, at], grad[:, at], 1, 1)
            ds = (p * (dp - delta_ref[row, queries])).astype(jnp.bfloat16)
            value_grads.append(dot(p.astype(jnp.bfloat16), grad[:, at], 1, 0))
            key_grads.append(dot(ds, query[:, at], 1, 0))
            into = pl.ds(aligned(g * lanes + e * HEAD_DIM, HEAD_DIM), HEAD_DIM)
            dq_acc[into, queries] += dot(key[:, at], ds, 0, 0)
        out_ref[0, keys, piece(1)] = jnp.concatenate(key_grads, axis=1).astype(jnp.bfloat16)
        out_ref[0, keys, piece(2)] = jnp.concatenate(value_grads, axis=1).astype(jnp.bfloat16)

    dq_acc[...] = jnp.zeros_like(dq_acc)

    def each(size, masked, queries_of):
        size = min(size, t)

        def body(j, _):
            keys = pl.ds(pl.multiple_of(j * size, size), size)
            bias = bias_of(col_ref, keys, row_ref, queries_of(j)) if masked else None
            over(heads // group, lambda g: back(g, keys, queries_of(j), bias))
            return 0

        lax.fori_loop(0, t // size, body, 0)

    @pl.when(kind == 0)
    def _():
        each(BACKWARD_SPAN, False, lambda j: pl.ds(0, t))

    @pl.when(kind == 2)
    def _():
        each(span, True, lambda j: pl.ds(0, t))

    @pl.when(kind == 1)
    def _():
        each(span, True, lambda j: pl.ds(pl.multiple_of(start_ref[b, j], ALIGN), win))

    out_ref[0, :, :hw] = (jnp.transpose(dq_acc[...]) * (HEAD_DIM**-0.5)).astype(jnp.bfloat16)


def attention_back(qkv, dparts, ctx, lse, segments, kind, start, places, which, buffer, waits):
    b, t, w = qkv.shape
    hw = w // 3
    heads = hw // HEAD_DIM
    ranks = len(dparts)
    length = t // ranks

    def kernel(kind_ref, start_ref, place_ref, qkv_ref, *refs):
        grad_ref = refs[-1]
        for q in range(ranks):
            grad_ref[0, pl.ds(pl.multiple_of(place_ref[q] * length, length), length), :] = refs[q][0]
        bwd_kernel(heads, which, kind_ref, start_ref, qkv_ref, grad_ref, *refs[ranks : ranks + 4], *refs[-4:-1])

    def at(i, *_):
        return (which, 0, 0)

    ins = [pl.BlockSpec((1, t, w), at)] + [pl.BlockSpec((1, length, hw), at)] * ranks
    ins += [
        pl.BlockSpec((1, t, hw), at),
        pl.BlockSpec((1, heads, t), at),
        pl.BlockSpec((1, 1, t), at),
        pl.BlockSpec((1, t, 1), at),
    ]
    operands = [qkv, *dparts, ctx, lse, segments[:, None, :], segments[:, :, None]]
    alias = None
    if buffer is not None:
        ins.append(pl.BlockSpec(memory_space=pl.ANY))
        operands.append(buffer)
        alias = {3 + len(ins) - 1: 0}
    return run(
        kernel,
        "attention_backward",
        (1,),
        ins,
        pl.BlockSpec((1, t, w), at),
        kind_of((b, t, w)),
        operands,
        prefetch=(kind, start, places),
        scratch=(
            pltpu.VMEM((hw, t), jnp.float32),
            pltpu.VMEM((-(-heads // 8) * 8, t), jnp.float32),
            pltpu.VMEM((1, t, hw), jnp.bfloat16),
        ),
        alias=alias,
        waits=waits,
    )


AXES = ("seq", "z", "core")
ROWS = ("z", "core")
EXTRA = 16


def low(tensor):
    return tensor.astype(jnp.bfloat16)


class Ring:
    def __init__(self):
        self.ranks = lax.axis_size("seq")
        self.chips = lax.axis_size("z")
        self.index = lax.axis_index("seq")
        self.core = lax.axis_index("core")
        self.count = self.ranks.bit_length() - 1

    def bit(self, k, core):
        if self.count == 2 and core == 1:
            k = 1 - k
        return 1 << k

    def offset(self, q, core):
        return sum(self.bit(k, core) for k in range(self.count) if q >> k & 1)

    def place(self, q):
        return jnp.bitwise_xor(self.index, jnp.where(self.core == 0, self.offset(q, 0), self.offset(q, 1)))

    def hop(self, block, k):
        pairs = []
        for s in range(self.ranks):
            for z in range(self.chips):
                for c in range(2):
                    to = s ^ self.bit(k, c)
                    pairs.append(((s * self.chips + z) * 2 + c, (to * self.chips + z) * 2 + c))
        return lax.ppermute(block, AXES, pairs)

    def gather(self, block):
        blocks = [block]
        for k in range(self.count):
            blocks = blocks + [self.hop(b, k) for b in blocks]
        return [View(b) for b in blocks]

    def exchange(self, blocks):
        out = [blocks[0]]
        for q in range(1, self.ranks):
            pairs = []
            for s in range(self.ranks):
                for z in range(self.chips):
                    for c in range(2):
                        to = s ^ self.offset(q, c)
                        pairs.append(((s * self.chips + z) * 2 + c, (to * self.chips + z) * 2 + c))
            out.append(lax.ppermute(blocks[q], AXES, pairs))
        return out

    def shift(self, block, d):
        return lax.ppermute(block, "z", [(z, (z + d) % self.chips) for z in range(self.chips)])


def swap(block):
    return lax.ppermute(block, "core", [(0, 1), (1, 0)])


def put(blocks, ring, axis):
    shape = list(blocks[0].shape)
    size = shape[axis]
    shape[axis] = size * len(blocks)
    whole = jnp.zeros(shape, blocks[0].dtype)
    for q, block in enumerate(blocks):
        whole = lax.dynamic_update_slice_in_dim(whole, block, ring.place(q) * size, axis)
    return whole


def local(
    hidden_in,
    segments,
    q_weight,
    k_weight,
    v_weight,
    out_weight,
    q_bias,
    v_bias,
    out_bias,
    up_weight,
    up_bias,
    down_weight,
    down_bias,
    norm1_gain,
    norm1_bias,
    norm2_gain,
    norm2_bias,
    out_grad,
):
    ring = Ring()
    here, core = ring.index, ring.core
    ranks, chips = ring.ranks, ring.chips
    owners = chips * 2
    z_index = lax.axis_index("z")
    owner = z_index * 2 + core
    seqs, length, width = hidden_in.shape
    full = length * ranks
    head_width = width // ranks
    out_width = 3 * head_width
    rows = width // owners
    units = down_weight.shape[0]
    part = units // ranks
    count = seqs * length
    score_scale = HEAD_DIM ** (-0.5)
    first_core = core == 0
    core_index = core.astype(jnp.int32).reshape(1)
    places = jnp.stack([ring.place(q) for q in range(ranks)]).astype(jnp.int32)
    blocks = range(ranks)

    heads_at = here * head_width
    mine = jnp.concatenate(
        [lax.dynamic_slice_in_dim(w, heads_at, head_width, 1) for w in (q_weight, k_weight, v_weight)], axis=1
    )
    vectors = (q_bias, v_bias, out_bias, down_bias, norm1_gain, norm1_bias, norm2_gain, norm2_bias)
    known = len(vectors)
    packed = jnp.pad(
        up_bias.reshape(-1, rows), ((known, EXTRA - known - units // rows), (0, out_width - rows))
    )
    for i, vector in enumerate(vectors):
        packed = packed + jnp.pad(vector[None], ((i, EXTRA - 1 - i), (0, out_width - rows)))
    mine = jnp.concatenate([mine, packed], axis=0)

    def up_columns(of_core):
        return jnp.concatenate(
            [
                lax.dynamic_slice_in_dim(up_weight, ((z * 2 + of_core) * ranks + here) * part, part, 1)
                for z in range(chips)
            ],
            axis=1,
        )

    own_up, other_up = up_columns(core), swap(up_columns(1 - core))
    up_rows = jnp.concatenate(
        [jnp.where(first_core, own_up, other_up), jnp.where(first_core, other_up, own_up)], axis=0
    )
    hidden = ring.gather(hidden_in)
    shifts = jnp.stack([(z_index - d) % chips for d in range(chips)]).astype(jnp.int32)
    up_block = lay_chips(shifts, [up_rows] + [ring.shift(up_rows, d) for d in range(1, chips)], ())
    up_block = hold(up_block.reshape(width, chips * part), (hidden[-1].array,))
    gathered = lax.all_gather(mine, ROWS, axis=0)
    down_rows = hold(lax.dynamic_slice_in_dim(down_weight, here * part, part, 0), (gathered,))
    down_block = lax.all_gather(down_rows, "z", axis=0, tiled=True)
    output_weight = lax.all_gather(hold(out_weight, (down_rows,)), ROWS, axis=0, tiled=True)
    up_weights = ring.gather(up_block)
    kind, start = plan_rows(segments)
    keep = wide(lax.dynamic_slice_in_dim(segments, here * length, length, 1) != 0)[:, :, None]

    qkv_weight = gathered[:, :rows].reshape(width, out_width)
    gathered = wide(gathered[:, rows:, :rows])
    vectors = gathered.transpose(1, 0, 2).reshape(EXTRA, width)
    biases = lax.dynamic_slice_in_dim(vectors, heads_at, head_width, 1)
    qkv_bias = jnp.concatenate([biases[0], jnp.zeros_like(biases[0]), biases[1]])[None]
    scales = jnp.where(jnp.arange(out_width) < head_width, score_scale, 1.0)[None]
    qkv = project(places, hidden, qkv_weight, qkv_bias, scales)
    contexts, log_totals, *context_parts = attention(
        qkv, segments, kind, start, places, (up_block,)
    )
    context_parts = ring.exchange(context_parts)
    down_weights = ring.gather(hold(down_block, (*context_parts[1:], *arrays(up_weights[1:3]))))
    sums_one, first_low = out_norm(
        places,
        context_parts,
        output_weight,
        hidden_in,
        vectors,
    )

    first_low = first_low.reshape(count, width)
    first_other = swap(first_low)
    upper_bias = gathered[:, known : known + units // rows].reshape(chips, 2, ranks, part)
    upper_bias = lax.dynamic_index_in_dim(upper_bias, core, 1, False)
    upper_bias = [
        lax.dynamic_index_in_dim(upper_bias, ring.place(q), 1, False).reshape(1, -1) for q in blocks
    ]
    actives, slopes = up_forward(
        first_low, first_other, up_weights, upper_bias, arrays(down_weights[1:2])
    )
    mixed_other = down_forward(actives, down_weights, count, count, jnp.bfloat16)
    mixed = down_forward(actives, down_weights, 0, count, jnp.float32, (mixed_other,))
    layer_out, dsum_two, dmixed, totals_two = norm_two(mixed, swap(mixed_other), sums_one, vectors, out_grad, keep)

    dmixed = dmixed.reshape(count, width)
    dmixed_other = swap(dmixed)
    none = [()] * ranks
    odd, even = [q for q in blocks if q % 2], [q for q in blocks if q % 2 == 0]
    down_sent = down_grad([actives[q] for q in odd], dmixed, dmixed_other, none)
    duppers, up_sums, dfirst, dfirst_other = ffn_back(
        dmixed, dmixed_other, slopes, down_weights, up_weights, (tick(down_sent),)
    )
    dfirst_other = swap(dfirst_other)
    dsum_one, dbranch, dcontexts, totals_one = norm_one_back(
        places, dfirst, dfirst_other, dsum_two, sums_one, vectors, output_weight, head_width, (tick(duppers[0], cost=10),)
    )
    dcontexts = ring.exchange(dcontexts)

    def spread(made, sent):
        came = {q: [] for q in blocks}
        for k in range(ring.count):
            step = 1 << k
            got = ring.hop(sent, k)
            for i, q in enumerate(range(0, ranks, 2 * step)):
                came[q].append(View(got, i))
            if k + 1 < ring.count:
                turn = [q + 2 * step for q in range(0, ranks, 4 * step)]
                sent = made(turn, [came[q] for q in turn])
        return came[0], sent

    def down_made(turn, addends):
        return down_grad([actives[q] for q in turn], dmixed, dmixed_other, addends, (tick(dbranch),))

    down_came, down_hop = spread(down_made, down_sent)
    up_sent = up_grad([duppers[q] for q in odd], first_low, first_other, none, (down_hop,))

    extra = -(-(6 + ranks) // EXTRA) * EXTRA
    up_totals = put([up_sums[q : q + 1] for q in blocks], ring, 0).reshape(ranks, chips, 1, part)
    up_totals = jnp.where(jnp.arange(2)[None, None, :, None] == core, up_totals, 0.0)
    up_totals = jnp.pad(up_totals, ((0, 0), (0, 0), (0, 0), (0, rows - part))).reshape(ranks, width)
    small = jnp.concatenate(
        [totals_two[:3], totals_one[:3], up_totals, jnp.zeros((extra - 6 - ranks, width), jnp.float32)], axis=0
    )
    out_pack = out_grad_pack(places, context_parts, dbranch, low(small), owners, (up_sent,))
    out_shard = lax.psum_scatter(out_pack.reshape(-1, width), ROWS, scatter_dimension=0, tiled=True)

    common = (qkv, dcontexts, contexts, log_totals, segments, kind, start, places)
    dqkv = attention_back(*common, 0, None, (out_pack,))

    def up_made(turn, addends):
        return up_grad([duppers[q] for q in turn], first_low, first_other, addends, (down_pieces[0],))

    down_own = down_grad([actives[0]], dmixed, dmixed_other, [down_came], (dqkv,))[0]
    ahead = jnp.stack([(z_index + d) % chips for d in range(chips)]).astype(jnp.int32)
    down_pieces = split(ahead, down_own, part)
    up_came, up_hop = spread(up_made, up_sent)
    for which in range(1, seqs):
        dqkv = attention_back(*common, which, dqkv, (up_hop,))

    def shifted(pieces):
        return [pieces[0]] + [ring.shift(pieces[d], d) for d in range(1, chips)]

    def hidden_made(turn, addends, waits=()):
        return hidden_grad(places, dqkv, qkv_weight, length, turn, addends, jnp.bfloat16, waits or (up_pieces[0],))

    qkv_pack = project_grad_pack(places, hidden, dqkv, owners, EXTRA, (out_shard,))
    qkv_shard = lax.psum_scatter(qkv_pack.reshape(-1, out_width), ROWS, scatter_dimension=0, tiled=True)
    out_sum = [wide(out_shard)]
    for k in range(ring.count):
        out_sent = low(out_sum[-1])
        out_sum.append(out_sum[-1] + wide(ring.hop(out_sent, k)))
    hidden_sent = hidden_made(odd, none, (qkv_pack, out_sent))
    down_shard = total_rows(shifted(down_pieces), (hidden_sent,))
    up_own = up_grad([duppers[0]], first_low, first_other, [up_came], (down_shard,))[0]
    up_pieces = split(ahead, up_own, 2 * rows)
    hidden_came, hidden_hop = spread(hidden_made, hidden_sent)
    keep_part, take_part = total_halves(core_index, shifted(up_pieces), (hidden_hop,))
    down_shard = hold(down_shard, (keep_part,))
    down_parts = ring.gather(down_shard)
    up_pair = pair(core_index, keep_part, swap(take_part), (down_shard,))
    input_grad = hidden_grad(
        places, dqkv, qkv_weight, length, [0], [[View(dsum_one)] + hidden_came], jnp.float32
    )[0]

    up_parts = ring.gather(up_pair)
    qkv_parts = ring.gather(qkv_shard)
    out_pack = out_sum[-1]
    down_weight_grad = lay_rows(places, down_parts, (input_grad,))
    if part % 128 == 0:
        up_weight_grad = lay_up(places, up_parts, chips, part, (input_grad,))
    else:
        up_weight_grad = wide(put([b.value()[None] for b in up_parts], ring, 0))
        up_weight_grad = (
            up_weight_grad.reshape(ranks, 2, rows, chips, part).transpose(2, 3, 1, 0, 4).reshape(rows, owners * units)
        )
    if head_width % 128 == 0:
        *qkv_grads, q_sums, _, v_sums = lay_columns(places, qkv_parts, rows)
    else:
        laid = wide(put([b.value()[None] for b in qkv_parts], ring, 0))
        laid = laid.reshape(ranks, rows + EXTRA, 3, head_width).transpose(2, 1, 0, 3).reshape(3, -1, width)
        qkv_grads, q_sums, v_sums = [g[:rows] for g in laid], laid[0, rows:], laid[2, rows:]

    def mine_of(sums):
        return lax.dynamic_slice_in_dim(sums[0], owner * rows, rows, 0)

    small = out_pack[rows:, :rows]
    up_bias_grad = small[6 : 6 + ranks, :part].reshape(-1)
    return (
        layer_out,
        input_grad,
        *qkv_grads,
        out_pack[:rows],
        mine_of(q_sums),
        mine_of(v_sums),
        small[3],
        up_weight_grad,
        up_bias_grad,
        down_weight_grad,
        small[0],
        small[4],
        small[5],
        small[1],
        small[2],
    )


def solution(mesh):
    ranks, owners = mesh.shape["seq"], mesh.shape["fsdp"]
    grid = Mesh(mesh.devices.reshape(ranks, owners // 2, 2), AXES)
    tokens, matrix, vector = P(ROWS, "seq", None), P(ROWS, None), P(ROWS)
    return jax.shard_map(
        local,
        mesh=grid,
        in_specs=(
            tokens,
            matrix,
            matrix,
            matrix,
            matrix,
            matrix,
            vector,
            vector,
            vector,
            matrix,
            vector,
            matrix,
            vector,
            vector,
            vector,
            vector,
            vector,
            tokens,
        ),
        out_specs=(
            tokens,
            tokens,
            matrix,
            matrix,
            matrix,
            matrix,
            vector,
            vector,
            vector,
            matrix,
            vector,
            matrix,
            vector,
            vector,
            vector,
            vector,
            vector,
        ),
        check_vma=False,
    )
```

```python
import functools

import jax
import jax.numpy as jnp
from jax import lax
from jax.experimental import pallas as pl
from jax.experimental.pallas import tpu as pltpu
from jax.sharding import Mesh
from jax.sharding import PartitionSpec as P

HEAD_DIM = 64
SPAN = 256
ALIGN = 128
WINDOW = 512
FORWARD_SPAN = 1024
BACKWARD_SPAN = 512
UNROLL = True
MASKED = -1e30


def dot(a,b,ca,cb):
    return lax.dot_general(a,b,(((ca,),(cb,)),((),())),preferred_element_type=jnp.float32)


TILE = 256


def run(kernel, name, grid, ins, outs, shapes, operands, prefetch=(), scratch=(), alias=None, waits=(), cost=10):
    known = len(prefetch) + len(ins)

    def waiting(*refs):
        kernel(*refs[:known], *refs[known + len(waits) :])

    ins = list(ins) + [pl.BlockSpec(memory_space=pl.ANY)] * len(waits)
    operands = list(operands) + list(waits)
    return pl.pallas_call(
        waiting,
        grid_spec=pltpu.PrefetchScalarGridSpec(
            num_scalar_prefetch=len(prefetch), grid=grid, in_specs=ins, out_specs=outs, scratch_shapes=scratch
        ),
        out_shape=shapes,
        input_output_aliases=alias or {},
        compiler_params=pltpu.CompilerParams(vmem_limit_bytes=50 << 20),
        cost_estimate=pl.CostEstimate(flops=cost * 3000000000, bytes_accessed=1000, transcendentals=0),
        name=name,
    )(*prefetch, *operands)


def fixed(array):
    rank = array.ndim
    return pl.BlockSpec(array.shape, lambda *_: (0,) * rank, pipeline_mode=pl.Buffered(buffer_count=1))


class View:
    def __init__(self, array, i=None):
        self.array, self.i = array, i
        self.shape = array.shape if i is None else array.shape[1:]

    def spec(self, block, place):
        i = self.i
        if i is None:
            return pl.BlockSpec(block, place)
        return pl.BlockSpec((None,) + tuple(block), lambda *a: (i,) + tuple(place(*a)))

    def whole(self):
        rank, i = len(self.shape), self.i
        once = pl.Buffered(buffer_count=1)
        if i is None:
            return pl.BlockSpec(self.shape, lambda *_: (0,) * rank, pipeline_mode=once)
        return pl.BlockSpec((None,) + tuple(self.shape), lambda *_: (i,) + (0,) * rank, pipeline_mode=once)

    def value(self):
        return self.array if self.i is None else self.array[self.i]


def arrays(views):
    return [v.array for v in views]


def kind_of(shape, dtype=jnp.bfloat16):
    return jax.ShapeDtypeStruct(tuple(shape), dtype)


def wide(tensor):
    return tensor.astype(jnp.float32)


def standardize(values):
    center = jnp.mean(values, axis=1, keepdims=True)
    offset = values - center
    inverse = lax.rsqrt(jnp.mean(offset * offset, axis=1, keepdims=True) + 1e-05)
    return offset * inverse, inverse


def standardize_back(upstream, normed, inverse, gain):
    scaled = upstream * gain
    return inverse * (
        scaled
        - jnp.mean(scaled, axis=1, keepdims=True)
        - normed * jnp.mean(scaled * normed, axis=1, keepdims=True)
    )


def column_sum(values):
    return jnp.sum(values, axis=0, keepdims=True)


OUT_BIAS, DOWN_BIAS, GAIN_ONE, SHIFT_ONE, GAIN_TWO, SHIFT_TWO = 2, 3, 4, 5, 6, 7


def project(places, blocks, weight, bias, scale):
    seqs, length, width = blocks[0].shape
    ranks = len(blocks)
    out_width = weight.shape[1]

    def kernel(place_ref, weight_ref, bias_ref, scale_ref, *refs):
        for q in range(ranks):

            @pl.when(pl.program_id(0) // seqs == q)
            def _(q=q):
                product = dot(refs[q][0], weight_ref[...], 1, 0) + bias_ref[...]
                refs[ranks][0] = (product * scale_ref[...]).astype(jnp.bfloat16)

    def source(q):
        return lambda i, p: (jnp.clip(i - q * seqs, 0, seqs - 1), 0, 0)

    return run(
        kernel,
        "project",
        (ranks * seqs,),
        [fixed(weight), fixed(bias), fixed(scale)]
        + [blocks[q].spec((1, length, width), source(q)) for q in range(ranks)],
        pl.BlockSpec((1, length, out_width), lambda i, p: (i % seqs, p[i // seqs], 0)),
        kind_of((seqs, length * ranks, out_width)),
        [weight, bias, scale, *arrays(blocks)],
        prefetch=(places,),
    )


def out_norm(places, contexts, weight, hidden, vectors, waits=()):
    seqs, length, width = hidden.shape
    ranks = len(contexts)
    part = contexts[0].shape[2]

    def kernel(place_ref, *refs):
        weight_ref, hidden_ref, vector_ref, sum_ref, first_ref = refs[ranks:]
        total = wide(hidden_ref[0]) + vector_ref[OUT_BIAS : OUT_BIAS + 1, :]
        for q in range(ranks):
            rows = pl.ds(pl.multiple_of(place_ref[q] * part, part), part)
            total = total + dot(refs[q][0], weight_ref[rows, :], 1, 0)
        total = total.astype(jnp.bfloat16)
        sum_ref[0] = total
        normed, _ = standardize(wide(total))
        first = normed * vector_ref[GAIN_ONE : GAIN_ONE + 1, :] + vector_ref[SHIFT_ONE : SHIFT_ONE + 1, :]
        first_ref[0] = first.astype(jnp.bfloat16)

    tokens = pl.BlockSpec((1, length, width), lambda b, p: (b, 0, 0))
    return run(
        kernel,
        "out_norm",
        (seqs,),
        [pl.BlockSpec((1, length, part), lambda b, p: (b, 0, 0))] * ranks + [fixed(weight), tokens, fixed(vectors)],
        [tokens, tokens],
        [kind_of(hidden.shape), kind_of(hidden.shape)],
        [*contexts, weight, hidden, vectors],
        prefetch=(places,),
        waits=waits,
    )


def up_forward(own, other, weights, biases, waits=()):
    count, width = own.shape
    units = weights[0].shape[1]
    blocks = len(weights)
    tile = min(TILE, count)
    half = count // tile

    def kernel(own_ref, other_ref, *refs):
        def body(tokens):
            uppers = [dot(tokens, refs[q][...], 1, 0) for q in range(blocks)]
            for q in range(blocks):
                upper = uppers[q] + refs[blocks + q][...]
                tail = 0.5 * (1.0 + lax.erf(upper * 0.7071067811865476))
                refs[2 * blocks + q][...] = (upper * tail).astype(jnp.bfloat16)
                bell = jnp.exp(-0.5 * upper * upper) * 0.3989422804014327
                refs[3 * blocks + q][...] = (tail + upper * bell).astype(jnp.bfloat16)

        @pl.when(pl.program_id(0) < half)
        def _():
            body(own_ref[...])

        @pl.when(pl.program_id(0) >= half)
        def _():
            body(other_ref[...])

    outs = run(
        kernel,
        "up_forward",
        (2 * half,),
        [
            pl.BlockSpec((tile, width), lambda i: (jnp.minimum(i, half - 1), 0)),
            pl.BlockSpec((tile, width), lambda i: (jnp.maximum(i - half, 0), 0)),
        ]
        + [w.whole() for w in weights]
        + [fixed(b) for b in biases],
        [pl.BlockSpec((tile, units), lambda i: (i, 0))] * (2 * blocks),
        [kind_of((2 * count, units))] * (2 * blocks),
        [own, other, *arrays(weights), *biases],
        waits=waits,
    )
    return list(outs[:blocks]), list(outs[blocks:])


def down_forward(actives, weights, first, count, dtype, waits=()):
    blocks = len(actives)
    units, width = weights[0].shape
    tile = min(TILE, count)

    def kernel(*refs):
        total = dot(refs[0][...], refs[blocks][...], 1, 0)
        for q in range(1, blocks):
            total = total + dot(refs[q][...], refs[blocks + q][...], 1, 0)
        refs[-1][...] = total.astype(dtype)

    return run(
        kernel,
        "down_forward",
        (count // tile,),
        [pl.BlockSpec((tile, units), lambda i: (i + first // tile, 0))] * blocks + [w.whole() for w in weights],
        pl.BlockSpec((tile, width), lambda i: (i, 0)),
        kind_of((count, width), dtype),
        [*actives, *arrays(weights)],
        waits=waits,
    )


def norm_two(mixed, mixed_other, sums_one, vectors, out_grad, keep):
    seqs, length, width = sums_one.shape

    def kernel(mixed_ref, other_ref, sum_ref, vector_ref, grad_ref, keep_ref, out_ref, dmixed_ref, total_ref):
        @pl.when(pl.program_id(0) == 0)
        def _():
            total_ref[...] = jnp.zeros_like(total_ref)

        def vector(i):
            return vector_ref[i : i + 1, :]

        normed, _ = standardize(wide(sum_ref[0]))
        first = normed * vector(GAIN_ONE) + vector(SHIFT_ONE)
        mixed = wide(mixed_ref[0]) + wide(other_ref[0]) + vector(DOWN_BIAS)
        normed, inverse = standardize(first + mixed)
        out_ref[0] = (normed * vector(GAIN_TWO) + vector(SHIFT_TWO)).astype(jnp.bfloat16)
        cot = wide(grad_ref[0]) * keep_ref[0]
        dmixed = standardize_back(cot, normed, inverse, vector(GAIN_TWO)).astype(jnp.bfloat16)
        dmixed_ref[0] = dmixed
        total_ref[0:1, :] += column_sum(wide(dmixed))
        total_ref[1:2, :] += column_sum(cot * normed)
        total_ref[2:3, :] += column_sum(cot)

    tokens = pl.BlockSpec((1, length, width), lambda b: (b, 0, 0))
    shape = sums_one.shape
    return run(
        kernel,
        "norm_two",
        (seqs,),
        [tokens, tokens, tokens, fixed(vectors), tokens, pl.BlockSpec((1, length, 1), lambda b: (b, 0, 0))],
        [tokens, tokens, pl.BlockSpec((8, width), lambda b: (0, 0))],
        [kind_of(shape), kind_of(shape), kind_of((8, width), jnp.float32)],
        [mixed.reshape(shape), mixed_other.reshape(shape), sums_one, vectors, out_grad, keep],
    )


def ffn_back(own, other, slopes, downs, ups, waits=()):
    blocks = len(slopes)
    count, width = own.shape
    units = slopes[0].shape[1]
    tile = min(TILE, count)
    half = count // tile

    def kernel(own_ref, other_ref, *refs):
        slope_refs, down_refs, up_refs = refs[:blocks], refs[blocks : 2 * blocks], refs[2 * blocks : 3 * blocks]
        upper_refs, total_ref, here_ref, there_ref = refs[3 * blocks : 4 * blocks], refs[-3], refs[-2], refs[-1]
        step = pl.program_id(0)

        @pl.when(step == 0)
        def _():
            total_ref[...] = jnp.zeros_like(total_ref)

        def body(grad):
            back = [dot(grad, down_refs[q][...], 1, 1) for q in range(blocks)]
            total = 0.0
            for q in range(blocks):
                upper = back[q] * wide(slope_refs[q][...])
                total_ref[q : q + 1, :] += column_sum(upper)
                upper_refs[q][...] = upper.astype(jnp.bfloat16)
            for q in range(blocks):
                total = total + dot(upper_refs[q][...], up_refs[q][...], 1, 1)
            return total

        @pl.when(step < half)
        def _():
            there_ref[...] = body(other_ref[...]).astype(jnp.bfloat16)

        @pl.when(step >= half)
        def _():
            here_ref[...] = body(own_ref[...]).astype(jnp.bfloat16)

    def early(i):
        return (jnp.minimum(i, half - 1), 0)

    def late(i):
        return (jnp.maximum(i - half, 0), 0)

    def both(i):
        return ((i + half) % (2 * half), 0)

    outs = run(
        kernel,
        "feed_forward_back",
        (2 * half,),
        [pl.BlockSpec((tile, width), late), pl.BlockSpec((tile, width), early)]
        + [pl.BlockSpec((tile, units), both)] * blocks
        + [w.whole() for w in (*downs, *ups)],
        [pl.BlockSpec((tile, units), both)] * blocks
        + [
            pl.BlockSpec((max(8, blocks), units), lambda i: (0, 0)),
            pl.BlockSpec((tile, width), late),
            pl.BlockSpec((tile, width), early),
        ],
        [kind_of((2 * count, units))] * blocks
        + [
            kind_of((max(8, blocks), units), jnp.float32),
            kind_of((count, width)),
            kind_of((count, width)),
        ],
        [own, other, *slopes, *arrays(downs), *arrays(ups)],
        waits=waits,
    )
    return list(outs[:blocks]), outs[blocks], outs[blocks + 1], outs[blocks + 2]


def down_grad(actives, own, other, addends, waits=()):
    count, width = own.shape
    units = actives[0].shape[1]
    tile = min(TILE, units)
    blocks = len(actives)
    spread = [(q, a) for q in range(blocks) for a in addends[q]]

    def kernel(own_ref, other_ref, *refs):
        for q in range(blocks):
            total = dot(refs[q][:count, :], own_ref[...], 0, 0) + dot(refs[q][count:, :], other_ref[...], 0, 0)
            for j, (of, _) in enumerate(spread):
                if of == q:
                    total = total + wide(refs[blocks + j][...])
            refs[-1][q] = total.astype(jnp.bfloat16)

    return run(
        kernel,
        "down_grad",
        (units // tile,),
        [fixed(own), fixed(other)]
        + [pl.BlockSpec((2 * count, tile), lambda i: (0, i))] * blocks
        + [a.spec((tile, width), lambda i: (i, 0)) for _, a in spread],
        pl.BlockSpec((blocks, tile, width), lambda i: (0, i, 0)),
        kind_of((blocks, units, width)),
        [own, other, *actives, *(a.array for _, a in spread)],
        waits=waits,
    )


def up_grad(uppers, own, other, addends, waits=()):
    count, width = own.shape
    units = uppers[0].shape[1]
    tile = min(TILE, width)
    blocks = len(uppers)
    spread = [(q, a) for q in range(blocks) for a in addends[q]]

    def kernel(own_ref, other_ref, *refs):
        for q in range(blocks):
            total = dot(own_ref[...], refs[q][:count, :], 0, 0) + dot(other_ref[...], refs[q][count:, :], 0, 0)
            for j, (of, _) in enumerate(spread):
                if of == q:
                    total = total + wide(refs[blocks + j][...])
            refs[-1][q] = total.astype(jnp.bfloat16)

    columns = pl.BlockSpec((count, tile), lambda i: (0, i))
    return run(
        kernel,
        "up_grad",
        (width // tile,),
        [columns, columns]
        + [fixed(u) for u in uppers]
        + [a.spec((tile, units), lambda i: (i, 0)) for _, a in spread],
        pl.BlockSpec((blocks, tile, units), lambda i: (0, i, 0)),
        kind_of((blocks, width, units)),
        [own, other, *uppers, *(a.array for _, a in spread)],
        waits=waits,
    )


def norm_one_back(places, dfirst, dfirst_other, dmixed, sums_one, vectors, weight, part, waits=()):
    seqs, length, width = sums_one.shape
    ranks = width // part

    def kernel(place_ref, own_ref, other_ref, dmixed_ref, sum_ref, vector_ref, weight_ref, *outs):
        @pl.when(pl.program_id(0) == 0)
        def _():
            outs[-1][...] = jnp.zeros_like(outs[-1])

        upstream = wide(dmixed_ref[0]) + wide(own_ref[0]) + wide(other_ref[0])
        normed, inverse = standardize(wide(sum_ref[0]))
        dsum = standardize_back(upstream, normed, inverse, vector_ref[GAIN_ONE : GAIN_ONE + 1, :])
        dbranch = dsum.astype(jnp.bfloat16)
        outs[0][0] = dbranch
        for q in range(ranks):
            rows = pl.ds(pl.multiple_of(place_ref[q] * part, part), part)
            outs[1 + q][0] = dot(dbranch, weight_ref[rows, :], 1, 1).astype(jnp.bfloat16)
        outs[-1][0:1, :] += column_sum(wide(dbranch))
        outs[-1][1:2, :] += column_sum(upstream * normed)
        outs[-1][2:3, :] += column_sum(upstream)

    tokens = pl.BlockSpec((1, length, width), lambda b, p: (b, 0, 0))
    shape = sums_one.shape
    outs = run(
        kernel,
        "norm_one_back",
        (seqs,),
        [tokens, tokens, tokens, tokens, fixed(vectors), fixed(weight)],
        [tokens]
        + [pl.BlockSpec((1, length, part), lambda b, p: (b, 0, 0))] * ranks
        + [pl.BlockSpec((8, width), lambda b, p: (0, 0))],
        [kind_of(shape)]
        + [kind_of((seqs, length, part))] * ranks
        + [kind_of((8, width), jnp.float32)],
        [dfirst.reshape(shape), dfirst_other.reshape(shape), dmixed.reshape(shape), sums_one, vectors, weight],
        prefetch=(places,),
        waits=waits,
    )
    return outs[0], list(outs[1 : 1 + ranks]), outs[-1]


def out_grad_pack(places, contexts, dbranch, small, owners, waits=()):
    seqs, length, width = dbranch.shape
    ranks = len(contexts)
    part = contexts[0].shape[2]
    rows = width // owners
    extra = small.shape[0]
    each = part // rows

    def kernel(place_ref, *refs):
        dbranch_ref, small_ref, out_ref = refs[ranks:]
        grad = dbranch_ref[...].reshape(seqs * length, width)
        for q in range(ranks):
            product = dot(refs[q][...].reshape(seqs * length, part), grad, 0, 0).astype(jnp.bfloat16)
            for e in range(each):
                out_ref[place_ref[q] * each + e, :rows, :] = product[e * rows : (e + 1) * rows, :]
        for f in range(owners):
            out_ref[f, rows:, :] = jnp.zeros((extra, width), jnp.bfloat16)
            out_ref[f, rows:, :rows] = small_ref[:, f * rows : (f + 1) * rows]

    shape = (owners, rows + extra, width)
    return run(
        kernel,
        "out_grad_pack",
        (1,),
        [fixed(c) for c in contexts] + [fixed(dbranch), fixed(small)],
        pl.BlockSpec(shape, lambda i, p: (0, 0, 0)),
        kind_of(shape),
        [*contexts, dbranch, small],
        prefetch=(places,),
        waits=waits,
    )


def hidden_grad(places, dqkv, weight, length, picks, addends, dtype, waits=()):
    seqs, _, out_width = dqkv.shape
    width = weight.shape[0]
    blocks = len(picks)
    spread = [(k, a) for k in range(blocks) for a in addends[k]]

    def kernel(place_ref, weight_ref, *refs):
        for k in range(blocks):
            total = dot(refs[k][0], weight_ref[...], 1, 1)
            for j, (of, _) in enumerate(spread):
                if of == k:
                    total = total + wide(refs[blocks + j][0])
            refs[-1][k, 0] = total.astype(dtype)

    return run(
        kernel,
        "hidden_grad",
        (seqs,),
        [fixed(weight)]
        + [pl.BlockSpec((1, length, out_width), lambda b, p, q=q: (b, p[q], 0)) for q in picks]
        + [a.spec((1, length, width), lambda b, p: (b, 0, 0)) for _, a in spread],
        pl.BlockSpec((blocks, 1, length, width), lambda b, p: (0, b, 0, 0)),
        kind_of((blocks, seqs, length, width), dtype),
        [weight] + [dqkv] * blocks + [a.array for _, a in spread],
        prefetch=(places,),
        waits=waits,
        cost=2,
    )


def project_grad_pack(places, blocks, dqkv, owners, extra, waits=()):
    seqs, length, width = blocks[0].shape
    ranks = len(blocks)
    out_width = dqkv.shape[2]
    rows = width // owners
    group = max(1, TILE // rows)

    def kernel(place_ref, *refs):
        dqkv_ref, out_ref, total_ref = refs[ranks:]

        @pl.when(pl.program_id(0) == 0)
        def _():
            total_ref[...] = jnp.zeros_like(total_ref)
            total_ref[0:1, :] = column_sum(wide(dqkv_ref[...].reshape(-1, out_width)))

        total = 0.0
        for q in range(ranks):
            at = pl.ds(pl.multiple_of(place_ref[q] * length, length), length)
            for b in range(seqs):
                total = total + dot(refs[q][b], dqkv_ref[b, at, :], 0, 0)
        total = total.astype(jnp.bfloat16)
        sums = total_ref[...].astype(jnp.bfloat16)
        for e in range(group):
            out_ref[e, :rows, :] = total[e * rows : (e + 1) * rows, :]
            out_ref[e, rows:, :] = sums

    return run(
        kernel,
        "project_grad_pack",
        (owners // group,),
        [x.spec((seqs, length, group * rows), lambda i, p: (0, 0, i)) for x in blocks] + [fixed(dqkv)],
        pl.BlockSpec((group, rows + extra, out_width), lambda i, p: (i, 0, 0)),
        kind_of((owners, rows + extra, out_width)),
        [*arrays(blocks), dqkv],
        prefetch=(places,),
        scratch=(pltpu.VMEM((extra, out_width), jnp.float32),),
        waits=waits,
        cost=2,
    )


def lay_columns(places, blocks, rows):
    total, out_width = blocks[0].shape
    part = out_width // 3
    ranks = len(blocks)
    width = part * ranks

    def kernel(place_ref, *refs):
        for q in range(ranks):
            at = pl.ds(pl.multiple_of(place_ref[q] * part, part), part)
            for k in range(3):
                block = wide(refs[q][:, k * part : (k + 1) * part])
                refs[ranks + k][:, at] = block[:rows, :]
                refs[ranks + 3 + k][:, at] = block[rows : rows + 8, :]

    shape, below = (rows, width), (8, width)
    return run(
        kernel,
        "lay_columns",
        (1,),
        [b.whole() for b in blocks],
        [pl.BlockSpec(shape, lambda i, p: (0, 0))] * 3 + [pl.BlockSpec(below, lambda i, p: (0, 0))] * 3,
        [kind_of(shape, jnp.float32)] * 3 + [kind_of(below, jnp.float32)] * 3,
        arrays(blocks),
        prefetch=(places,),
        cost=2,
    )


def lay_up(places, blocks, chips, part, waits=()):
    _, rows, _ = blocks[0].shape
    ranks = len(blocks)
    shape = (rows, 2 * chips * ranks * part)

    def kernel(place_ref, *refs):
        for q in range(ranks):
            for c in range(2):
                for z in range(chips):
                    at = pl.multiple_of(((z * 2 + c) * ranks + place_ref[q]) * part, part)
                    refs[ranks][:, pl.ds(at, part)] = wide(refs[q][c, :, z * part : (z + 1) * part])

    return run(
        kernel,
        "lay_up",
        (1,),
        [b.whole() for b in blocks],
        pl.BlockSpec(shape, lambda i, p: (0, 0)),
        kind_of(shape, jnp.float32),
        arrays(blocks),
        prefetch=(places,),
        waits=waits,
        cost=2,
    )


def lay_rows(places, blocks, waits=()):
    part, width = blocks[0].shape
    ranks = len(blocks)
    shape = (part * ranks, width)

    def kernel(place_ref, *refs):
        for q in range(ranks):
            refs[ranks][pl.ds(pl.multiple_of(place_ref[q] * part, part), part), :] = wide(refs[q][...])

    return run(
        kernel,
        "lay_rows",
        (1,),
        [b.whole() for b in blocks],
        pl.BlockSpec(shape, lambda i, p: (0, 0)),
        kind_of(shape, jnp.float32),
        arrays(blocks),
        prefetch=(places,),
        waits=waits,
        cost=2,
    )


def lay_chips(at, blocks, waits):
    rows, width = blocks[0].shape
    chips = len(blocks)

    def kernel(at_ref, *refs):
        for d in range(chips):
            refs[chips][at_ref[d]] = refs[d][...]

    shape = (chips, rows, width)
    return run(
        kernel,
        "lay_chips",
        (1,),
        [fixed(b) for b in blocks],
        pl.BlockSpec(shape, lambda i, p: (0, 0, 0)),
        kind_of(shape),
        blocks,
        prefetch=(at,),
        cost=100,
        waits=waits,
    )


def hold(array, waits):
    def kernel(from_ref, to_ref):
        to_ref[...] = from_ref[...]

    rank = array.ndim
    return run(
        kernel,
        "hold",
        (1,),
        [fixed(array)],
        pl.BlockSpec(array.shape, lambda i: (0,) * rank),
        kind_of(array.shape, array.dtype),
        [array],
        waits=waits,
    )


def split(at, own, size, waits=()):
    _, width = own.shape
    chips = at.shape[0]

    def kernel(at_ref, own_ref, *outs):
        for d in range(chips):
            outs[d][...] = own_ref[pl.ds(pl.multiple_of(at_ref[d] * size, size), size), :]

    return run(
        kernel,
        "split",
        (1,),
        [fixed(own)],
        [pl.BlockSpec((size, width), lambda i, p: (0, 0))] * chips,
        [kind_of((size, width))] * chips,
        [own],
        prefetch=(at,),
        cost=100,
        waits=waits,
    )


def tick(*waits, cost=10):
    def kernel(out_ref):
        out_ref[...] = jnp.zeros_like(out_ref)

    return run(
        kernel, "tick", (1,), [], pl.BlockSpec((8, 128), lambda i: (0, 0)), kind_of((8, 128), jnp.float32), [], waits=waits, cost=cost
    )


def total_rows(pieces, waits=()):
    def kernel(*refs):
        total = wide(refs[0][...])
        for ref in refs[1:-1]:
            total = total + wide(ref[...])
        refs[-1][...] = total.astype(jnp.bfloat16)

    shape = pieces[0].shape
    return run(
        kernel,
        "total_rows",
        (1,),
        [fixed(p) for p in pieces],
        pl.BlockSpec(shape, lambda i: (0, 0)),
        kind_of(shape),
        pieces,
        waits=waits,
    )


def total_halves(core, pieces, waits=()):
    rows, width = pieces[0].shape
    half = rows // 2

    def kernel(core_ref, *refs):
        for out_ref, of in ((refs[-2], core_ref[0]), (refs[-1], 1 - core_ref[0])):
            at = pl.ds(pl.multiple_of(of * half, half), half)
            total = wide(refs[0][at, :])
            for ref in refs[1:-2]:
                total = total + wide(ref[at, :])
            out_ref[...] = total.astype(jnp.bfloat16)

    return run(
        kernel,
        "total_halves",
        (1,),
        [fixed(p) for p in pieces],
        [pl.BlockSpec((half, width), lambda i, p: (0, 0))] * 2,
        [kind_of((half, width))] * 2,
        pieces,
        prefetch=(core,),
        waits=waits,
    )


def pair(core, own, other, waits=()):
    rows, width = own.shape

    def kernel(core_ref, own_ref, other_ref, out_ref):
        out_ref[core_ref[0]] = own_ref[...]
        out_ref[1 - core_ref[0]] = other_ref[...]

    shape = (2, rows, width)
    return run(
        kernel,
        "pair",
        (1,),
        [fixed(own), fixed(other)],
        pl.BlockSpec(shape, lambda i, p: (0, 0, 0)),
        kind_of(shape),
        [own, other],
        prefetch=(core,),
        waits=waits,
    )


def plan_rows(segments):
    b, t = segments.shape
    span, win = min(SPAN, t), min(WINDOW, t)
    spans = segments.reshape(b, t // span, span)
    place = jnp.arange(t, dtype=jnp.int32)
    low = jnp.min(jnp.where(segments[:, None, :] == spans[:, :, :1], place, t), axis=2)
    high = jnp.max(jnp.where(segments[:, None, :] == spans[:, :, -1:], place, -1), axis=2)
    start = jnp.minimum(low // ALIGN * ALIGN, t - win)
    fits = jnp.all(high < start + win, axis=1)
    single = jnp.all(segments == segments[:, :1], axis=1)
    kind = jnp.where(single, 0, jnp.where(fits, 1, 2))
    return kind.astype(jnp.int32), start.astype(jnp.int32)

def aligned(start, size):
    return start if isinstance(start, int) else pl.multiple_of(start, size)


def bias_of(col_ref, keys, row_ref, queries):
    return jnp.where(col_ref[0, keys, :] == row_ref[0, :, queries], 0.0, MASKED)


def over(count, body):
    if count == 1:
        body(0)
    else:
        lax.fori_loop(0, count, lambda g, c: (body(g), c)[1], 0, unroll=UNROLL)


def fwd_kernel(heads, kind_ref, start_ref, place_ref, qkv_ref, row_ref, col_ref, ctx_ref, lse_ref, *part_refs):
    b = pl.program_id(0)
    t = qkv_ref.shape[1]
    hw = heads * HEAD_DIM
    span, win = min(SPAN, t), min(WINDOW, t)
    kind = kind_ref[b]

    group = min(2, heads)
    lanes = group * HEAD_DIM

    def attend(g, rows, keys, bias):
        def piece(which):
            return pl.ds(aligned(which * hw + g * lanes, lanes), lanes)

        query, key, value = (qkv_ref[0, r, piece(w)] for w, r in enumerate((rows, keys, keys)))
        parts = []
        for e in range(group):
            at = slice(e * HEAD_DIM, (e + 1) * HEAD_DIM)
            s = dot(key[:, at], query[:, at], 1, 1)
            if bias is not None:
                s = s + bias
            m = jnp.max(s, axis=0, keepdims=True)
            p = jnp.exp(s - m)
            total = jnp.sum(p, axis=0, keepdims=True)
            parts.append(dot(value[:, at], p.astype(jnp.bfloat16), 0, 0) / total)
            lse_ref[0, pl.ds(g * group + e, 1), rows] = m + jnp.log(total)
        ctx_ref[0, rows, piece(0)] = jnp.transpose(jnp.concatenate(parts, axis=0)).astype(jnp.bfloat16)

    def each(size, masked, keys_of):
        size = min(size, t)

        def body(i, _):
            rows = pl.ds(pl.multiple_of(i * size, size), size)
            bias = bias_of(col_ref, keys_of(i), row_ref, rows) if masked else None
            over(heads // group, lambda g: attend(g, rows, keys_of(i), bias))
            return 0

        lax.fori_loop(0, t // size, body, 0)

    @pl.when(kind == 0)
    def _():
        each(FORWARD_SPAN, False, lambda i: pl.ds(0, t))

    @pl.when(kind == 2)
    def _():
        each(span, True, lambda i: pl.ds(0, t))

    @pl.when(kind == 1)
    def _():
        each(span, True, lambda i: pl.ds(pl.multiple_of(start_ref[b, i], ALIGN), win))

    length = part_refs[0].shape[1]
    for q, part_ref in enumerate(part_refs):
        part_ref[0] = ctx_ref[0, pl.ds(pl.multiple_of(place_ref[q] * length, length), length), :]


def attention(qkv, segments, kind, start, places, waits):
    ranks = places.shape[0]
    b, t, w = qkv.shape
    hw = w // 3
    heads = hw // HEAD_DIM

    def at(i, *_):
        return (i, 0, 0)

    return run(
        functools.partial(fwd_kernel, heads),
        "attention_forward",
        (b,),
        [pl.BlockSpec((1, t, w), at), pl.BlockSpec((1, 1, t), at), pl.BlockSpec((1, t, 1), at)],
        [pl.BlockSpec((1, t, hw), at), pl.BlockSpec((1, heads, t), at)]
        + [pl.BlockSpec((1, t // ranks, hw), at)] * ranks,
        [kind_of((b, t, hw)), kind_of((b, heads, t), jnp.float32)] + [kind_of((b, t // ranks, hw))] * ranks,
        [qkv, segments[:, None, :], segments[:, :, None]],
        prefetch=(kind, start, places),
        waits=waits,
        cost=100,
    )

def bwd_kernel(heads, b, kind_ref, start_ref, qkv_ref, do_ref, ctx_ref, lse_ref, row_ref, col_ref, out_ref, dq_acc, delta_ref):
    t = qkv_ref.shape[1]
    hw = heads * HEAD_DIM
    span, win = min(SPAN, t), min(WINDOW, t)
    kind = kind_ref[b]

    def lanes(h, which=0):
        lo = which * hw + h * HEAD_DIM
        return slice(lo, lo + HEAD_DIM)

    prod = do_ref[0].astype(jnp.float32) * ctx_ref[0].astype(jnp.float32)
    high = prod.astype(jnp.bfloat16)
    rest = (prod - high.astype(jnp.float32)).astype(jnp.bfloat16)
    head = lax.broadcasted_iota(jnp.int32, (delta_ref.shape[0], hw), 0)
    of = lax.broadcasted_iota(jnp.int32, (delta_ref.shape[0], hw), 1) // HEAD_DIM
    ones = (head == of).astype(jnp.bfloat16)
    delta_ref[...] = dot(ones, high, 1, 1) + dot(ones, rest, 1, 1)

    group = min(2, heads)
    lanes = group * HEAD_DIM

    def back(g, keys, queries, bias):
        def piece(which):
            return pl.ds(aligned(which * hw + g * lanes, lanes), lanes)

        query, key, value = (qkv_ref[0, r, piece(w)] for w, r in enumerate((queries, keys, keys)))
        grad = do_ref[0, queries, piece(0)]
        key_grads, value_grads = [], []
        for e in range(group):
            at = slice(e * HEAD_DIM, (e + 1) * HEAD_DIM)
            row = pl.ds(g * group + e, 1)
            s = dot(key[:, at], query[:, at], 1, 1)
            if bias is not None:
                s = s + bias
            p = jnp.exp(s - lse_ref[0, row, queries])
            dp = dot(value[:, at], grad[:, at], 1, 1)
            ds = (p * (dp - delta_ref[row, queries])).astype(jnp.bfloat16)
            value_grads.append(dot(p.astype(jnp.bfloat16), grad[:, at], 1, 0))
            key_grads.append(dot(ds, query[:, at], 1, 0))
            into = pl.ds(aligned(g * lanes + e * HEAD_DIM, HEAD_DIM), HEAD_DIM)
            dq_acc[into, queries] += dot(key[:, at], ds, 0, 0)
        out_ref[0, keys, piece(1)] = jnp.concatenate(key_grads, axis=1).astype(jnp.bfloat16)
        out_ref[0, keys, piece(2)] = jnp.concatenate(value_grads, axis=1).astype(jnp.bfloat16)

    dq_acc[...] = jnp.zeros_like(dq_acc)

    def each(size, masked, queries_of):
        size = min(size, t)

        def body(j, _):
            keys = pl.ds(pl.multiple_of(j * size, size), size)
            bias = bias_of(col_ref, keys, row_ref, queries_of(j)) if masked else None
            over(heads // group, lambda g: back(g, keys, queries_of(j), bias))
            return 0

        lax.fori_loop(0, t // size, body, 0)

    @pl.when(kind == 0)
    def _():
        each(BACKWARD_SPAN, False, lambda j: pl.ds(0, t))

    @pl.when(kind == 2)
    def _():
        each(span, True, lambda j: pl.ds(0, t))

    @pl.when(kind == 1)
    def _():
        each(span, True, lambda j: pl.ds(pl.multiple_of(start_ref[b, j], ALIGN), win))

    out_ref[0, :, :hw] = (jnp.transpose(dq_acc[...]) * (HEAD_DIM**-0.5)).astype(jnp.bfloat16)


def attention_back(qkv, dparts, ctx, lse, segments, kind, start, places, which, buffer, waits):
    b, t, w = qkv.shape
    hw = w // 3
    heads = hw // HEAD_DIM
    ranks = len(dparts)
    length = t // ranks

    def kernel(kind_ref, start_ref, place_ref, qkv_ref, *refs):
        grad_ref = refs[-1]
        for q in range(ranks):
            grad_ref[0, pl.ds(pl.multiple_of(place_ref[q] * length, length), length), :] = refs[q][0]
        bwd_kernel(heads, which, kind_ref, start_ref, qkv_ref, grad_ref, *refs[ranks : ranks + 4], *refs[-4:-1])

    def at(i, *_):
        return (which, 0, 0)

    ins = [pl.BlockSpec((1, t, w), at)] + [pl.BlockSpec((1, length, hw), at)] * ranks
    ins += [
        pl.BlockSpec((1, t, hw), at),
        pl.BlockSpec((1, heads, t), at),
        pl.BlockSpec((1, 1, t), at),
        pl.BlockSpec((1, t, 1), at),
    ]
    operands = [qkv, *dparts, ctx, lse, segments[:, None, :], segments[:, :, None]]
    alias = None
    if buffer is not None:
        ins.append(pl.BlockSpec(memory_space=pl.ANY))
        operands.append(buffer)
        alias = {3 + len(ins) - 1: 0}
    return run(
        kernel,
        "attention_backward",
        (1,),
        ins,
        pl.BlockSpec((1, t, w), at),
        kind_of((b, t, w)),
        operands,
        prefetch=(kind, start, places),
        scratch=(
            pltpu.VMEM((hw, t), jnp.float32),
            pltpu.VMEM((-(-heads // 8) * 8, t), jnp.float32),
            pltpu.VMEM((1, t, hw), jnp.bfloat16),
        ),
        alias=alias,
        waits=waits,
    )


AXES = ("seq", "z", "core")
ROWS = ("z", "core")
EXTRA = 16


def low(tensor):
    return tensor.astype(jnp.bfloat16)


class Ring:
    def __init__(self):
        self.ranks = lax.axis_size("seq")
        self.chips = lax.axis_size("z")
        self.index = lax.axis_index("seq")
        self.core = lax.axis_index("core")
        self.count = self.ranks.bit_length() - 1

    def bit(self, k, core):
        if self.count == 2 and core == 1:
            k = 1 - k
        return 1 << k

    def offset(self, q, core):
        return sum(self.bit(k, core) for k in range(self.count) if q >> k & 1)

    def place(self, q):
        return jnp.bitwise_xor(self.index, jnp.where(self.core == 0, self.offset(q, 0), self.offset(q, 1)))

    def hop(self, block, k):
        pairs = []
        for s in range(self.ranks):
            for z in range(self.chips):
                for c in range(2):
                    to = s ^ self.bit(k, c)
                    pairs.append(((s * self.chips + z) * 2 + c, (to * self.chips + z) * 2 + c))
        return lax.ppermute(block, AXES, pairs)

    def gather(self, block):
        blocks = [block]
        for k in range(self.count):
            blocks = blocks + [self.hop(b, k) for b in blocks]
        return [View(b) for b in blocks]

    def exchange(self, blocks):
        out = [blocks[0]]
        for q in range(1, self.ranks):
            pairs = []
            for s in range(self.ranks):
                for z in range(self.chips):
                    for c in range(2):
                        to = s ^ self.offset(q, c)
                        pairs.append(((s * self.chips + z) * 2 + c, (to * self.chips + z) * 2 + c))
            out.append(lax.ppermute(blocks[q], AXES, pairs))
        return out

    def shift(self, block, d):
        return lax.ppermute(block, "z", [(z, (z + d) % self.chips) for z in range(self.chips)])


def swap(block):
    return lax.ppermute(block, "core", [(0, 1), (1, 0)])


def put(blocks, ring, axis):
    shape = list(blocks[0].shape)
    size = shape[axis]
    shape[axis] = size * len(blocks)
    whole = jnp.zeros(shape, blocks[0].dtype)
    for q, block in enumerate(blocks):
        whole = lax.dynamic_update_slice_in_dim(whole, block, ring.place(q) * size, axis)
    return whole


def local(
    hidden_in,
    segments,
    q_weight,
    k_weight,
    v_weight,
    out_weight,
    q_bias,
    v_bias,
    out_bias,
    up_weight,
    up_bias,
    down_weight,
    down_bias,
    norm1_gain,
    norm1_bias,
    norm2_gain,
    norm2_bias,
    out_grad,
):
    ring = Ring()
    here, core = ring.index, ring.core
    ranks, chips = ring.ranks, ring.chips
    owners = chips * 2
    z_index = lax.axis_index("z")
    owner = z_index * 2 + core
    seqs, length, width = hidden_in.shape
    full = length * ranks
    head_width = width // ranks
    out_width = 3 * head_width
    rows = width // owners
    units = down_weight.shape[0]
    part = units // ranks
    count = seqs * length
    score_scale = HEAD_DIM ** (-0.5)
    first_core = core == 0
    core_index = core.astype(jnp.int32).reshape(1)
    places = jnp.stack([ring.place(q) for q in range(ranks)]).astype(jnp.int32)
    blocks = range(ranks)

    heads_at = here * head_width
    mine = jnp.concatenate(
        [lax.dynamic_slice_in_dim(w, heads_at, head_width, 1) for w in (q_weight, k_weight, v_weight)], axis=1
    )
    vectors = (q_bias, v_bias, out_bias, down_bias, norm1_gain, norm1_bias, norm2_gain, norm2_bias)
    known = len(vectors)
    packed = jnp.pad(
        up_bias.reshape(-1, rows), ((known, EXTRA - known - units // rows), (0, out_width - rows))
    )
    for i, vector in enumerate(vectors):
        packed = packed + jnp.pad(vector[None], ((i, EXTRA - 1 - i), (0, out_width - rows)))
    mine = jnp.concatenate([mine, packed], axis=0)

    def up_columns(of_core):
        return jnp.concatenate(
            [
                lax.dynamic_slice_in_dim(up_weight, ((z * 2 + of_core) * ranks + here) * part, part, 1)
                for z in range(chips)
            ],
            axis=1,
        )

    own_up, other_up = up_columns(core), swap(up_columns(1 - core))
    up_rows = jnp.concatenate(
        [jnp.where(first_core, own_up, other_up), jnp.where(first_core, other_up, own_up)], axis=0
    )
    hidden = ring.gather(hidden_in)
    shifts = jnp.stack([(z_index - d) % chips for d in range(chips)]).astype(jnp.int32)
    up_block = lay_chips(shifts, [up_rows] + [ring.shift(up_rows, d) for d in range(1, chips)], ())
    up_block = hold(up_block.reshape(width, chips * part), (hidden[-1].array,))
    gathered = lax.all_gather(mine, ROWS, axis=0)
    down_rows = hold(lax.dynamic_slice_in_dim(down_weight, here * part, part, 0), (gathered,))
    down_block = lax.all_gather(down_rows, "z", axis=0, tiled=True)
    output_weight = lax.all_gather(hold(out_weight, (down_rows,)), ROWS, axis=0, tiled=True)
    up_weights = ring.gather(up_block)
    kind, start = plan_rows(segments)
    keep = wide(lax.dynamic_slice_in_dim(segments, here * length, length, 1) != 0)[:, :, None]

    qkv_weight = gathered[:, :rows].reshape(width, out_width)
    gathered = wide(gathered[:, rows:, :rows])
    vectors = gathered.transpose(1, 0, 2).reshape(EXTRA, width)
    biases = lax.dynamic_slice_in_dim(vectors, heads_at, head_width, 1)
    qkv_bias = jnp.concatenate([biases[0], jnp.zeros_like(biases[0]), biases[1]])[None]
    scales = jnp.where(jnp.arange(out_width) < head_width, score_scale, 1.0)[None]
    qkv = project(places, hidden, qkv_weight, qkv_bias, scales)
    contexts, log_totals, *context_parts = attention(
        qkv, segments, kind, start, places, (up_block,)
    )
    context_parts = ring.exchange(context_parts)
    down_weights = ring.gather(hold(down_block, (*context_parts[1:], *arrays(up_weights[1:3]))))
    sums_one, first_low = out_norm(
        places,
        context_parts,
        output_weight,
        hidden_in,
        vectors,
    )

    first_low = first_low.reshape(count, width)
    first_other = swap(first_low)
    upper_bias = gathered[:, known : known + units // rows].reshape(chips, 2, ranks, part)
    upper_bias = lax.dynamic_index_in_dim(upper_bias, core, 1, False)
    upper_bias = [
        lax.dynamic_index_in_dim(upper_bias, ring.place(q), 1, False).reshape(1, -1) for q in blocks
    ]
    actives, slopes = up_forward(
        first_low, first_other, up_weights, upper_bias, arrays(down_weights[1:2])
    )
    mixed_other = down_forward(actives, down_weights, count, count, jnp.bfloat16)
    mixed = down_forward(actives, down_weights, 0, count, jnp.bfloat16, (mixed_other,))
    layer_out, dmixed, totals_two = norm_two(mixed, swap(mixed_other), sums_one, vectors, out_grad, keep)

    dmixed = dmixed.reshape(count, width)
    dmixed_other = swap(dmixed)
    none = [()] * ranks
    odd, even = [q for q in blocks if q % 2], [q for q in blocks if q % 2 == 0]
    down_sent = down_grad([actives[q] for q in odd], dmixed, dmixed_other, none)
    duppers, up_sums, dfirst, dfirst_other = ffn_back(
        dmixed, dmixed_other, slopes, down_weights, up_weights, (tick(down_sent),)
    )
    dfirst_other = swap(dfirst_other)
    dbranch, dcontexts, totals_one = norm_one_back(
        places, dfirst, dfirst_other, dmixed, sums_one, vectors, output_weight, head_width, (tick(duppers[0], cost=10),)
    )
    dcontexts = ring.exchange(dcontexts)

    def spread(made, sent):
        came = {q: [] for q in blocks}
        for k in range(ring.count):
            step = 1 << k
            got = ring.hop(sent, k)
            for i, q in enumerate(range(0, ranks, 2 * step)):
                came[q].append(View(got, i))
            if k + 1 < ring.count:
                turn = [q + 2 * step for q in range(0, ranks, 4 * step)]
                sent = made(turn, [came[q] for q in turn])
        return came[0], sent

    def down_made(turn, addends):
        return down_grad([actives[q] for q in turn], dmixed, dmixed_other, addends, (tick(dbranch),))

    down_came, down_hop = spread(down_made, down_sent)
    up_sent = up_grad([duppers[q] for q in odd], first_low, first_other, none, (down_hop,))

    extra = -(-(6 + ranks) // EXTRA) * EXTRA
    up_totals = put([up_sums[q : q + 1] for q in blocks], ring, 0).reshape(ranks, chips, 1, part)
    up_totals = jnp.where(jnp.arange(2)[None, None, :, None] == core, up_totals, 0.0)
    up_totals = jnp.pad(up_totals, ((0, 0), (0, 0), (0, 0), (0, rows - part))).reshape(ranks, width)
    small = jnp.concatenate(
        [totals_two[:3], totals_one[:3], up_totals, jnp.zeros((extra - 6 - ranks, width), jnp.float32)], axis=0
    )
    out_pack = out_grad_pack(places, context_parts, dbranch, low(small), owners, (up_sent,))
    out_shard = lax.psum_scatter(out_pack.reshape(-1, width), ROWS, scatter_dimension=0, tiled=True)

    common = (qkv, dcontexts, contexts, log_totals, segments, kind, start, places)
    dqkv = attention_back(*common, 0, None, (out_pack,))

    def up_made(turn, addends):
        return up_grad([duppers[q] for q in turn], first_low, first_other, addends, (down_pieces[0],))

    down_own = down_grad([actives[0]], dmixed, dmixed_other, [down_came], (dqkv,))[0]
    ahead = jnp.stack([(z_index + d) % chips for d in range(chips)]).astype(jnp.int32)
    down_pieces = split(ahead, down_own, part)
    up_came, up_hop = spread(up_made, up_sent)
    for which in range(1, seqs):
        dqkv = attention_back(*common, which, dqkv, (up_hop,))

    def shifted(pieces):
        return [pieces[0]] + [ring.shift(pieces[d], d) for d in range(1, chips)]

    def hidden_made(turn, addends, waits=()):
        return hidden_grad(places, dqkv, qkv_weight, length, turn, addends, jnp.bfloat16, waits or (up_pair,))

    down_shard = total_rows(shifted(down_pieces), (dqkv, up_came[-1].array))
    down_parts = ring.gather(down_shard)
    up_own = up_grad([duppers[0]], first_low, first_other, [up_came], (down_shard,))[0]
    up_pieces = split(ahead, up_own, 2 * rows)
    hidden_sent = hidden_made(odd, none, (up_pieces[0], *arrays(down_parts[1:2])))
    qkv_pack = project_grad_pack(
        places, hidden, dqkv, owners, EXTRA, (hidden_sent, out_shard, *arrays(down_parts[2:]))
    )
    qkv_shard = lax.psum_scatter(qkv_pack.reshape(-1, out_width), ROWS, scatter_dimension=0, tiled=True)
    out_sum = [wide(out_shard)]
    for k in range(ring.count):
        out_sent = low(out_sum[-1])
        out_sum.append(out_sum[-1] + wide(ring.hop(out_sent, k)))
    keep_part, take_part = total_halves(core_index, shifted(up_pieces), (qkv_pack,))
    down_weight_grad = lay_rows(places, down_parts, (keep_part,))
    up_pair = pair(core_index, keep_part, swap(take_part), (down_weight_grad,))
    hidden_came, hidden_hop = spread(hidden_made, hidden_sent)
    input_grad = hidden_grad(
        places, dqkv, qkv_weight, length, [0], [[View(dbranch)] + hidden_came], jnp.float32
    )[0]

    up_parts = ring.gather(up_pair)
    qkv_parts = ring.gather(qkv_shard)
    out_pack = out_sum[-1]
    if part % 128 == 0:
        up_weight_grad = lay_up(places, up_parts, chips, part, (hidden_hop,))
    else:
        up_weight_grad = wide(put([b.value()[None] for b in up_parts], ring, 0))
        up_weight_grad = (
            up_weight_grad.reshape(ranks, 2, rows, chips, part).transpose(2, 3, 1, 0, 4).reshape(rows, owners * units)
        )
    if head_width % 128 == 0:
        *qkv_grads, q_sums, _, v_sums = lay_columns(places, qkv_parts, rows)
    else:
        laid = wide(put([b.value()[None] for b in qkv_parts], ring, 0))
        laid = laid.reshape(ranks, rows + EXTRA, 3, head_width).transpose(2, 1, 0, 3).reshape(3, -1, width)
        qkv_grads, q_sums, v_sums = [g[:rows] for g in laid], laid[0, rows:], laid[2, rows:]

    def mine_of(sums):
        return lax.dynamic_slice_in_dim(sums[0], owner * rows, rows, 0)

    small = out_pack[rows:, :rows]
    up_bias_grad = small[6 : 6 + ranks, :part].reshape(-1)
    return (
        layer_out,
        input_grad,
        *qkv_grads,
        out_pack[:rows],
        mine_of(q_sums),
        mine_of(v_sums),
        small[3],
        up_weight_grad,
        up_bias_grad,
        down_weight_grad,
        small[0],
        small[4],
        small[5],
        small[1],
        small[2],
    )


def solution(mesh):
    ranks, owners = mesh.shape["seq"], mesh.shape["fsdp"]
    grid = Mesh(mesh.devices.reshape(ranks, owners // 2, 2), AXES)
    tokens, matrix, vector = P(ROWS, "seq", None), P(ROWS, None), P(ROWS)
    return jax.shard_map(
        local,
        mesh=grid,
        in_specs=(
            tokens,
            matrix,
            matrix,
            matrix,
            matrix,
            matrix,
            vector,
            vector,
            vector,
            matrix,
            vector,
            matrix,
            vector,
            vector,
            vector,
            vector,
            vector,
            tokens,
        ),
        out_specs=(
            tokens,
            tokens,
            matrix,
            matrix,
            matrix,
            matrix,
            vector,
            vector,
            vector,
            matrix,
            vector,
            matrix,
            vector,
            vector,
            vector,
            vector,
            vector,
        ),
        check_vma=False,
    )
```

```python
import functools

import jax
import jax.numpy as jnp
from jax import lax
from jax.experimental import pallas as pl
from jax.experimental.pallas import tpu as pltpu
from jax.sharding import Mesh
from jax.sharding import PartitionSpec as P

HEAD_DIM = 64
SPAN = 256
ALIGN = 128
WINDOW = 512
FORWARD_SPAN = 1024
BACKWARD_SPAN = 512
UNROLL = True
MASKED = -1e30


def dot(a,b,ca,cb):
    return lax.dot_general(a,b,(((ca,),(cb,)),((),())),preferred_element_type=jnp.float32)


TILE = 256


def run(kernel, name, grid, ins, outs, shapes, operands, prefetch=(), scratch=(), alias=None, waits=(), cost=10):
    known = len(prefetch) + len(ins)

    def waiting(*refs):
        kernel(*refs[:known], *refs[known + len(waits) :])

    ins = list(ins) + [pl.BlockSpec(memory_space=pl.ANY)] * len(waits)
    operands = list(operands) + list(waits)
    return pl.pallas_call(
        waiting,
        grid_spec=pltpu.PrefetchScalarGridSpec(
            num_scalar_prefetch=len(prefetch), grid=grid, in_specs=ins, out_specs=outs, scratch_shapes=scratch
        ),
        out_shape=shapes,
        input_output_aliases=alias or {},
        compiler_params=pltpu.CompilerParams(vmem_limit_bytes=50 << 20),
        cost_estimate=pl.CostEstimate(flops=cost * 3000000000, bytes_accessed=1000, transcendentals=0),
        name=name,
    )(*prefetch, *operands)


def fixed(array):
    rank = array.ndim
    return pl.BlockSpec(array.shape, lambda *_: (0,) * rank, pipeline_mode=pl.Buffered(buffer_count=1))


class View:
    def __init__(self, array, i=None):
        self.array, self.i = array, i
        self.shape = array.shape if i is None else array.shape[1:]

    def spec(self, block, place):
        i = self.i
        if i is None:
            return pl.BlockSpec(block, place)
        return pl.BlockSpec((None,) + tuple(block), lambda *a: (i,) + tuple(place(*a)))

    def whole(self):
        rank, i = len(self.shape), self.i
        once = pl.Buffered(buffer_count=1)
        if i is None:
            return pl.BlockSpec(self.shape, lambda *_: (0,) * rank, pipeline_mode=once)
        return pl.BlockSpec((None,) + tuple(self.shape), lambda *_: (i,) + (0,) * rank, pipeline_mode=once)

    def value(self):
        return self.array if self.i is None else self.array[self.i]


def arrays(views):
    return [v.array for v in views]


def kind_of(shape, dtype=jnp.bfloat16):
    return jax.ShapeDtypeStruct(tuple(shape), dtype)


def wide(tensor):
    return tensor.astype(jnp.float32)


def standardize(values):
    center = jnp.mean(values, axis=1, keepdims=True)
    offset = values - center
    inverse = lax.rsqrt(jnp.mean(offset * offset, axis=1, keepdims=True) + 1e-05)
    return offset * inverse, inverse


def standardize_back(upstream, normed, inverse, gain):
    scaled = upstream * gain
    return inverse * (
        scaled
        - jnp.mean(scaled, axis=1, keepdims=True)
        - normed * jnp.mean(scaled * normed, axis=1, keepdims=True)
    )


def column_sum(values):
    return jnp.sum(values, axis=0, keepdims=True)


OUT_BIAS, DOWN_BIAS, GAIN_ONE, SHIFT_ONE, GAIN_TWO, SHIFT_TWO = 2, 3, 4, 5, 6, 7


def project(places, blocks, weight, bias, scale):
    seqs, length, width = blocks[0].shape
    ranks = len(blocks)
    owners, _, out_width = weight.shape
    rows = width // owners

    def kernel(place_ref, weight_ref, bias_ref, scale_ref, *refs):
        for q in range(ranks):

            @pl.when(pl.program_id(0) // seqs == q)
            def _(q=q):
                whole = weight_ref[:, :rows, :].reshape(width, out_width)
                product = dot(refs[q][0], whole, 1, 0) + bias_ref[...]
                refs[ranks][0] = (product * scale_ref[...]).astype(jnp.bfloat16)

    def source(q):
        return lambda i, p: (jnp.clip(i - q * seqs, 0, seqs - 1), 0, 0)

    return run(
        kernel,
        "project",
        (ranks * seqs,),
        [fixed(weight), fixed(bias), fixed(scale)]
        + [blocks[q].spec((1, length, width), source(q)) for q in range(ranks)],
        pl.BlockSpec((1, length, out_width), lambda i, p: (i % seqs, p[i // seqs], 0)),
        kind_of((seqs, length * ranks, out_width)),
        [weight, bias, scale, *arrays(blocks)],
        prefetch=(places,),
    )


def out_norm(places, contexts, weight, hidden, vectors, waits=()):
    seqs, length, width = hidden.shape
    ranks = len(contexts)
    part = contexts[0].shape[2]

    def kernel(place_ref, *refs):
        weight_ref, hidden_ref, vector_ref, sum_ref, first_ref = refs[ranks:]
        total = wide(hidden_ref[0]) + vector_ref[OUT_BIAS : OUT_BIAS + 1, :]
        for q in range(ranks):
            rows = pl.ds(pl.multiple_of(place_ref[q] * part, part), part)
            total = total + dot(refs[q][0], weight_ref[rows, :], 1, 0)
        total = total.astype(jnp.bfloat16)
        sum_ref[0] = total
        normed, _ = standardize(wide(total))
        first = normed * vector_ref[GAIN_ONE : GAIN_ONE + 1, :] + vector_ref[SHIFT_ONE : SHIFT_ONE + 1, :]
        first_ref[0] = first.astype(jnp.bfloat16)

    tokens = pl.BlockSpec((1, length, width), lambda b, p: (b, 0, 0))
    return run(
        kernel,
        "out_norm",
        (seqs,),
        [pl.BlockSpec((1, length, part), lambda b, p: (b, 0, 0))] * ranks + [fixed(weight), tokens, fixed(vectors)],
        [tokens, tokens],
        [kind_of(hidden.shape), kind_of(hidden.shape)],
        [*contexts, weight, hidden, vectors],
        prefetch=(places,),
        waits=waits,
    )


def up_forward(own, other, weights, biases, waits=()):
    count, width = own.shape
    units = weights[0].shape[1]
    blocks = len(weights)
    tile = min(TILE, count)
    half = count // tile

    def kernel(own_ref, other_ref, *refs):
        def body(tokens):
            uppers = [dot(tokens, refs[q][...], 1, 0) for q in range(blocks)]
            for q in range(blocks):
                upper = uppers[q] + refs[blocks + q][...]
                tail = 0.5 * (1.0 + lax.erf(upper * 0.7071067811865476))
                refs[2 * blocks + q][...] = (upper * tail).astype(jnp.bfloat16)
                bell = jnp.exp(-0.5 * upper * upper) * 0.3989422804014327
                refs[3 * blocks + q][...] = (tail + upper * bell).astype(jnp.bfloat16)

        @pl.when(pl.program_id(0) < half)
        def _():
            body(own_ref[...])

        @pl.when(pl.program_id(0) >= half)
        def _():
            body(other_ref[...])

    outs = run(
        kernel,
        "up_forward",
        (2 * half,),
        [
            pl.BlockSpec((tile, width), lambda i: (jnp.minimum(i, half - 1), 0)),
            pl.BlockSpec((tile, width), lambda i: (jnp.maximum(i - half, 0), 0)),
        ]
        + [w.whole() for w in weights]
        + [fixed(b) for b in biases],
        [pl.BlockSpec((tile, units), lambda i: (i, 0))] * (2 * blocks),
        [kind_of((2 * count, units))] * (2 * blocks),
        [own, other, *arrays(weights), *biases],
        waits=waits,
    )
    return list(outs[:blocks]), list(outs[blocks:])


def down_forward(actives, weights, first, count, dtype, waits=()):
    blocks = len(actives)
    units, width = weights[0].shape
    tile = min(TILE, count)

    def kernel(*refs):
        total = dot(refs[0][...], refs[blocks][...], 1, 0)
        for q in range(1, blocks):
            total = total + dot(refs[q][...], refs[blocks + q][...], 1, 0)
        refs[-1][...] = total.astype(dtype)

    return run(
        kernel,
        "down_forward",
        (count // tile,),
        [pl.BlockSpec((tile, units), lambda i: (i + first // tile, 0))] * blocks + [w.whole() for w in weights],
        pl.BlockSpec((tile, width), lambda i: (i, 0)),
        kind_of((count, width), dtype),
        [*actives, *arrays(weights)],
        waits=waits,
    )


def norm_two(mixed, mixed_other, sums_one, vectors, out_grad, keep):
    seqs, length, width = sums_one.shape

    def kernel(mixed_ref, other_ref, sum_ref, vector_ref, grad_ref, keep_ref, out_ref, dmixed_ref, total_ref):
        @pl.when(pl.program_id(0) == 0)
        def _():
            total_ref[...] = jnp.zeros_like(total_ref)

        def vector(i):
            return vector_ref[i : i + 1, :]

        normed, _ = standardize(wide(sum_ref[0]))
        first = normed * vector(GAIN_ONE) + vector(SHIFT_ONE)
        mixed = wide(mixed_ref[0]) + wide(other_ref[0]) + vector(DOWN_BIAS)
        normed, inverse = standardize(first + mixed)
        out_ref[0] = (normed * vector(GAIN_TWO) + vector(SHIFT_TWO)).astype(jnp.bfloat16)
        cot = wide(grad_ref[0]) * keep_ref[0]
        dmixed = standardize_back(cot, normed, inverse, vector(GAIN_TWO)).astype(jnp.bfloat16)
        dmixed_ref[0] = dmixed
        total_ref[0:1, :] += column_sum(wide(dmixed))
        total_ref[1:2, :] += column_sum(cot * normed)
        total_ref[2:3, :] += column_sum(cot)

    tokens = pl.BlockSpec((1, length, width), lambda b: (b, 0, 0))
    shape = sums_one.shape
    return run(
        kernel,
        "norm_two",
        (seqs,),
        [tokens, tokens, tokens, fixed(vectors), tokens, pl.BlockSpec((1, length, 1), lambda b: (b, 0, 0))],
        [tokens, tokens, pl.BlockSpec((8, width), lambda b: (0, 0))],
        [kind_of(shape), kind_of(shape), kind_of((8, width), jnp.float32)],
        [mixed.reshape(shape), mixed_other.reshape(shape), sums_one, vectors, out_grad, keep],
    )


def ffn_back(own, other, slopes, downs, ups, waits=()):
    blocks = len(slopes)
    count, width = own.shape
    units = slopes[0].shape[1]
    tile = min(TILE, count)
    half = count // tile

    def kernel(own_ref, other_ref, *refs):
        slope_refs, down_refs, up_refs = refs[:blocks], refs[blocks : 2 * blocks], refs[2 * blocks : 3 * blocks]
        upper_refs, total_ref, here_ref, there_ref = refs[3 * blocks : 4 * blocks], refs[-3], refs[-2], refs[-1]
        step = pl.program_id(0)

        @pl.when(step == 0)
        def _():
            total_ref[...] = jnp.zeros_like(total_ref)

        def body(grad):
            back = [dot(grad, down_refs[q][...], 1, 1) for q in range(blocks)]
            total = 0.0
            for q in range(blocks):
                upper = back[q] * wide(slope_refs[q][...])
                total_ref[q : q + 1, :] += column_sum(upper)
                upper_refs[q][...] = upper.astype(jnp.bfloat16)
            for q in range(blocks):
                total = total + dot(upper_refs[q][...], up_refs[q][...], 1, 1)
            return total

        @pl.when(step < half)
        def _():
            there_ref[...] = body(other_ref[...]).astype(jnp.bfloat16)

        @pl.when(step >= half)
        def _():
            here_ref[...] = body(own_ref[...]).astype(jnp.bfloat16)

    def early(i):
        return (jnp.minimum(i, half - 1), 0)

    def late(i):
        return (jnp.maximum(i - half, 0), 0)

    def both(i):
        return ((i + half) % (2 * half), 0)

    outs = run(
        kernel,
        "feed_forward_back",
        (2 * half,),
        [pl.BlockSpec((tile, width), late), pl.BlockSpec((tile, width), early)]
        + [pl.BlockSpec((tile, units), both)] * blocks
        + [w.whole() for w in (*downs, *ups)],
        [pl.BlockSpec((tile, units), both)] * blocks
        + [
            pl.BlockSpec((max(8, blocks), units), lambda i: (0, 0)),
            pl.BlockSpec((tile, width), late),
            pl.BlockSpec((tile, width), early),
        ],
        [kind_of((2 * count, units))] * blocks
        + [
            kind_of((max(8, blocks), units), jnp.float32),
            kind_of((count, width)),
            kind_of((count, width)),
        ],
        [own, other, *slopes, *arrays(downs), *arrays(ups)],
        waits=waits,
    )
    return list(outs[:blocks]), outs[blocks], outs[blocks + 1], outs[blocks + 2]


def down_grad(actives, own, other, addends, waits=()):
    count, width = own.shape
    units = actives[0].shape[1]
    tile = min(TILE, units)
    blocks = len(actives)
    spread = [(q, a) for q in range(blocks) for a in addends[q]]

    def kernel(own_ref, other_ref, *refs):
        for q in range(blocks):
            total = dot(refs[q][:count, :], own_ref[...], 0, 0) + dot(refs[q][count:, :], other_ref[...], 0, 0)
            for j, (of, _) in enumerate(spread):
                if of == q:
                    total = total + wide(refs[blocks + j][...])
            refs[-1][q] = total.astype(jnp.bfloat16)

    return run(
        kernel,
        "down_grad",
        (units // tile,),
        [fixed(own), fixed(other)]
        + [pl.BlockSpec((2 * count, tile), lambda i: (0, i))] * blocks
        + [a.spec((tile, width), lambda i: (i, 0)) for _, a in spread],
        pl.BlockSpec((blocks, tile, width), lambda i: (0, i, 0)),
        kind_of((blocks, units, width)),
        [own, other, *actives, *(a.array for _, a in spread)],
        waits=waits,
    )


def up_grad(uppers, own, other, addends, waits=()):
    count, width = own.shape
    units = uppers[0].shape[1]
    tile = min(2 * TILE, width)
    blocks = len(uppers)
    spread = [(q, a) for q in range(blocks) for a in addends[q]]

    def kernel(own_ref, other_ref, *refs):
        for q in range(blocks):
            total = dot(own_ref[...], refs[q][:count, :], 0, 0) + dot(other_ref[...], refs[q][count:, :], 0, 0)
            for j, (of, _) in enumerate(spread):
                if of == q:
                    total = total + wide(refs[blocks + j][...])
            refs[-1][q] = total.astype(jnp.bfloat16)

    columns = pl.BlockSpec((count, tile), lambda i: (0, i))
    return run(
        kernel,
        "up_grad",
        (width // tile,),
        [columns, columns]
        + [fixed(u) for u in uppers]
        + [a.spec((tile, units), lambda i: (i, 0)) for _, a in spread],
        pl.BlockSpec((blocks, tile, units), lambda i: (0, i, 0)),
        kind_of((blocks, width, units)),
        [own, other, *uppers, *(a.array for _, a in spread)],
        waits=waits,
    )


def norm_one_back(places, dfirst, dfirst_other, dmixed, sums_one, vectors, weight, part, waits=()):
    seqs, length, width = sums_one.shape
    ranks = width // part

    def kernel(place_ref, own_ref, other_ref, dmixed_ref, sum_ref, vector_ref, weight_ref, *outs):
        @pl.when(pl.program_id(0) == 0)
        def _():
            outs[-1][...] = jnp.zeros_like(outs[-1])

        upstream = wide(dmixed_ref[0]) + wide(own_ref[0]) + wide(other_ref[0])
        normed, inverse = standardize(wide(sum_ref[0]))
        dsum = standardize_back(upstream, normed, inverse, vector_ref[GAIN_ONE : GAIN_ONE + 1, :])
        dbranch = dsum.astype(jnp.bfloat16)
        outs[0][0] = dbranch
        for q in range(ranks):
            rows = pl.ds(pl.multiple_of(place_ref[q] * part, part), part)
            outs[1 + q][0] = dot(dbranch, weight_ref[rows, :], 1, 1).astype(jnp.bfloat16)
        outs[-1][0:1, :] += column_sum(wide(dbranch))
        outs[-1][1:2, :] += column_sum(upstream * normed)
        outs[-1][2:3, :] += column_sum(upstream)

    tokens = pl.BlockSpec((1, length, width), lambda b, p: (b, 0, 0))
    shape = sums_one.shape
    outs = run(
        kernel,
        "norm_one_back",
        (seqs,),
        [tokens, tokens, tokens, tokens, fixed(vectors), fixed(weight)],
        [tokens]
        + [pl.BlockSpec((1, length, part), lambda b, p: (b, 0, 0))] * ranks
        + [pl.BlockSpec((8, width), lambda b, p: (0, 0))],
        [kind_of(shape)]
        + [kind_of((seqs, length, part))] * ranks
        + [kind_of((8, width), jnp.float32)],
        [dfirst.reshape(shape), dfirst_other.reshape(shape), dmixed.reshape(shape), sums_one, vectors, weight],
        prefetch=(places,),
        waits=waits,
    )
    return outs[0], list(outs[1 : 1 + ranks]), outs[-1]


def out_grad_pack(places, contexts, dbranch, small, owners, waits=()):
    seqs, length, width = dbranch.shape
    ranks = len(contexts)
    part = contexts[0].shape[2]
    rows = width // owners
    extra = small.shape[0]
    each = part // rows

    def kernel(place_ref, *refs):
        dbranch_ref, small_ref, out_ref = refs[ranks:]
        grad = dbranch_ref[...].reshape(seqs * length, width)
        for q in range(ranks):
            product = dot(refs[q][...].reshape(seqs * length, part), grad, 0, 0).astype(jnp.bfloat16)
            for e in range(each):
                out_ref[place_ref[q] * each + e, :rows, :] = product[e * rows : (e + 1) * rows, :]
        for f in range(owners):
            out_ref[f, rows:, :] = jnp.zeros((extra, width), jnp.bfloat16)
            out_ref[f, rows:, :rows] = small_ref[:, f * rows : (f + 1) * rows]

    shape = (owners, rows + extra, width)
    return run(
        kernel,
        "out_grad_pack",
        (1,),
        [fixed(c) for c in contexts] + [fixed(dbranch), fixed(small)],
        pl.BlockSpec(shape, lambda i, p: (0, 0, 0)),
        kind_of(shape),
        [*contexts, dbranch, small],
        prefetch=(places,),
        waits=waits,
    )


def hidden_grad(places, dqkv, weight, width, length, picks, addends, dtype, waits=()):
    seqs, _, out_width = dqkv.shape
    owners = weight.shape[0]
    rows = width // owners
    blocks = len(picks)
    spread = [(k, a) for k in range(blocks) for a in addends[k]]

    def kernel(place_ref, weight_ref, *refs):
        whole = weight_ref[:, :rows, :].reshape(width, out_width)
        for k in range(blocks):
            total = dot(refs[k][0], whole, 1, 1)
            for j, (of, _) in enumerate(spread):
                if of == k:
                    total = total + wide(refs[blocks + j][0])
            refs[-1][k, 0] = total.astype(dtype)

    return run(
        kernel,
        "hidden_grad",
        (seqs,),
        [fixed(weight)]
        + [pl.BlockSpec((1, length, out_width), lambda b, p, q=q: (b, p[q], 0)) for q in picks]
        + [a.spec((1, length, width), lambda b, p: (b, 0, 0)) for _, a in spread],
        pl.BlockSpec((blocks, 1, length, width), lambda b, p: (0, b, 0, 0)),
        kind_of((blocks, seqs, length, width), dtype),
        [weight] + [dqkv] * blocks + [a.array for _, a in spread],
        prefetch=(places,),
        waits=waits,
        cost=2,
    )


def project_grad_pack(places, blocks, dqkv, owners, extra, waits=()):
    seqs, length, width = blocks[0].shape
    ranks = len(blocks)
    out_width = dqkv.shape[2]
    rows = width // owners
    group = max(1, TILE // rows)

    def kernel(place_ref, *refs):
        dqkv_ref, out_ref, total_ref = refs[ranks:]

        @pl.when(pl.program_id(0) == 0)
        def _():
            total_ref[...] = jnp.zeros_like(total_ref)
            total_ref[0:1, :] = column_sum(wide(dqkv_ref[...].reshape(-1, out_width)))

        total = 0.0
        for q in range(ranks):
            at = pl.ds(pl.multiple_of(place_ref[q] * length, length), length)
            for b in range(seqs):
                total = total + dot(refs[q][b], dqkv_ref[b, at, :], 0, 0)
        total = total.astype(jnp.bfloat16)
        sums = total_ref[...].astype(jnp.bfloat16)
        for e in range(group):
            out_ref[e, :rows, :] = total[e * rows : (e + 1) * rows, :]
            out_ref[e, rows:, :] = sums

    return run(
        kernel,
        "project_grad_pack",
        (owners // group,),
        [x.spec((seqs, length, group * rows), lambda i, p: (0, 0, i)) for x in blocks] + [fixed(dqkv)],
        pl.BlockSpec((group, rows + extra, out_width), lambda i, p: (i, 0, 0)),
        kind_of((owners, rows + extra, out_width)),
        [*arrays(blocks), dqkv],
        prefetch=(places,),
        scratch=(pltpu.VMEM((extra, out_width), jnp.float32),),
        waits=waits,
        cost=2,
    )


def lay_columns(places, blocks, rows):
    total, out_width = blocks[0].shape
    part = out_width // 3
    ranks = len(blocks)
    width = part * ranks

    def kernel(place_ref, *refs):
        for q in range(ranks):
            at = pl.ds(pl.multiple_of(place_ref[q] * part, part), part)
            for k in range(3):
                block = wide(refs[q][:, k * part : (k + 1) * part])
                refs[ranks + k][:, at] = block[:rows, :]
                refs[ranks + 3 + k][:, at] = block[rows : rows + 8, :]

    shape, below = (rows, width), (8, width)
    return run(
        kernel,
        "lay_columns",
        (1,),
        [b.whole() for b in blocks],
        [pl.BlockSpec(shape, lambda i, p: (0, 0))] * 3 + [pl.BlockSpec(below, lambda i, p: (0, 0))] * 3,
        [kind_of(shape, jnp.float32)] * 3 + [kind_of(below, jnp.float32)] * 3,
        arrays(blocks),
        prefetch=(places,),
        cost=2,
    )


def lay_up(places, blocks, chips, part, waits=()):
    _, rows, _ = blocks[0].shape
    ranks = len(blocks)
    shape = (rows, 2 * chips * ranks * part)

    def kernel(place_ref, *refs):
        for q in range(ranks):
            for c in range(2):
                for z in range(chips):
                    at = pl.multiple_of(((z * 2 + c) * ranks + place_ref[q]) * part, part)
                    refs[ranks][:, pl.ds(at, part)] = wide(refs[q][c, :, z * part : (z + 1) * part])

    return run(
        kernel,
        "lay_up",
        (1,),
        [b.whole() for b in blocks],
        pl.BlockSpec(shape, lambda i, p: (0, 0)),
        kind_of(shape, jnp.float32),
        arrays(blocks),
        prefetch=(places,),
        waits=waits,
        cost=2,
    )


def lay_rows(places, blocks, waits=()):
    part, width = blocks[0].shape
    ranks = len(blocks)
    shape = (part * ranks, width)

    def kernel(place_ref, *refs):
        for q in range(ranks):
            refs[ranks][pl.ds(pl.multiple_of(place_ref[q] * part, part), part), :] = wide(refs[q][...])

    return run(
        kernel,
        "lay_rows",
        (1,),
        [b.whole() for b in blocks],
        pl.BlockSpec(shape, lambda i, p: (0, 0)),
        kind_of(shape, jnp.float32),
        arrays(blocks),
        prefetch=(places,),
        waits=waits,
        cost=2,
    )


def lay_chips(at, blocks, waits):
    rows, width = blocks[0].shape
    chips = len(blocks)

    def kernel(at_ref, *refs):
        for d in range(chips):
            refs[chips][at_ref[d]] = refs[d][...]

    shape = (chips, rows, width)
    return run(
        kernel,
        "lay_chips",
        (1,),
        [fixed(b) for b in blocks],
        pl.BlockSpec(shape, lambda i, p: (0, 0, 0)),
        kind_of(shape),
        blocks,
        prefetch=(at,),
        cost=100,
        waits=waits,
    )


def hold(array, waits):
    def kernel(from_ref, to_ref):
        to_ref[...] = from_ref[...]

    rank = array.ndim
    return run(
        kernel,
        "hold",
        (1,),
        [fixed(array)],
        pl.BlockSpec(array.shape, lambda i: (0,) * rank),
        kind_of(array.shape, array.dtype),
        [array],
        waits=waits,
    )


def split(at, own, size, waits=()):
    _, width = own.shape
    chips = at.shape[0]

    def kernel(at_ref, own_ref, *outs):
        for d in range(chips):
            outs[d][...] = own_ref[pl.ds(pl.multiple_of(at_ref[d] * size, size), size), :]

    return run(
        kernel,
        "split",
        (1,),
        [fixed(own)],
        [pl.BlockSpec((size, width), lambda i, p: (0, 0))] * chips,
        [kind_of((size, width))] * chips,
        [own],
        prefetch=(at,),
        cost=100,
        waits=waits,
    )


def tick(*waits, cost=10):
    def kernel(out_ref):
        out_ref[...] = jnp.zeros_like(out_ref)

    return run(
        kernel, "tick", (1,), [], pl.BlockSpec((8, 128), lambda i: (0, 0)), kind_of((8, 128), jnp.float32), [], waits=waits, cost=cost
    )


def total_rows(pieces, waits=()):
    def kernel(*refs):
        total = wide(refs[0][...])
        for ref in refs[1:-1]:
            total = total + wide(ref[...])
        refs[-1][...] = total.astype(jnp.bfloat16)

    shape = pieces[0].shape
    return run(
        kernel,
        "total_rows",
        (1,),
        [fixed(p) for p in pieces],
        pl.BlockSpec(shape, lambda i: (0, 0)),
        kind_of(shape),
        pieces,
        waits=waits,
    )


def total_halves(core, pieces, waits=()):
    rows, width = pieces[0].shape
    half = rows // 2

    def kernel(core_ref, *refs):
        for out_ref, of in ((refs[-2], core_ref[0]), (refs[-1], 1 - core_ref[0])):
            at = pl.ds(pl.multiple_of(of * half, half), half)
            total = wide(refs[0][at, :])
            for ref in refs[1:-2]:
                total = total + wide(ref[at, :])
            out_ref[...] = total.astype(jnp.bfloat16)

    return run(
        kernel,
        "total_halves",
        (1,),
        [fixed(p) for p in pieces],
        [pl.BlockSpec((half, width), lambda i, p: (0, 0))] * 2,
        [kind_of((half, width))] * 2,
        pieces,
        prefetch=(core,),
        waits=waits,
    )


def pair(core, own, other, waits=()):
    rows, width = own.shape

    def kernel(core_ref, own_ref, other_ref, out_ref):
        out_ref[core_ref[0]] = own_ref[...]
        out_ref[1 - core_ref[0]] = other_ref[...]

    shape = (2, rows, width)
    return run(
        kernel,
        "pair",
        (1,),
        [fixed(own), fixed(other)],
        pl.BlockSpec(shape, lambda i, p: (0, 0, 0)),
        kind_of(shape),
        [own, other],
        prefetch=(core,),
        waits=waits,
    )


def plan_rows(segments):
    b, t = segments.shape
    span, win = min(SPAN, t), min(WINDOW, t)
    spans = segments.reshape(b, t // span, span)
    place = jnp.arange(t, dtype=jnp.int32)
    low = jnp.min(jnp.where(segments[:, None, :] == spans[:, :, :1], place, t), axis=2)
    high = jnp.max(jnp.where(segments[:, None, :] == spans[:, :, -1:], place, -1), axis=2)
    start = jnp.minimum(low // ALIGN * ALIGN, t - win)
    fits = jnp.all(high < start + win, axis=1)
    single = jnp.all(segments == segments[:, :1], axis=1)
    kind = jnp.where(single, 0, jnp.where(fits, 1, 2))
    return kind.astype(jnp.int32), start.astype(jnp.int32)

def aligned(start, size):
    return start if isinstance(start, int) else pl.multiple_of(start, size)


def bias_of(col_ref, keys, row_ref, queries):
    return jnp.where(col_ref[0, keys, :] == row_ref[0, :, queries], 0.0, MASKED)


def over(count, body):
    if count == 1:
        body(0)
    else:
        lax.fori_loop(0, count, lambda g, c: (body(g), c)[1], 0, unroll=UNROLL)


def fwd_kernel(heads, kind_ref, start_ref, place_ref, qkv_ref, row_ref, col_ref, ctx_ref, lse_ref, *part_refs):
    b = pl.program_id(0)
    t = qkv_ref.shape[1]
    hw = heads * HEAD_DIM
    span, win = min(SPAN, t), min(WINDOW, t)
    kind = kind_ref[b]

    group = min(2, heads)
    lanes = group * HEAD_DIM

    def attend(g, rows, keys, bias):
        def piece(which):
            return pl.ds(aligned(which * hw + g * lanes, lanes), lanes)

        query, key, value = (qkv_ref[0, r, piece(w)] for w, r in enumerate((rows, keys, keys)))
        parts = []
        for e in range(group):
            at = slice(e * HEAD_DIM, (e + 1) * HEAD_DIM)
            s = dot(key[:, at], query[:, at], 1, 1)
            if bias is not None:
                s = s + bias
            m = jnp.max(s, axis=0, keepdims=True)
            p = jnp.exp(s - m)
            total = jnp.sum(p, axis=0, keepdims=True)
            parts.append(dot(value[:, at], p.astype(jnp.bfloat16), 0, 0) / total)
            lse_ref[0, pl.ds(g * group + e, 1), rows] = m + jnp.log(total)
        ctx_ref[0, rows, piece(0)] = jnp.transpose(jnp.concatenate(parts, axis=0)).astype(jnp.bfloat16)

    def each(size, masked, keys_of):
        size = min(size, t)

        def body(i, _):
            rows = pl.ds(pl.multiple_of(i * size, size), size)
            bias = bias_of(col_ref, keys_of(i), row_ref, rows) if masked else None
            over(heads // group, lambda g: attend(g, rows, keys_of(i), bias))
            return 0

        lax.fori_loop(0, t // size, body, 0)

    @pl.when(kind == 0)
    def _():
        each(FORWARD_SPAN, False, lambda i: pl.ds(0, t))

    @pl.when(kind == 2)
    def _():
        each(span, True, lambda i: pl.ds(0, t))

    @pl.when(kind == 1)
    def _():
        each(span, True, lambda i: pl.ds(pl.multiple_of(start_ref[b, i], ALIGN), win))

    length = part_refs[0].shape[1]
    for q, part_ref in enumerate(part_refs):
        part_ref[0] = ctx_ref[0, pl.ds(pl.multiple_of(place_ref[q] * length, length), length), :]


def attention(qkv, segments, kind, start, places, waits):
    ranks = places.shape[0]
    b, t, w = qkv.shape
    hw = w // 3
    heads = hw // HEAD_DIM

    def at(i, *_):
        return (i, 0, 0)

    return run(
        functools.partial(fwd_kernel, heads),
        "attention_forward",
        (b,),
        [pl.BlockSpec((1, t, w), at), pl.BlockSpec((1, 1, t), at), pl.BlockSpec((1, t, 1), at)],
        [pl.BlockSpec((1, t, hw), at), pl.BlockSpec((1, heads, t), at)]
        + [pl.BlockSpec((1, t // ranks, hw), at)] * ranks,
        [kind_of((b, t, hw)), kind_of((b, heads, t), jnp.float32)] + [kind_of((b, t // ranks, hw))] * ranks,
        [qkv, segments[:, None, :], segments[:, :, None]],
        prefetch=(kind, start, places),
        waits=waits,
        cost=100,
    )

def bwd_kernel(heads, b, kind_ref, start_ref, qkv_ref, do_ref, ctx_ref, lse_ref, row_ref, col_ref, out_ref, dq_acc, delta_ref):
    t = qkv_ref.shape[1]
    hw = heads * HEAD_DIM
    span, win = min(SPAN, t), min(WINDOW, t)
    kind = kind_ref[b]

    def lanes(h, which=0):
        lo = which * hw + h * HEAD_DIM
        return slice(lo, lo + HEAD_DIM)

    prod = do_ref[0].astype(jnp.float32) * ctx_ref[0].astype(jnp.float32)
    high = prod.astype(jnp.bfloat16)
    rest = (prod - high.astype(jnp.float32)).astype(jnp.bfloat16)
    head = lax.broadcasted_iota(jnp.int32, (delta_ref.shape[0], hw), 0)
    of = lax.broadcasted_iota(jnp.int32, (delta_ref.shape[0], hw), 1) // HEAD_DIM
    ones = (head == of).astype(jnp.bfloat16)
    delta_ref[...] = dot(ones, high, 1, 1) + dot(ones, rest, 1, 1)

    group = min(2, heads)
    lanes = group * HEAD_DIM

    def back(g, keys, queries, bias):
        def piece(which):
            return pl.ds(aligned(which * hw + g * lanes, lanes), lanes)

        query, key, value = (qkv_ref[0, r, piece(w)] for w, r in enumerate((queries, keys, keys)))
        grad = do_ref[0, queries, piece(0)]
        key_grads, value_grads = [], []
        for e in range(group):
            at = slice(e * HEAD_DIM, (e + 1) * HEAD_DIM)
            row = pl.ds(g * group + e, 1)
            s = dot(key[:, at], query[:, at], 1, 1)
            if bias is not None:
                s = s + bias
            p = jnp.exp(s - lse_ref[0, row, queries])
            dp = dot(value[:, at], grad[:, at], 1, 1)
            ds = (p * (dp - delta_ref[row, queries])).astype(jnp.bfloat16)
            value_grads.append(dot(p.astype(jnp.bfloat16), grad[:, at], 1, 0))
            key_grads.append(dot(ds, query[:, at], 1, 0))
            into = pl.ds(aligned(g * lanes + e * HEAD_DIM, HEAD_DIM), HEAD_DIM)
            dq_acc[into, queries] += dot(key[:, at], ds, 0, 0)
        out_ref[0, keys, piece(1)] = jnp.concatenate(key_grads, axis=1).astype(jnp.bfloat16)
        out_ref[0, keys, piece(2)] = jnp.concatenate(value_grads, axis=1).astype(jnp.bfloat16)

    dq_acc[...] = jnp.zeros_like(dq_acc)

    def each(size, masked, queries_of):
        size = min(size, t)

        def body(j, _):
            keys = pl.ds(pl.multiple_of(j * size, size), size)
            bias = bias_of(col_ref, keys, row_ref, queries_of(j)) if masked else None
            over(heads // group, lambda g: back(g, keys, queries_of(j), bias))
            return 0

        lax.fori_loop(0, t // size, body, 0)

    @pl.when(kind == 0)
    def _():
        each(BACKWARD_SPAN, False, lambda j: pl.ds(0, t))

    @pl.when(kind == 2)
    def _():
        each(span, True, lambda j: pl.ds(0, t))

    @pl.when(kind == 1)
    def _():
        each(span, True, lambda j: pl.ds(pl.multiple_of(start_ref[b, j], ALIGN), win))

    out_ref[0, :, :hw] = (jnp.transpose(dq_acc[...]) * (HEAD_DIM**-0.5)).astype(jnp.bfloat16)


def attention_back(qkv, dparts, ctx, lse, segments, kind, start, places, which, buffer, waits):
    b, t, w = qkv.shape
    hw = w // 3
    heads = hw // HEAD_DIM
    ranks = len(dparts)
    length = t // ranks

    def kernel(kind_ref, start_ref, place_ref, qkv_ref, *refs):
        grad_ref = refs[-1]
        for q in range(ranks):
            grad_ref[0, pl.ds(pl.multiple_of(place_ref[q] * length, length), length), :] = refs[q][0]
        bwd_kernel(heads, which, kind_ref, start_ref, qkv_ref, grad_ref, *refs[ranks : ranks + 4], *refs[-4:-1])

    def at(i, *_):
        return (which, 0, 0)

    ins = [pl.BlockSpec((1, t, w), at)] + [pl.BlockSpec((1, length, hw), at)] * ranks
    ins += [
        pl.BlockSpec((1, t, hw), at),
        pl.BlockSpec((1, heads, t), at),
        pl.BlockSpec((1, 1, t), at),
        pl.BlockSpec((1, t, 1), at),
    ]
    operands = [qkv, *dparts, ctx, lse, segments[:, None, :], segments[:, :, None]]
    alias = None
    if buffer is not None:
        ins.append(pl.BlockSpec(memory_space=pl.ANY))
        operands.append(buffer)
        alias = {3 + len(ins) - 1: 0}
    return run(
        kernel,
        "attention_backward",
        (1,),
        ins,
        pl.BlockSpec((1, t, w), at),
        kind_of((b, t, w)),
        operands,
        prefetch=(kind, start, places),
        scratch=(
            pltpu.VMEM((hw, t), jnp.float32),
            pltpu.VMEM((-(-heads // 8) * 8, t), jnp.float32),
            pltpu.VMEM((1, t, hw), jnp.bfloat16),
        ),
        alias=alias,
        waits=waits,
    )


AXES = ("seq", "z", "core")
ROWS = ("z", "core")
EXTRA = 16


def low(tensor):
    return tensor.astype(jnp.bfloat16)


class Ring:
    def __init__(self):
        self.ranks = lax.axis_size("seq")
        self.chips = lax.axis_size("z")
        self.index = lax.axis_index("seq")
        self.core = lax.axis_index("core")
        self.count = self.ranks.bit_length() - 1

    def bit(self, k, core):
        if self.count == 2 and core == 1:
            k = 1 - k
        return 1 << k

    def offset(self, q, core):
        return sum(self.bit(k, core) for k in range(self.count) if q >> k & 1)

    def place(self, q):
        return jnp.bitwise_xor(self.index, jnp.where(self.core == 0, self.offset(q, 0), self.offset(q, 1)))

    def hop(self, block, k):
        pairs = []
        for s in range(self.ranks):
            for z in range(self.chips):
                for c in range(2):
                    to = s ^ self.bit(k, c)
                    pairs.append(((s * self.chips + z) * 2 + c, (to * self.chips + z) * 2 + c))
        return lax.ppermute(block, AXES, pairs)

    def gather(self, block):
        blocks = [block]
        for k in range(self.count):
            blocks = blocks + [self.hop(b, k) for b in blocks]
        return [View(b) for b in blocks]

    def exchange(self, blocks):
        out = [blocks[0]]
        for q in range(1, self.ranks):
            pairs = []
            for s in range(self.ranks):
                for z in range(self.chips):
                    for c in range(2):
                        to = s ^ self.offset(q, c)
                        pairs.append(((s * self.chips + z) * 2 + c, (to * self.chips + z) * 2 + c))
            out.append(lax.ppermute(blocks[q], AXES, pairs))
        return out

    def shift(self, block, d):
        return lax.ppermute(block, "z", [(z, (z + d) % self.chips) for z in range(self.chips)])


def swap(block):
    return lax.ppermute(block, "core", [(0, 1), (1, 0)])


def put(blocks, ring, axis):
    shape = list(blocks[0].shape)
    size = shape[axis]
    shape[axis] = size * len(blocks)
    whole = jnp.zeros(shape, blocks[0].dtype)
    for q, block in enumerate(blocks):
        whole = lax.dynamic_update_slice_in_dim(whole, block, ring.place(q) * size, axis)
    return whole


def local(
    hidden_in,
    segments,
    q_weight,
    k_weight,
    v_weight,
    out_weight,
    q_bias,
    v_bias,
    out_bias,
    up_weight,
    up_bias,
    down_weight,
    down_bias,
    norm1_gain,
    norm1_bias,
    norm2_gain,
    norm2_bias,
    out_grad,
):
    ring = Ring()
    here, core = ring.index, ring.core
    ranks, chips = ring.ranks, ring.chips
    owners = chips * 2
    z_index = lax.axis_index("z")
    owner = z_index * 2 + core
    seqs, length, width = hidden_in.shape
    full = length * ranks
    head_width = width // ranks
    out_width = 3 * head_width
    rows = width // owners
    units = down_weight.shape[0]
    part = units // ranks
    count = seqs * length
    score_scale = HEAD_DIM ** (-0.5)
    first_core = core == 0
    core_index = core.astype(jnp.int32).reshape(1)
    places = jnp.stack([ring.place(q) for q in range(ranks)]).astype(jnp.int32)
    blocks = range(ranks)

    heads_at = here * head_width
    mine = jnp.concatenate(
        [lax.dynamic_slice_in_dim(w, heads_at, head_width, 1) for w in (q_weight, k_weight, v_weight)], axis=1
    )
    vectors = (q_bias, v_bias, out_bias, down_bias, norm1_gain, norm1_bias, norm2_gain, norm2_bias)
    known = len(vectors)
    packed = jnp.pad(
        up_bias.reshape(-1, rows), ((known, EXTRA - known - units // rows), (0, out_width - rows))
    )
    for i, vector in enumerate(vectors):
        packed = packed + jnp.pad(vector[None], ((i, EXTRA - 1 - i), (0, out_width - rows)))
    mine = jnp.concatenate([mine, packed], axis=0)

    def up_columns(of_core):
        return jnp.concatenate(
            [
                lax.dynamic_slice_in_dim(up_weight, ((z * 2 + of_core) * ranks + here) * part, part, 1)
                for z in range(chips)
            ],
            axis=1,
        )

    own_up, other_up = up_columns(core), swap(up_columns(1 - core))
    up_rows = jnp.concatenate(
        [jnp.where(first_core, own_up, other_up), jnp.where(first_core, other_up, own_up)], axis=0
    )
    hidden = ring.gather(hidden_in)
    shifts = jnp.stack([(z_index - d) % chips for d in range(chips)]).astype(jnp.int32)
    up_block = lay_chips(shifts, [up_rows] + [ring.shift(up_rows, d) for d in range(1, chips)], ())
    up_block = hold(up_block.reshape(width, chips * part), (hidden[-1].array,))
    gathered = lax.all_gather(mine, ROWS, axis=0)
    down_rows = hold(lax.dynamic_slice_in_dim(down_weight, here * part, part, 0), (gathered,))
    down_block = lax.all_gather(down_rows, "z", axis=0, tiled=True)
    output_weight = lax.all_gather(hold(out_weight, (down_rows,)), ROWS, axis=0, tiled=True)
    up_weights = ring.gather(up_block)
    kind, start = plan_rows(segments)
    keep = wide(lax.dynamic_slice_in_dim(segments, here * length, length, 1) != 0)[:, :, None]

    qkv_weight = gathered
    gathered = wide(gathered[:, rows:, :rows])
    vectors = gathered.transpose(1, 0, 2).reshape(EXTRA, width)
    biases = lax.dynamic_slice_in_dim(vectors, heads_at, head_width, 1)
    qkv_bias = jnp.concatenate([biases[0], jnp.zeros_like(biases[0]), biases[1]])[None]
    scales = jnp.where(jnp.arange(out_width) < head_width, score_scale, 1.0)[None]
    qkv = project(places, hidden, qkv_weight, qkv_bias, scales)
    contexts, log_totals, *context_parts = attention(
        qkv, segments, kind, start, places, (up_block,)
    )
    context_parts = ring.exchange(context_parts)
    down_weights = ring.gather(hold(down_block, (*context_parts[1:], *arrays(up_weights[1:3]))))
    sums_one, first_low = out_norm(
        places,
        context_parts,
        output_weight,
        hidden_in,
        vectors,
    )

    first_low = first_low.reshape(count, width)
    first_other = swap(first_low)
    upper_bias = gathered[:, known : known + units // rows].reshape(chips, 2, ranks, part)
    upper_bias = lax.dynamic_index_in_dim(upper_bias, core, 1, False)
    upper_bias = [
        lax.dynamic_index_in_dim(upper_bias, ring.place(q), 1, False).reshape(1, -1) for q in blocks
    ]
    actives, slopes = up_forward(
        first_low, first_other, up_weights, upper_bias, arrays(down_weights[1:2])
    )
    mixed_other = down_forward(actives, down_weights, count, count, jnp.bfloat16)
    mixed = down_forward(actives, down_weights, 0, count, jnp.bfloat16, (mixed_other,))
    layer_out, dmixed, totals_two = norm_two(mixed, swap(mixed_other), sums_one, vectors, out_grad, keep)

    dmixed = dmixed.reshape(count, width)
    dmixed_other = swap(dmixed)
    none = [()] * ranks
    odd, even = [q for q in blocks if q % 2], [q for q in blocks if q % 2 == 0]
    down_sent = down_grad([actives[q] for q in odd], dmixed, dmixed_other, none)
    duppers, up_sums, dfirst, dfirst_other = ffn_back(
        dmixed, dmixed_other, slopes, down_weights, up_weights, (tick(down_sent),)
    )
    dfirst_other = swap(dfirst_other)
    dbranch, dcontexts, totals_one = norm_one_back(
        places, dfirst, dfirst_other, dmixed, sums_one, vectors, output_weight, head_width, (tick(duppers[0], cost=10),)
    )
    dcontexts = ring.exchange(dcontexts)

    def spread(made, sent):
        came = {q: [] for q in blocks}
        for k in range(ring.count):
            step = 1 << k
            got = ring.hop(sent, k)
            for i, q in enumerate(range(0, ranks, 2 * step)):
                came[q].append(View(got, i))
            if k + 1 < ring.count:
                turn = [q + 2 * step for q in range(0, ranks, 4 * step)]
                sent = made(turn, [came[q] for q in turn])
        return came[0], sent

    def down_made(turn, addends):
        return down_grad([actives[q] for q in turn], dmixed, dmixed_other, addends, (tick(dbranch),))

    down_came, down_hop = spread(down_made, down_sent)
    up_sent = up_grad([duppers[q] for q in odd], first_low, first_other, none, (down_hop,))

    extra = -(-(6 + ranks) // EXTRA) * EXTRA
    up_totals = put([up_sums[q : q + 1] for q in blocks], ring, 0).reshape(ranks, chips, 1, part)
    up_totals = jnp.where(jnp.arange(2)[None, None, :, None] == core, up_totals, 0.0)
    up_totals = jnp.pad(up_totals, ((0, 0), (0, 0), (0, 0), (0, rows - part))).reshape(ranks, width)
    small = jnp.concatenate(
        [totals_two[:3], totals_one[:3], up_totals, jnp.zeros((extra - 6 - ranks, width), jnp.float32)], axis=0
    )
    out_pack = out_grad_pack(places, context_parts, dbranch, low(small), owners, (up_sent,))
    out_shard = lax.psum_scatter(out_pack.reshape(-1, width), ROWS, scatter_dimension=0, tiled=True)

    common = (qkv, dcontexts, contexts, log_totals, segments, kind, start, places)
    dqkv = attention_back(*common, 0, None, (out_pack,))

    def up_made(turn, addends):
        return up_grad([duppers[q] for q in turn], first_low, first_other, addends, (down_pieces[0],))

    down_own = down_grad([actives[0]], dmixed, dmixed_other, [down_came], (dqkv,))[0]
    ahead = jnp.stack([(z_index + d) % chips for d in range(chips)]).astype(jnp.int32)
    down_pieces = split(ahead, down_own, part)
    up_came, up_hop = spread(up_made, up_sent)
    for which in range(1, seqs):
        dqkv = attention_back(*common, which, dqkv, (up_hop,))

    def shifted(pieces):
        return [pieces[0]] + [ring.shift(pieces[d], d) for d in range(1, chips)]

    def hidden_made(turn, addends, waits=()):
        return hidden_grad(places, dqkv, qkv_weight, width, length, turn, addends, jnp.bfloat16, waits or (up_pair,))

    down_shard = total_rows(shifted(down_pieces), (dqkv, up_came[-1].array))
    down_parts = ring.gather(down_shard)
    up_own = up_grad([duppers[0]], first_low, first_other, [up_came], (down_shard,))[0]
    up_pieces = split(ahead, up_own, 2 * rows)
    hidden_sent = hidden_made(odd, none, (up_pieces[0], *arrays(down_parts[1:2])))
    qkv_pack = project_grad_pack(
        places, hidden, dqkv, owners, EXTRA, (hidden_sent, out_shard, *arrays(down_parts[2:]))
    )
    qkv_shard = lax.psum_scatter(qkv_pack.reshape(-1, out_width), ROWS, scatter_dimension=0, tiled=True)
    out_sum = [wide(out_shard)]
    for k in range(ring.count):
        out_sent = low(out_sum[-1])
        out_sum.append(out_sum[-1] + wide(ring.hop(out_sent, k)))
    keep_part, take_part = total_halves(core_index, shifted(up_pieces), (qkv_pack,))
    down_weight_grad = lay_rows(places, down_parts, (keep_part,))
    up_pair = pair(core_index, keep_part, swap(take_part), (down_weight_grad,))
    hidden_came, hidden_hop = spread(hidden_made, hidden_sent)
    input_grad = hidden_grad(
        places, dqkv, qkv_weight, width, length, [0], [[View(dbranch)] + hidden_came], jnp.float32
    )[0]

    up_parts = ring.gather(up_pair)
    qkv_parts = ring.gather(qkv_shard)
    out_pack = out_sum[-1]
    if part % 128 == 0:
        up_weight_grad = lay_up(places, up_parts, chips, part, (hidden_hop,))
    else:
        up_weight_grad = wide(put([b.value()[None] for b in up_parts], ring, 0))
        up_weight_grad = (
            up_weight_grad.reshape(ranks, 2, rows, chips, part).transpose(2, 3, 1, 0, 4).reshape(rows, owners * units)
        )
    if head_width % 128 == 0:
        *qkv_grads, q_sums, _, v_sums = lay_columns(places, qkv_parts, rows)
    else:
        laid = wide(put([b.value()[None] for b in qkv_parts], ring, 0))
        laid = laid.reshape(ranks, rows + EXTRA, 3, head_width).transpose(2, 1, 0, 3).reshape(3, -1, width)
        qkv_grads, q_sums, v_sums = [g[:rows] for g in laid], laid[0, rows:], laid[2, rows:]

    def mine_of(sums):
        return lax.dynamic_slice_in_dim(sums[0], owner * rows, rows, 0)

    small = out_pack[rows:, :rows]
    up_bias_grad = small[6 : 6 + ranks, :part].reshape(-1)
    return (
        layer_out,
        input_grad,
        *qkv_grads,
        out_pack[:rows],
        mine_of(q_sums),
        mine_of(v_sums),
        small[3],
        up_weight_grad,
        up_bias_grad,
        down_weight_grad,
        small[0],
        small[4],
        small[5],
        small[1],
        small[2],
    )


def solution(mesh):
    ranks, owners = mesh.shape["seq"], mesh.shape["fsdp"]
    grid = Mesh(mesh.devices.reshape(ranks, owners // 2, 2), AXES)
    tokens, matrix, vector = P(ROWS, "seq", None), P(ROWS, None), P(ROWS)
    return jax.shard_map(
        local,
        mesh=grid,
        in_specs=(
            tokens,
            matrix,
            matrix,
            matrix,
            matrix,
            matrix,
            vector,
            vector,
            vector,
            matrix,
            vector,
            matrix,
            vector,
            vector,
            vector,
            vector,
            vector,
            tokens,
        ),
        out_specs=(
            tokens,
            tokens,
            matrix,
            matrix,
            matrix,
            matrix,
            vector,
            vector,
            vector,
            matrix,
            vector,
            matrix,
            vector,
            vector,
            vector,
            vector,
            vector,
        ),
        check_vma=False,
    )
```

```python
import functools

import jax
import jax.numpy as jnp
from jax import lax
from jax.experimental import pallas as pl
from jax.experimental.pallas import tpu as pltpu
from jax.sharding import Mesh
from jax.sharding import PartitionSpec as P

HEAD_DIM = 64
SPAN = 256
ALIGN = 128
WINDOW = 512
FORWARD_SPAN = 1024
BACKWARD_SPAN = 512
UNROLL = True
MASKED = -1e30


def dot(a,b,ca,cb):
    return lax.dot_general(a,b,(((ca,),(cb,)),((),())),preferred_element_type=jnp.float32)


TILE = 256


def run(kernel, name, grid, ins, outs, shapes, operands, prefetch=(), scratch=(), alias=None, waits=(), cost=10):
    known = len(prefetch) + len(ins)

    def waiting(*refs):
        kernel(*refs[:known], *refs[known + len(waits) :])

    ins = list(ins) + [pl.BlockSpec(memory_space=pl.ANY)] * len(waits)
    operands = list(operands) + list(waits)
    return pl.pallas_call(
        waiting,
        grid_spec=pltpu.PrefetchScalarGridSpec(
            num_scalar_prefetch=len(prefetch), grid=grid, in_specs=ins, out_specs=outs, scratch_shapes=scratch
        ),
        out_shape=shapes,
        input_output_aliases=alias or {},
        compiler_params=pltpu.CompilerParams(vmem_limit_bytes=50 << 20),
        cost_estimate=pl.CostEstimate(flops=cost * 3000000000, bytes_accessed=1000, transcendentals=0),
        name=name,
    )(*prefetch, *operands)


def fixed(array):
    rank = array.ndim
    return pl.BlockSpec(array.shape, lambda *_: (0,) * rank, pipeline_mode=pl.Buffered(buffer_count=1))


class View:
    def __init__(self, array, i=None):
        self.array, self.i = array, i
        self.shape = array.shape if i is None else array.shape[1:]

    def spec(self, block, place):
        i = self.i
        if i is None:
            return pl.BlockSpec(block, place)
        return pl.BlockSpec((None,) + tuple(block), lambda *a: (i,) + tuple(place(*a)))

    def whole(self):
        rank, i = len(self.shape), self.i
        once = pl.Buffered(buffer_count=1)
        if i is None:
            return pl.BlockSpec(self.shape, lambda *_: (0,) * rank, pipeline_mode=once)
        return pl.BlockSpec((None,) + tuple(self.shape), lambda *_: (i,) + (0,) * rank, pipeline_mode=once)

    def value(self):
        return self.array if self.i is None else self.array[self.i]


def arrays(views):
    return [v.array for v in views]


def kind_of(shape, dtype=jnp.bfloat16):
    return jax.ShapeDtypeStruct(tuple(shape), dtype)


def wide(tensor):
    return tensor.astype(jnp.float32)


def standardize(values):
    center = jnp.mean(values, axis=1, keepdims=True)
    offset = values - center
    inverse = lax.rsqrt(jnp.mean(offset * offset, axis=1, keepdims=True) + 1e-05)
    return offset * inverse, inverse


def standardize_back(upstream, normed, inverse, gain):
    scaled = upstream * gain
    return inverse * (
        scaled
        - jnp.mean(scaled, axis=1, keepdims=True)
        - normed * jnp.mean(scaled * normed, axis=1, keepdims=True)
    )


def column_sum(values):
    return jnp.sum(values, axis=0, keepdims=True)


OUT_BIAS, DOWN_BIAS, GAIN_ONE, SHIFT_ONE, GAIN_TWO, SHIFT_TWO = 2, 3, 4, 5, 6, 7


def project(places, blocks, weight, bias, scale):
    seqs, length, width = blocks[0].shape
    ranks = len(blocks)
    owners, _, out_width = weight.shape
    rows = width // owners

    def kernel(place_ref, weight_ref, bias_ref, scale_ref, *refs):
        for q in range(ranks):

            @pl.when(pl.program_id(0) == q)
            def _(q=q):
                whole = weight_ref[:, :rows, :].reshape(width, out_width)
                product = dot(refs[q][...].reshape(seqs * length, width), whole, 1, 0) + bias_ref[...]
                product = (product * scale_ref[...]).astype(jnp.bfloat16)
                refs[ranks][...] = product.reshape(seqs, length, out_width)

    return run(
        kernel,
        "project",
        (ranks,),
        [fixed(weight), fixed(bias), fixed(scale)] + [block.whole() for block in blocks],
        pl.BlockSpec((seqs, length, out_width), lambda i, p: (0, p[i], 0)),
        kind_of((seqs, length * ranks, out_width)),
        [weight, bias, scale, *arrays(blocks)],
        prefetch=(places,),
    )


def out_norm(places, contexts, weight, hidden, vectors, waits=()):
    seqs, length, width = hidden.shape
    ranks = len(contexts)
    part = contexts[0].shape[2]

    def kernel(place_ref, *refs):
        weight_ref, hidden_ref, vector_ref, sum_ref, first_ref = refs[ranks:]
        total = wide(hidden_ref[0]) + vector_ref[OUT_BIAS : OUT_BIAS + 1, :]
        for q in range(ranks):
            rows = pl.ds(pl.multiple_of(place_ref[q] * part, part), part)
            total = total + dot(refs[q][0], weight_ref[rows, :], 1, 0)
        total = total.astype(jnp.bfloat16)
        sum_ref[0] = total
        normed, _ = standardize(wide(total))
        first = normed * vector_ref[GAIN_ONE : GAIN_ONE + 1, :] + vector_ref[SHIFT_ONE : SHIFT_ONE + 1, :]
        first_ref[0] = first.astype(jnp.bfloat16)

    tokens = pl.BlockSpec((1, length, width), lambda b, p: (b, 0, 0))
    return run(
        kernel,
        "out_norm",
        (seqs,),
        [pl.BlockSpec((1, length, part), lambda b, p: (b, 0, 0))] * ranks + [fixed(weight), tokens, fixed(vectors)],
        [tokens, tokens],
        [kind_of(hidden.shape), kind_of(hidden.shape)],
        [*contexts, weight, hidden, vectors],
        prefetch=(places,),
        waits=waits,
    )


def up_forward(own, other, weights, biases, waits=()):
    count, width = own.shape
    units = weights[0].shape[1]
    blocks = len(weights)
    tile = min(TILE, count)
    half = count // tile

    def kernel(own_ref, other_ref, *refs):
        def body(tokens):
            uppers = [dot(tokens, refs[q][...], 1, 0) for q in range(blocks)]
            for q in range(blocks):
                upper = uppers[q] + refs[blocks + q][...]
                tail = 0.5 * (1.0 + lax.erf(upper * 0.7071067811865476))
                refs[2 * blocks + q][...] = (upper * tail).astype(jnp.bfloat16)
                bell = jnp.exp(-0.5 * upper * upper) * 0.3989422804014327
                refs[3 * blocks + q][...] = (tail + upper * bell).astype(jnp.bfloat16)

        @pl.when(pl.program_id(0) < half)
        def _():
            body(own_ref[...])

        @pl.when(pl.program_id(0) >= half)
        def _():
            body(other_ref[...])

    outs = run(
        kernel,
        "up_forward",
        (2 * half,),
        [
            pl.BlockSpec((tile, width), lambda i: (jnp.minimum(i, half - 1), 0)),
            pl.BlockSpec((tile, width), lambda i: (jnp.maximum(i - half, 0), 0)),
        ]
        + [w.whole() for w in weights]
        + [fixed(b) for b in biases],
        [pl.BlockSpec((tile, units), lambda i: (i, 0))] * (2 * blocks),
        [kind_of((2 * count, units))] * (2 * blocks),
        [own, other, *arrays(weights), *biases],
        waits=waits,
    )
    return list(outs[:blocks]), list(outs[blocks:])


def down_forward(actives, weights, first, count, dtype, waits=()):
    blocks = len(actives)
    units, width = weights[0].shape
    tile = min(TILE, count)

    def kernel(*refs):
        total = dot(refs[0][...], refs[blocks][...], 1, 0)
        for q in range(1, blocks):
            total = total + dot(refs[q][...], refs[blocks + q][...], 1, 0)
        refs[-1][...] = total.astype(dtype)

    return run(
        kernel,
        "down_forward",
        (count // tile,),
        [pl.BlockSpec((tile, units), lambda i: (i + first // tile, 0))] * blocks + [w.whole() for w in weights],
        pl.BlockSpec((tile, width), lambda i: (i, 0)),
        kind_of((count, width), dtype),
        [*actives, *arrays(weights)],
        waits=waits,
    )


def norm_two(mixed, mixed_other, sums_one, vectors, out_grad, keep):
    seqs, length, width = sums_one.shape

    def kernel(mixed_ref, other_ref, sum_ref, vector_ref, grad_ref, keep_ref, out_ref, dmixed_ref, total_ref):
        @pl.when(pl.program_id(0) == 0)
        def _():
            total_ref[...] = jnp.zeros_like(total_ref)

        def vector(i):
            return vector_ref[i : i + 1, :]

        normed, _ = standardize(wide(sum_ref[0]))
        first = normed * vector(GAIN_ONE) + vector(SHIFT_ONE)
        mixed = wide(mixed_ref[0]) + wide(other_ref[0]) + vector(DOWN_BIAS)
        normed, inverse = standardize(first + mixed)
        out_ref[0] = (normed * vector(GAIN_TWO) + vector(SHIFT_TWO)).astype(jnp.bfloat16)
        cot = wide(grad_ref[0]) * keep_ref[0]
        dmixed = standardize_back(cot, normed, inverse, vector(GAIN_TWO)).astype(jnp.bfloat16)
        dmixed_ref[0] = dmixed
        total_ref[0:1, :] += column_sum(wide(dmixed))
        total_ref[1:2, :] += column_sum(cot * normed)
        total_ref[2:3, :] += column_sum(cot)

    tokens = pl.BlockSpec((1, length, width), lambda b: (b, 0, 0))
    shape = sums_one.shape
    return run(
        kernel,
        "norm_two",
        (seqs,),
        [tokens, tokens, tokens, fixed(vectors), tokens, pl.BlockSpec((1, length, 1), lambda b: (b, 0, 0))],
        [tokens, tokens, pl.BlockSpec((8, width), lambda b: (0, 0))],
        [kind_of(shape), kind_of(shape), kind_of((8, width), jnp.float32)],
        [mixed.reshape(shape), mixed_other.reshape(shape), sums_one, vectors, out_grad, keep],
    )


def ffn_back(own, other, slopes, downs, ups, waits=()):
    blocks = len(slopes)
    count, width = own.shape
    units = slopes[0].shape[1]
    tile = min(2 * TILE, count)
    half = count // tile

    def kernel(own_ref, other_ref, *refs):
        slope_refs, down_refs, up_refs = refs[:blocks], refs[blocks : 2 * blocks], refs[2 * blocks : 3 * blocks]
        upper_refs, total_ref, here_ref, there_ref = refs[3 * blocks : 4 * blocks], refs[-3], refs[-2], refs[-1]
        step = pl.program_id(0)

        @pl.when(step == 0)
        def _():
            total_ref[...] = jnp.zeros_like(total_ref)

        def body(grad):
            back = [dot(grad, down_refs[q][...], 1, 1) for q in range(blocks)]
            total = 0.0
            for q in range(blocks):
                upper = back[q] * wide(slope_refs[q][...])
                total_ref[q : q + 1, :] += column_sum(upper)
                upper_refs[q][...] = upper.astype(jnp.bfloat16)
            for q in range(blocks):
                total = total + dot(upper_refs[q][...], up_refs[q][...], 1, 1)
            return total

        @pl.when(step < half)
        def _():
            there_ref[...] = body(other_ref[...]).astype(jnp.bfloat16)

        @pl.when(step >= half)
        def _():
            here_ref[...] = body(own_ref[...]).astype(jnp.bfloat16)

    def early(i):
        return (jnp.minimum(i, half - 1), 0)

    def late(i):
        return (jnp.maximum(i - half, 0), 0)

    def both(i):
        return ((i + half) % (2 * half), 0)

    outs = run(
        kernel,
        "feed_forward_back",
        (2 * half,),
        [pl.BlockSpec((tile, width), late), pl.BlockSpec((tile, width), early)]
        + [pl.BlockSpec((tile, units), both)] * blocks
        + [w.whole() for w in (*downs, *ups)],
        [pl.BlockSpec((tile, units), both)] * blocks
        + [
            pl.BlockSpec((max(8, blocks), units), lambda i: (0, 0)),
            pl.BlockSpec((tile, width), late),
            pl.BlockSpec((tile, width), early),
        ],
        [kind_of((2 * count, units))] * blocks
        + [
            kind_of((max(8, blocks), units), jnp.float32),
            kind_of((count, width)),
            kind_of((count, width)),
        ],
        [own, other, *slopes, *arrays(downs), *arrays(ups)],
        waits=waits,
    )
    return list(outs[:blocks]), outs[blocks], outs[blocks + 1], outs[blocks + 2]


def down_grad(actives, own, other, addends, waits=()):
    count, width = own.shape
    units = actives[0].shape[1]
    tile = min(TILE, units)
    blocks = len(actives)
    spread = [(q, a) for q in range(blocks) for a in addends[q]]

    def kernel(own_ref, other_ref, *refs):
        for q in range(blocks):
            total = dot(refs[q][:count, :], own_ref[...], 0, 0) + dot(refs[q][count:, :], other_ref[...], 0, 0)
            for j, (of, _) in enumerate(spread):
                if of == q:
                    total = total + wide(refs[blocks + j][...])
            refs[-1][q] = total.astype(jnp.bfloat16)

    return run(
        kernel,
        "down_grad",
        (units // tile,),
        [fixed(own), fixed(other)]
        + [pl.BlockSpec((2 * count, tile), lambda i: (0, i))] * blocks
        + [a.spec((tile, width), lambda i: (i, 0)) for _, a in spread],
        pl.BlockSpec((blocks, tile, width), lambda i: (0, i, 0)),
        kind_of((blocks, units, width)),
        [own, other, *actives, *(a.array for _, a in spread)],
        waits=waits,
    )


def up_grad(uppers, own, other, addends, waits=()):
    count, width = own.shape
    units = uppers[0].shape[1]
    tile = min(2 * TILE, width)
    blocks = len(uppers)
    spread = [(q, a) for q in range(blocks) for a in addends[q]]

    def kernel(own_ref, other_ref, *refs):
        for q in range(blocks):
            total = dot(own_ref[...], refs[q][:count, :], 0, 0) + dot(other_ref[...], refs[q][count:, :], 0, 0)
            for j, (of, _) in enumerate(spread):
                if of == q:
                    total = total + wide(refs[blocks + j][...])
            refs[-1][q] = total.astype(jnp.bfloat16)

    columns = pl.BlockSpec((count, tile), lambda i: (0, i))
    return run(
        kernel,
        "up_grad",
        (width // tile,),
        [columns, columns]
        + [fixed(u) for u in uppers]
        + [a.spec((tile, units), lambda i: (i, 0)) for _, a in spread],
        pl.BlockSpec((blocks, tile, units), lambda i: (0, i, 0)),
        kind_of((blocks, width, units)),
        [own, other, *uppers, *(a.array for _, a in spread)],
        waits=waits,
    )


def norm_one_back(places, dfirst, dfirst_other, dmixed, sums_one, vectors, weight, part, waits=()):
    seqs, length, width = sums_one.shape
    ranks = width // part

    def kernel(place_ref, own_ref, other_ref, dmixed_ref, sum_ref, vector_ref, weight_ref, *outs):
        @pl.when(pl.program_id(0) == 0)
        def _():
            outs[-1][...] = jnp.zeros_like(outs[-1])

        upstream = wide(dmixed_ref[0]) + wide(own_ref[0]) + wide(other_ref[0])
        normed, inverse = standardize(wide(sum_ref[0]))
        dsum = standardize_back(upstream, normed, inverse, vector_ref[GAIN_ONE : GAIN_ONE + 1, :])
        dbranch = dsum.astype(jnp.bfloat16)
        outs[0][0] = dbranch
        for q in range(ranks):
            rows = pl.ds(pl.multiple_of(place_ref[q] * part, part), part)
            outs[1 + q][0] = dot(dbranch, weight_ref[rows, :], 1, 1).astype(jnp.bfloat16)
        outs[-1][0:1, :] += column_sum(wide(dbranch))
        outs[-1][1:2, :] += column_sum(upstream * normed)
        outs[-1][2:3, :] += column_sum(upstream)

    tokens = pl.BlockSpec((1, length, width), lambda b, p: (b, 0, 0))
    shape = sums_one.shape
    outs = run(
        kernel,
        "norm_one_back",
        (seqs,),
        [tokens, tokens, tokens, tokens, fixed(vectors), fixed(weight)],
        [tokens]
        + [pl.BlockSpec((1, length, part), lambda b, p: (b, 0, 0))] * ranks
        + [pl.BlockSpec((8, width), lambda b, p: (0, 0))],
        [kind_of(shape)]
        + [kind_of((seqs, length, part))] * ranks
        + [kind_of((8, width), jnp.float32)],
        [dfirst.reshape(shape), dfirst_other.reshape(shape), dmixed.reshape(shape), sums_one, vectors, weight],
        prefetch=(places,),
        waits=waits,
    )
    return outs[0], list(outs[1 : 1 + ranks]), outs[-1]


def out_grad_pack(places, contexts, dbranch, small, owners, waits=()):
    seqs, length, width = dbranch.shape
    ranks = len(contexts)
    part = contexts[0].shape[2]
    rows = width // owners
    extra = small.shape[0]
    each = part // rows

    def kernel(place_ref, *refs):
        dbranch_ref, small_ref, out_ref = refs[ranks:]
        grad = dbranch_ref[...].reshape(seqs * length, width)
        for q in range(ranks):
            product = dot(refs[q][...].reshape(seqs * length, part), grad, 0, 0).astype(jnp.bfloat16)
            for e in range(each):
                out_ref[place_ref[q] * each + e, :rows, :] = product[e * rows : (e + 1) * rows, :]
        for f in range(owners):
            out_ref[f, rows:, :] = jnp.zeros((extra, width), jnp.bfloat16)
            out_ref[f, rows:, :rows] = small_ref[:, f * rows : (f + 1) * rows]

    shape = (owners, rows + extra, width)
    return run(
        kernel,
        "out_grad_pack",
        (1,),
        [fixed(c) for c in contexts] + [fixed(dbranch), fixed(small)],
        pl.BlockSpec(shape, lambda i, p: (0, 0, 0)),
        kind_of(shape),
        [*contexts, dbranch, small],
        prefetch=(places,),
        waits=waits,
    )


def hidden_grad(places, dqkv, weight, width, length, picks, addends, dtype, waits=()):
    seqs, _, out_width = dqkv.shape
    owners = weight.shape[0]
    rows = width // owners
    blocks = len(picks)
    spread = [(k, a) for k in range(blocks) for a in addends[k]]

    def kernel(place_ref, weight_ref, *refs):
        whole = weight_ref[:, :rows, :].reshape(width, out_width)
        for k in range(blocks):
            total = dot(refs[k][0], whole, 1, 1)
            for j, (of, _) in enumerate(spread):
                if of == k:
                    total = total + wide(refs[blocks + j][0])
            refs[-1][k, 0] = total.astype(dtype)

    return run(
        kernel,
        "hidden_grad",
        (seqs,),
        [fixed(weight)]
        + [pl.BlockSpec((1, length, out_width), lambda b, p, q=q: (b, p[q], 0)) for q in picks]
        + [a.spec((1, length, width), lambda b, p: (b, 0, 0)) for _, a in spread],
        pl.BlockSpec((blocks, 1, length, width), lambda b, p: (0, b, 0, 0)),
        kind_of((blocks, seqs, length, width), dtype),
        [weight] + [dqkv] * blocks + [a.array for _, a in spread],
        prefetch=(places,),
        waits=waits,
        cost=2,
    )


def project_grad_pack(places, blocks, dqkv, owners, extra, waits=()):
    seqs, length, width = blocks[0].shape
    ranks = len(blocks)
    out_width = dqkv.shape[2]
    rows = width // owners
    group = max(1, min(owners, 2 * TILE // rows))

    def kernel(place_ref, *refs):
        dqkv_ref, out_ref, total_ref = refs[ranks:]

        @pl.when(pl.program_id(0) == 0)
        def _():
            total_ref[...] = jnp.zeros_like(total_ref)
            total_ref[0:1, :] = column_sum(wide(dqkv_ref[...].reshape(-1, out_width)))

        total = 0.0
        for q in range(ranks):
            at = pl.ds(pl.multiple_of(place_ref[q] * length, length), length)
            for b in range(seqs):
                total = total + dot(refs[q][b], dqkv_ref[b, at, :], 0, 0)
        total = total.astype(jnp.bfloat16)
        sums = total_ref[...].astype(jnp.bfloat16)
        for e in range(group):
            out_ref[e, :rows, :] = total[e * rows : (e + 1) * rows, :]
            out_ref[e, rows:, :] = sums

    return run(
        kernel,
        "project_grad_pack",
        (owners // group,),
        [x.spec((seqs, length, group * rows), lambda i, p: (0, 0, i)) for x in blocks] + [fixed(dqkv)],
        pl.BlockSpec((group, rows + extra, out_width), lambda i, p: (i, 0, 0)),
        kind_of((owners, rows + extra, out_width)),
        [*arrays(blocks), dqkv],
        prefetch=(places,),
        scratch=(pltpu.VMEM((extra, out_width), jnp.float32),),
        waits=waits,
        cost=2,
    )


def lay_columns(places, blocks, rows):
    total, out_width = blocks[0].shape
    part = out_width // 3
    ranks = len(blocks)
    width = part * ranks

    def kernel(place_ref, *refs):
        for q in range(ranks):
            at = pl.ds(pl.multiple_of(place_ref[q] * part, part), part)
            for k in range(3):
                block = wide(refs[q][:, k * part : (k + 1) * part])
                refs[ranks + k][:, at] = block[:rows, :]
                refs[ranks + 3 + k][:, at] = block[rows : rows + 8, :]

    shape, below = (rows, width), (8, width)
    return run(
        kernel,
        "lay_columns",
        (1,),
        [b.whole() for b in blocks],
        [pl.BlockSpec(shape, lambda i, p: (0, 0))] * 3 + [pl.BlockSpec(below, lambda i, p: (0, 0))] * 3,
        [kind_of(shape, jnp.float32)] * 3 + [kind_of(below, jnp.float32)] * 3,
        arrays(blocks),
        prefetch=(places,),
        cost=2,
    )


def lay_up(places, blocks, chips, part, waits=()):
    _, rows, _ = blocks[0].shape
    ranks = len(blocks)
    shape = (rows, 2 * chips * ranks * part)

    def kernel(place_ref, *refs):
        for q in range(ranks):
            for c in range(2):
                for z in range(chips):
                    at = pl.multiple_of(((z * 2 + c) * ranks + place_ref[q]) * part, part)
                    refs[ranks][:, pl.ds(at, part)] = wide(refs[q][c, :, z * part : (z + 1) * part])

    return run(
        kernel,
        "lay_up",
        (1,),
        [b.whole() for b in blocks],
        pl.BlockSpec(shape, lambda i, p: (0, 0)),
        kind_of(shape, jnp.float32),
        arrays(blocks),
        prefetch=(places,),
        waits=waits,
        cost=2,
    )


def lay_rows(places, blocks, waits=()):
    part, width = blocks[0].shape
    ranks = len(blocks)
    shape = (part * ranks, width)

    def kernel(place_ref, *refs):
        for q in range(ranks):
            refs[ranks][pl.ds(pl.multiple_of(place_ref[q] * part, part), part), :] = wide(refs[q][...])

    return run(
        kernel,
        "lay_rows",
        (1,),
        [b.whole() for b in blocks],
        pl.BlockSpec(shape, lambda i, p: (0, 0)),
        kind_of(shape, jnp.float32),
        arrays(blocks),
        prefetch=(places,),
        waits=waits,
        cost=2,
    )


def lay_chips(at, blocks, waits):
    rows, width = blocks[0].shape
    chips = len(blocks)

    def kernel(at_ref, *refs):
        for d in range(chips):
            refs[chips][at_ref[d]] = refs[d][...]

    shape = (chips, rows, width)
    return run(
        kernel,
        "lay_chips",
        (1,),
        [fixed(b) for b in blocks],
        pl.BlockSpec(shape, lambda i, p: (0, 0, 0)),
        kind_of(shape),
        blocks,
        prefetch=(at,),
        cost=100,
        waits=waits,
    )


def hold(array, waits):
    def kernel(from_ref, to_ref):
        to_ref[...] = from_ref[...]

    rank = array.ndim
    return run(
        kernel,
        "hold",
        (1,),
        [fixed(array)],
        pl.BlockSpec(array.shape, lambda i: (0,) * rank),
        kind_of(array.shape, array.dtype),
        [array],
        waits=waits,
    )


def split(at, own, size, waits=()):
    _, width = own.shape
    chips = at.shape[0]

    def kernel(at_ref, own_ref, *outs):
        for d in range(chips):
            outs[d][...] = own_ref[pl.ds(pl.multiple_of(at_ref[d] * size, size), size), :]

    return run(
        kernel,
        "split",
        (1,),
        [fixed(own)],
        [pl.BlockSpec((size, width), lambda i, p: (0, 0))] * chips,
        [kind_of((size, width))] * chips,
        [own],
        prefetch=(at,),
        cost=100,
        waits=waits,
    )


def tick(*waits, cost=10):
    def kernel(out_ref):
        out_ref[...] = jnp.zeros_like(out_ref)

    return run(
        kernel, "tick", (1,), [], pl.BlockSpec((8, 128), lambda i: (0, 0)), kind_of((8, 128), jnp.float32), [], waits=waits, cost=cost
    )


def total_rows(pieces, waits=()):
    def kernel(*refs):
        total = wide(refs[0][...])
        for ref in refs[1:-1]:
            total = total + wide(ref[...])
        refs[-1][...] = total.astype(jnp.bfloat16)

    shape = pieces[0].shape
    return run(
        kernel,
        "total_rows",
        (1,),
        [fixed(p) for p in pieces],
        pl.BlockSpec(shape, lambda i: (0, 0)),
        kind_of(shape),
        pieces,
        waits=waits,
    )


def total_halves(core, pieces, waits=()):
    rows, width = pieces[0].shape
    half = rows // 2

    def kernel(core_ref, *refs):
        for out_ref, of in ((refs[-2], core_ref[0]), (refs[-1], 1 - core_ref[0])):
            at = pl.ds(pl.multiple_of(of * half, half), half)
            total = wide(refs[0][at, :])
            for ref in refs[1:-2]:
                total = total + wide(ref[at, :])
            out_ref[...] = total.astype(jnp.bfloat16)

    return run(
        kernel,
        "total_halves",
        (1,),
        [fixed(p) for p in pieces],
        [pl.BlockSpec((half, width), lambda i, p: (0, 0))] * 2,
        [kind_of((half, width))] * 2,
        pieces,
        prefetch=(core,),
        waits=waits,
    )


def pair(core, own, other, waits=()):
    rows, width = own.shape

    def kernel(core_ref, own_ref, other_ref, out_ref):
        out_ref[core_ref[0]] = own_ref[...]
        out_ref[1 - core_ref[0]] = other_ref[...]

    shape = (2, rows, width)
    return run(
        kernel,
        "pair",
        (1,),
        [fixed(own), fixed(other)],
        pl.BlockSpec(shape, lambda i, p: (0, 0, 0)),
        kind_of(shape),
        [own, other],
        prefetch=(core,),
        waits=waits,
    )


def plan_rows(segments):
    b, t = segments.shape
    span, win = min(SPAN, t), min(WINDOW, t)
    spans = segments.reshape(b, t // span, span)
    place = jnp.arange(t, dtype=jnp.int32)
    low = jnp.min(jnp.where(segments[:, None, :] == spans[:, :, :1], place, t), axis=2)
    high = jnp.max(jnp.where(segments[:, None, :] == spans[:, :, -1:], place, -1), axis=2)
    start = jnp.minimum(low // ALIGN * ALIGN, t - win)
    fits = jnp.all(high < start + win, axis=1)
    single = jnp.all(segments == segments[:, :1], axis=1)
    kind = jnp.where(single, 0, jnp.where(fits, 1, 2))
    return kind.astype(jnp.int32), start.astype(jnp.int32)

def aligned(start, size):
    return start if isinstance(start, int) else pl.multiple_of(start, size)


def bias_of(col_ref, keys, row_ref, queries):
    return jnp.where(col_ref[0, keys, :] == row_ref[0, :, queries], 0.0, MASKED)


def over(count, body):
    if count == 1:
        body(0)
    else:
        lax.fori_loop(0, count, lambda g, c: (body(g), c)[1], 0, unroll=UNROLL)


def fwd_kernel(heads, kind_ref, start_ref, place_ref, qkv_ref, row_ref, col_ref, ctx_ref, lse_ref, *part_refs):
    b = pl.program_id(0)
    t = qkv_ref.shape[1]
    hw = heads * HEAD_DIM
    span, win = min(SPAN, t), min(WINDOW, t)
    kind = kind_ref[b]

    group = min(2, heads)
    lanes = group * HEAD_DIM

    def attend(g, rows, keys, bias):
        def piece(which):
            return pl.ds(aligned(which * hw + g * lanes, lanes), lanes)

        query, key, value = (qkv_ref[0, r, piece(w)] for w, r in enumerate((rows, keys, keys)))
        parts = []
        for e in range(group):
            at = slice(e * HEAD_DIM, (e + 1) * HEAD_DIM)
            s = dot(key[:, at], query[:, at], 1, 1)
            if bias is not None:
                s = s + bias
            m = jnp.max(s, axis=0, keepdims=True)
            p = jnp.exp(s - m)
            total = jnp.sum(p, axis=0, keepdims=True)
            parts.append(dot(value[:, at], p.astype(jnp.bfloat16), 0, 0) / total)
            lse_ref[0, pl.ds(g * group + e, 1), rows] = m + jnp.log(total)
        ctx_ref[0, rows, piece(0)] = jnp.transpose(jnp.concatenate(parts, axis=0)).astype(jnp.bfloat16)

    def each(size, masked, keys_of):
        size = min(size, t)

        def body(i, _):
            rows = pl.ds(pl.multiple_of(i * size, size), size)
            bias = bias_of(col_ref, keys_of(i), row_ref, rows) if masked else None
            over(heads // group, lambda g: attend(g, rows, keys_of(i), bias))
            return 0

        lax.fori_loop(0, t // size, body, 0)

    @pl.when(kind == 0)
    def _():
        each(FORWARD_SPAN, False, lambda i: pl.ds(0, t))

    @pl.when(kind == 2)
    def _():
        each(span, True, lambda i: pl.ds(0, t))

    @pl.when(kind == 1)
    def _():
        each(span, True, lambda i: pl.ds(pl.multiple_of(start_ref[b, i], ALIGN), win))

    length = part_refs[0].shape[1]
    for q, part_ref in enumerate(part_refs):
        part_ref[0] = ctx_ref[0, pl.ds(pl.multiple_of(place_ref[q] * length, length), length), :]


def attention(qkv, segments, kind, start, places, waits):
    ranks = places.shape[0]
    b, t, w = qkv.shape
    hw = w // 3
    heads = hw // HEAD_DIM

    def at(i, *_):
        return (i, 0, 0)

    return run(
        functools.partial(fwd_kernel, heads),
        "attention_forward",
        (b,),
        [pl.BlockSpec((1, t, w), at), pl.BlockSpec((1, 1, t), at), pl.BlockSpec((1, t, 1), at)],
        [pl.BlockSpec((1, t, hw), at), pl.BlockSpec((1, heads, t), at)]
        + [pl.BlockSpec((1, t // ranks, hw), at)] * ranks,
        [kind_of((b, t, hw)), kind_of((b, heads, t), jnp.float32)] + [kind_of((b, t // ranks, hw))] * ranks,
        [qkv, segments[:, None, :], segments[:, :, None]],
        prefetch=(kind, start, places),
        waits=waits,
        cost=100,
    )

def bwd_kernel(heads, b, kind_ref, start_ref, qkv_ref, do_ref, ctx_ref, lse_ref, row_ref, col_ref, out_ref, dq_acc, delta_ref):
    t = qkv_ref.shape[1]
    hw = heads * HEAD_DIM
    span, win = min(SPAN, t), min(WINDOW, t)
    kind = kind_ref[b]

    def lanes(h, which=0):
        lo = which * hw + h * HEAD_DIM
        return slice(lo, lo + HEAD_DIM)

    prod = do_ref[0].astype(jnp.float32) * ctx_ref[0].astype(jnp.float32)
    high = prod.astype(jnp.bfloat16)
    rest = (prod - high.astype(jnp.float32)).astype(jnp.bfloat16)
    head = lax.broadcasted_iota(jnp.int32, (delta_ref.shape[0], hw), 0)
    of = lax.broadcasted_iota(jnp.int32, (delta_ref.shape[0], hw), 1) // HEAD_DIM
    ones = (head == of).astype(jnp.bfloat16)
    delta_ref[...] = dot(ones, high, 1, 1) + dot(ones, rest, 1, 1)

    group = min(2, heads)
    lanes = group * HEAD_DIM

    def back(g, keys, queries, bias):
        def piece(which):
            return pl.ds(aligned(which * hw + g * lanes, lanes), lanes)

        query, key, value = (qkv_ref[0, r, piece(w)] for w, r in enumerate((queries, keys, keys)))
        grad = do_ref[0, queries, piece(0)]
        key_grads, value_grads = [], []
        for e in range(group):
            at = slice(e * HEAD_DIM, (e + 1) * HEAD_DIM)
            row = pl.ds(g * group + e, 1)
            s = dot(key[:, at], query[:, at], 1, 1)
            if bias is not None:
                s = s + bias
            p = jnp.exp(s - lse_ref[0, row, queries])
            dp = dot(value[:, at], grad[:, at], 1, 1)
            ds = (p * (dp - delta_ref[row, queries])).astype(jnp.bfloat16)
            value_grads.append(dot(p.astype(jnp.bfloat16), grad[:, at], 1, 0))
            key_grads.append(dot(ds, query[:, at], 1, 0))
            into = pl.ds(aligned(g * lanes + e * HEAD_DIM, HEAD_DIM), HEAD_DIM)
            dq_acc[into, queries] += dot(key[:, at], ds, 0, 0)
        out_ref[0, keys, piece(1)] = jnp.concatenate(key_grads, axis=1).astype(jnp.bfloat16)
        out_ref[0, keys, piece(2)] = jnp.concatenate(value_grads, axis=1).astype(jnp.bfloat16)

    dq_acc[...] = jnp.zeros_like(dq_acc)

    def each(size, masked, queries_of):
        size = min(size, t)

        def body(j, _):
            keys = pl.ds(pl.multiple_of(j * size, size), size)
            bias = bias_of(col_ref, keys, row_ref, queries_of(j)) if masked else None
            over(heads // group, lambda g: back(g, keys, queries_of(j), bias))
            return 0

        lax.fori_loop(0, t // size, body, 0)

    @pl.when(kind == 0)
    def _():
        each(BACKWARD_SPAN, False, lambda j: pl.ds(0, t))

    @pl.when(kind == 2)
    def _():
        each(span, True, lambda j: pl.ds(0, t))

    @pl.when(kind == 1)
    def _():
        each(span, True, lambda j: pl.ds(pl.multiple_of(start_ref[b, j], ALIGN), win))

    out_ref[0, :, :hw] = (jnp.transpose(dq_acc[...]) * (HEAD_DIM**-0.5)).astype(jnp.bfloat16)


def attention_back(qkv, dparts, ctx, lse, segments, kind, start, places, which, buffer, waits):
    b, t, w = qkv.shape
    hw = w // 3
    heads = hw // HEAD_DIM
    ranks = len(dparts)
    length = t // ranks

    def kernel(kind_ref, start_ref, place_ref, qkv_ref, *refs):
        grad_ref = refs[-1]
        for q in range(ranks):
            grad_ref[0, pl.ds(pl.multiple_of(place_ref[q] * length, length), length), :] = refs[q][0]
        bwd_kernel(heads, which, kind_ref, start_ref, qkv_ref, grad_ref, *refs[ranks : ranks + 4], *refs[-4:-1])

    def at(i, *_):
        return (which, 0, 0)

    ins = [pl.BlockSpec((1, t, w), at)] + [pl.BlockSpec((1, length, hw), at)] * ranks
    ins += [
        pl.BlockSpec((1, t, hw), at),
        pl.BlockSpec((1, heads, t), at),
        pl.BlockSpec((1, 1, t), at),
        pl.BlockSpec((1, t, 1), at),
    ]
    operands = [qkv, *dparts, ctx, lse, segments[:, None, :], segments[:, :, None]]
    alias = None
    if buffer is not None:
        ins.append(pl.BlockSpec(memory_space=pl.ANY))
        operands.append(buffer)
        alias = {3 + len(ins) - 1: 0}
    return run(
        kernel,
        "attention_backward",
        (1,),
        ins,
        pl.BlockSpec((1, t, w), at),
        kind_of((b, t, w)),
        operands,
        prefetch=(kind, start, places),
        scratch=(
            pltpu.VMEM((hw, t), jnp.float32),
            pltpu.VMEM((-(-heads // 8) * 8, t), jnp.float32),
            pltpu.VMEM((1, t, hw), jnp.bfloat16),
        ),
        alias=alias,
        waits=waits,
    )


AXES = ("seq", "z", "core")
ROWS = ("z", "core")
EXTRA = 16


def low(tensor):
    return tensor.astype(jnp.bfloat16)


class Ring:
    def __init__(self):
        self.ranks = lax.axis_size("seq")
        self.chips = lax.axis_size("z")
        self.index = lax.axis_index("seq")
        self.core = lax.axis_index("core")
        self.count = self.ranks.bit_length() - 1

    def bit(self, k, core):
        if self.count == 2 and core == 1:
            k = 1 - k
        return 1 << k

    def offset(self, q, core):
        return sum(self.bit(k, core) for k in range(self.count) if q >> k & 1)

    def place(self, q):
        return jnp.bitwise_xor(self.index, jnp.where(self.core == 0, self.offset(q, 0), self.offset(q, 1)))

    def hop(self, block, k):
        pairs = []
        for s in range(self.ranks):
            for z in range(self.chips):
                for c in range(2):
                    to = s ^ self.bit(k, c)
                    pairs.append(((s * self.chips + z) * 2 + c, (to * self.chips + z) * 2 + c))
        return lax.ppermute(block, AXES, pairs)

    def gather(self, block):
        blocks = [block]
        for k in range(self.count):
            blocks = blocks + [self.hop(b, k) for b in blocks]
        return [View(b) for b in blocks]

    def exchange(self, blocks):
        out = [blocks[0]]
        for q in range(1, self.ranks):
            pairs = []
            for s in range(self.ranks):
                for z in range(self.chips):
                    for c in range(2):
                        to = s ^ self.offset(q, c)
                        pairs.append(((s * self.chips + z) * 2 + c, (to * self.chips + z) * 2 + c))
            out.append(lax.ppermute(blocks[q], AXES, pairs))
        return out

    def shift(self, block, d):
        return lax.ppermute(block, "z", [(z, (z + d) % self.chips) for z in range(self.chips)])


def swap(block):
    return lax.ppermute(block, "core", [(0, 1), (1, 0)])


def put(blocks, ring, axis):
    shape = list(blocks[0].shape)
    size = shape[axis]
    shape[axis] = size * len(blocks)
    whole = jnp.zeros(shape, blocks[0].dtype)
    for q, block in enumerate(blocks):
        whole = lax.dynamic_update_slice_in_dim(whole, block, ring.place(q) * size, axis)
    return whole


def local(
    hidden_in,
    segments,
    q_weight,
    k_weight,
    v_weight,
    out_weight,
    q_bias,
    v_bias,
    out_bias,
    up_weight,
    up_bias,
    down_weight,
    down_bias,
    norm1_gain,
    norm1_bias,
    norm2_gain,
    norm2_bias,
    out_grad,
):
    ring = Ring()
    here, core = ring.index, ring.core
    ranks, chips = ring.ranks, ring.chips
    owners = chips * 2
    z_index = lax.axis_index("z")
    owner = z_index * 2 + core
    seqs, length, width = hidden_in.shape
    full = length * ranks
    head_width = width // ranks
    out_width = 3 * head_width
    rows = width // owners
    units = down_weight.shape[0]
    part = units // ranks
    count = seqs * length
    score_scale = HEAD_DIM ** (-0.5)
    first_core = core == 0
    core_index = core.astype(jnp.int32).reshape(1)
    places = jnp.stack([ring.place(q) for q in range(ranks)]).astype(jnp.int32)
    blocks = range(ranks)

    heads_at = here * head_width
    mine = jnp.concatenate(
        [lax.dynamic_slice_in_dim(w, heads_at, head_width, 1) for w in (q_weight, k_weight, v_weight)], axis=1
    )
    vectors = (q_bias, v_bias, out_bias, down_bias, norm1_gain, norm1_bias, norm2_gain, norm2_bias)
    known = len(vectors)
    packed = jnp.pad(
        up_bias.reshape(-1, rows), ((known, EXTRA - known - units // rows), (0, out_width - rows))
    )
    for i, vector in enumerate(vectors):
        packed = packed + jnp.pad(vector[None], ((i, EXTRA - 1 - i), (0, out_width - rows)))
    mine = jnp.concatenate([mine, packed], axis=0)

    def up_columns(of_core):
        return jnp.concatenate(
            [
                lax.dynamic_slice_in_dim(up_weight, ((z * 2 + of_core) * ranks + here) * part, part, 1)
                for z in range(chips)
            ],
            axis=1,
        )

    own_up, other_up = up_columns(core), swap(up_columns(1 - core))
    up_rows = jnp.concatenate(
        [jnp.where(first_core, own_up, other_up), jnp.where(first_core, other_up, own_up)], axis=0
    )
    hidden = ring.gather(hidden_in)
    shifts = jnp.stack([(z_index - d) % chips for d in range(chips)]).astype(jnp.int32)
    up_block = lay_chips(shifts, [up_rows] + [ring.shift(up_rows, d) for d in range(1, chips)], ())
    up_block = hold(up_block.reshape(width, chips * part), (hidden[-1].array,))
    gathered = lax.all_gather(mine, ROWS, axis=0)
    down_rows = hold(lax.dynamic_slice_in_dim(down_weight, here * part, part, 0), (gathered,))
    down_block = lax.all_gather(down_rows, "z", axis=0, tiled=True)
    output_weight = lax.all_gather(hold(out_weight, (down_rows,)), ROWS, axis=0, tiled=True)
    up_weights = ring.gather(up_block)
    kind, start = plan_rows(segments)
    keep = wide(lax.dynamic_slice_in_dim(segments, here * length, length, 1) != 0)[:, :, None]

    qkv_weight = gathered
    gathered = wide(gathered[:, rows:, :rows])
    vectors = gathered.transpose(1, 0, 2).reshape(EXTRA, width)
    biases = lax.dynamic_slice_in_dim(vectors, heads_at, head_width, 1)
    qkv_bias = jnp.concatenate([biases[0], jnp.zeros_like(biases[0]), biases[1]])[None]
    scales = jnp.where(jnp.arange(out_width) < head_width, score_scale, 1.0)[None]
    qkv = project(places, hidden, qkv_weight, qkv_bias, scales)
    contexts, log_totals, *context_parts = attention(
        qkv, segments, kind, start, places, (up_block,)
    )
    context_parts = ring.exchange(context_parts)
    down_weights = ring.gather(hold(down_block, (*context_parts[1:], *arrays(up_weights[1:3]))))
    sums_one, first_low = out_norm(
        places,
        context_parts,
        output_weight,
        hidden_in,
        vectors,
    )

    first_low = first_low.reshape(count, width)
    first_other = swap(first_low)
    upper_bias = gathered[:, known : known + units // rows].reshape(chips, 2, ranks, part)
    upper_bias = lax.dynamic_index_in_dim(upper_bias, core, 1, False)
    upper_bias = [
        lax.dynamic_index_in_dim(upper_bias, ring.place(q), 1, False).reshape(1, -1) for q in blocks
    ]
    actives, slopes = up_forward(
        first_low, first_other, up_weights, upper_bias, arrays(down_weights[1:2])
    )
    mixed_other = down_forward(actives, down_weights, count, count, jnp.bfloat16)
    mixed = down_forward(actives, down_weights, 0, count, jnp.bfloat16, (mixed_other,))
    layer_out, dmixed, totals_two = norm_two(mixed, swap(mixed_other), sums_one, vectors, out_grad, keep)

    dmixed = dmixed.reshape(count, width)
    dmixed_other = swap(dmixed)
    none = [()] * ranks
    odd, even = [q for q in blocks if q % 2], [q for q in blocks if q % 2 == 0]
    down_sent = down_grad([actives[q] for q in odd], dmixed, dmixed_other, none)
    duppers, up_sums, dfirst, dfirst_other = ffn_back(
        dmixed, dmixed_other, slopes, down_weights, up_weights, (tick(down_sent),)
    )
    dfirst_other = swap(dfirst_other)
    dbranch, dcontexts, totals_one = norm_one_back(
        places, dfirst, dfirst_other, dmixed, sums_one, vectors, output_weight, head_width, (tick(duppers[0], cost=10),)
    )
    dcontexts = ring.exchange(dcontexts)

    def spread(made, sent):
        came = {q: [] for q in blocks}
        for k in range(ring.count):
            step = 1 << k
            got = ring.hop(sent, k)
            for i, q in enumerate(range(0, ranks, 2 * step)):
                came[q].append(View(got, i))
            if k + 1 < ring.count:
                turn = [q + 2 * step for q in range(0, ranks, 4 * step)]
                sent = made(turn, [came[q] for q in turn])
        return came[0], sent

    def down_made(turn, addends):
        return down_grad([actives[q] for q in turn], dmixed, dmixed_other, addends, (tick(dbranch),))

    down_came, down_hop = spread(down_made, down_sent)
    up_sent = up_grad([duppers[q] for q in odd], first_low, first_other, none, (down_hop,))

    extra = -(-(6 + ranks) // EXTRA) * EXTRA
    up_totals = put([up_sums[q : q + 1] for q in blocks], ring, 0).reshape(ranks, chips, 1, part)
    up_totals = jnp.where(jnp.arange(2)[None, None, :, None] == core, up_totals, 0.0)
    up_totals = jnp.pad(up_totals, ((0, 0), (0, 0), (0, 0), (0, rows - part))).reshape(ranks, width)
    small = jnp.concatenate(
        [totals_two[:3], totals_one[:3], up_totals, jnp.zeros((extra - 6 - ranks, width), jnp.float32)], axis=0
    )
    out_pack = out_grad_pack(places, context_parts, dbranch, low(small), owners, (up_sent,))
    out_shard = lax.psum_scatter(out_pack.reshape(-1, width), ROWS, scatter_dimension=0, tiled=True)

    common = (qkv, dcontexts, contexts, log_totals, segments, kind, start, places)
    dqkv = attention_back(*common, 0, None, (out_pack,))

    def up_made(turn, addends):
        return up_grad([duppers[q] for q in turn], first_low, first_other, addends, (down_pieces[0],))

    down_own = down_grad([actives[0]], dmixed, dmixed_other, [down_came], (dqkv,))[0]
    ahead = jnp.stack([(z_index + d) % chips for d in range(chips)]).astype(jnp.int32)
    down_pieces = split(ahead, down_own, part)
    up_came, up_hop = spread(up_made, up_sent)
    for which in range(1, seqs):
        dqkv = attention_back(*common, which, dqkv, (up_hop,))

    def shifted(pieces):
        return [pieces[0]] + [ring.shift(pieces[d], d) for d in range(1, chips)]

    def hidden_made(turn, addends, waits=()):
        return hidden_grad(places, dqkv, qkv_weight, width, length, turn, addends, jnp.bfloat16, waits or (up_pair,))

    down_shard = total_rows(shifted(down_pieces), (dqkv, up_came[-1].array))
    down_parts = ring.gather(down_shard)
    up_own = up_grad([duppers[0]], first_low, first_other, [up_came], (down_shard,))[0]
    up_pieces = split(ahead, up_own, 2 * rows)
    hidden_sent = hidden_made(odd, none, (up_pieces[0], *arrays(down_parts[1:2])))
    qkv_pack = project_grad_pack(
        places, hidden, dqkv, owners, EXTRA, (hidden_sent, out_shard, *arrays(down_parts[2:]))
    )
    qkv_shard = lax.psum_scatter(qkv_pack.reshape(-1, out_width), ROWS, scatter_dimension=0, tiled=True)
    out_sum = [wide(out_shard)]
    for k in range(ring.count):
        out_sent = low(out_sum[-1])
        out_sum.append(out_sum[-1] + wide(ring.hop(out_sent, k)))
    keep_part, take_part = total_halves(core_index, shifted(up_pieces), (qkv_pack,))
    down_weight_grad = lay_rows(places, down_parts, (keep_part,))
    up_pair = pair(core_index, keep_part, swap(take_part), (down_weight_grad,))
    hidden_came, hidden_hop = spread(hidden_made, hidden_sent)
    input_grad = hidden_grad(
        places, dqkv, qkv_weight, width, length, [0], [[View(dbranch)] + hidden_came], jnp.float32
    )[0]

    up_parts = ring.gather(up_pair)
    qkv_parts = ring.gather(qkv_shard)
    out_pack = out_sum[-1]
    if part % 128 == 0:
        up_weight_grad = lay_up(places, up_parts, chips, part, (hidden_hop,))
    else:
        up_weight_grad = wide(put([b.value()[None] for b in up_parts], ring, 0))
        up_weight_grad = (
            up_weight_grad.reshape(ranks, 2, rows, chips, part).transpose(2, 3, 1, 0, 4).reshape(rows, owners * units)
        )
    if head_width % 128 == 0:
        *qkv_grads, q_sums, _, v_sums = lay_columns(places, qkv_parts, rows)
    else:
        laid = wide(put([b.value()[None] for b in qkv_parts], ring, 0))
        laid = laid.reshape(ranks, rows + EXTRA, 3, head_width).transpose(2, 1, 0, 3).reshape(3, -1, width)
        qkv_grads, q_sums, v_sums = [g[:rows] for g in laid], laid[0, rows:], laid[2, rows:]

    def mine_of(sums):
        return lax.dynamic_slice_in_dim(sums[0], owner * rows, rows, 0)

    small = out_pack[rows:, :rows]
    up_bias_grad = small[6 : 6 + ranks, :part].reshape(-1)
    return (
        layer_out,
        input_grad,
        *qkv_grads,
        out_pack[:rows],
        mine_of(q_sums),
        mine_of(v_sums),
        small[3],
        up_weight_grad,
        up_bias_grad,
        down_weight_grad,
        small[0],
        small[4],
        small[5],
        small[1],
        small[2],
    )


def solution(mesh):
    ranks, owners = mesh.shape["seq"], mesh.shape["fsdp"]
    grid = Mesh(mesh.devices.reshape(ranks, owners // 2, 2), AXES)
    tokens, matrix, vector = P(ROWS, "seq", None), P(ROWS, None), P(ROWS)
    return jax.shard_map(
        local,
        mesh=grid,
        in_specs=(
            tokens,
            matrix,
            matrix,
            matrix,
            matrix,
            matrix,
            vector,
            vector,
            vector,
            matrix,
            vector,
            matrix,
            vector,
            vector,
            vector,
            vector,
            vector,
            tokens,
        ),
        out_specs=(
            tokens,
            tokens,
            matrix,
            matrix,
            matrix,
            matrix,
            vector,
            vector,
            vector,
            matrix,
            vector,
            matrix,
            vector,
            vector,
            vector,
            vector,
            vector,
        ),
        check_vma=False,
    )
```
